512 devices in a mesh: sector: 64 (over y_lo, z, core), dof: 8 (over x, y_hi).
Axes of the slice: x: 4, y: 4 (y_hi: 2, y_lo: 2; y = y_hi * 2 + y_lo), z: 16, core: 2. Of those that a mesh axis runs over, the one named last changes fastest.
Arguments:
- wake_field: bfloat16 [64, 8, 14336], P('sector', None, 'dof'), may hold values from -6 to 6
- sector_basis: bfloat16 [64, 128, 14336], P('sector', None, 'dof'), may hold values from -0.046875 to 0.046875
- block_index: int32 [64, 256], P('sector'), may hold values from 0 to 63
- phase_index: int32 [64, 256], P('sector'), may hold values from 0 to 7
- mode_shapes: bfloat16 [64, 40, 128], P('sector'), may hold values from -0.5 to 0.5
- residual_flex: bfloat16 [64, 128, 128], P('sector'), may hold values from -0.5 to 0.5
- mode_omega: float32 [64, 40], P('sector'), may hold values from 0.2 to 2
- mode_zeta: float32 [64, 40], P('sector'), may hold values from 0.01 to 0.2
- stress_map: bfloat16 [64, 16384, 128], P('sector', 'dof'), may hold values from -0.5 to 0.5
Outputs:
- stress: bfloat16 [64, 16384, 256], P('sector', 'dof')
The draws below stay inside these ranges and needn't reach their ends.
All inputs are finite; a program needn't handle non-finite values.
Results may differ from the reference program's by a relative error of at most 0.027.
Values may be sent and summed in bfloat16 or wider, within the bound.
No kernel may reach another device: no remote copies, remote signals or barrier semaphores. Data moves between devices by JAX's collectives and lax.ppermute only.
A program may use at most 64 MiB of HBM per device.

```python
import math
import jax
import jax.numpy as jnp
from jax import lax

NB = 128
MODES = 40
PH = 8
NT = 256
BLADES = 64
BLOCKS = 64
ROWS = 14336
SROWS = 16384


def plant(drawn, key, least, largest):
    longest = drawn.shape.index(max(drawn.shape))
    spots = []
    for shift in (0, 1):
        where = [jax.random.randint(jax.random.fold_in(key, axis), (), 0, length) for axis, length in enumerate(drawn.shape)]
        where[longest] = (where[longest] + shift) % drawn.shape[longest]
        spots.append(tuple(where))
    return drawn.at[spots[0]].set(least).at[spots[1]].set(largest)


def block_scale(stream_key, shape, cuts, smallest, largest):
    factor_of, own = 1.0, jax.random.fold_in(stream_key, 6)
    for dim, shards_of in cuts:
        draws = jnp.exp(jax.random.uniform(jax.random.fold_in(own, dim), (shards_of,), jnp.float32, smallest / len(cuts), largest / len(cuts)))
        factor_of = factor_of * jnp.repeat(draws, shape[dim] // shards_of).reshape([-1 if axis == dim else 1 for axis in range(len(shape))])
    return factor_of


def bell_draw(rng, shape, spread, most, pieces=(), kind=jnp.bfloat16):
    gain = block_scale(rng, shape, pieces, -0.22, 0.18) if pieces else 1.0
    array = jax.random.normal(rng, shape, jnp.float32) * spread * gain
    return jnp.minimum(jnp.maximum(array, -most), most).astype(kind)


def setup_inputs(seed: int = 0) -> dict:
    streams_of = jax.random.split(jax.random.key(seed), 10)
    wake_field = bell_draw(streams_of[0], (BLOCKS, PH, ROWS), 1.0, 6.0, ((0, 64), (2, 8)))
    sector_basis = bell_draw(streams_of[1], (BLADES, NB, ROWS), ROWS ** -0.5, 0.046875, ((0, 64), (2, 8)))
    block_index = plant(jax.random.randint(streams_of[2], (BLADES, NT), 0, BLOCKS), jax.random.fold_in(streams_of[2], 1), 0, BLOCKS - 1).astype(jnp.int32)
    phase_index = plant(jax.random.randint(streams_of[3], (BLADES, NT), 0, PH), jax.random.fold_in(streams_of[3], 1), 0, PH - 1).astype(jnp.int32)
    mode_shapes = bell_draw(streams_of[4], (BLADES, MODES, NB), NB ** -0.5, 0.5, ((0, 64),))
    residual_flex = bell_draw(streams_of[5], (BLADES, NB, NB), NB ** -0.5, 0.5, ((0, 64),))
    mode_omega = jnp.clip(jnp.exp(math.log(2.0) - 2.3025851 * jax.random.uniform(streams_of[6], (BLADES, MODES), jnp.float32) ** block_scale(streams_of[6], (BLADES, MODES), ((0, 64),), -0.2, 0.2)), 0.2, 2.0)
    mode_zeta = jnp.clip(jnp.exp(math.log(0.2) - 2.9957323 * jax.random.uniform(streams_of[7], (BLADES, MODES), jnp.float32) ** block_scale(streams_of[7], (BLADES, MODES), ((0, 64),), -0.2, 0.2)), 0.01, 0.2)
    stress_map = bell_draw(streams_of[8], (BLADES, SROWS, NB), NB ** -0.5, 0.5, ((0, 64), (1, 8)))
    return {"wake_field": wake_field, "sector_basis": sector_basis, "block_index": block_index, "phase_index": phase_index, "mode_shapes": mode_shapes, "residual_flex": residual_flex, "mode_omega": mode_omega, "mode_zeta": mode_zeta, "stress_map": stress_map}


def fourier(count):
    row_ids = jnp.arange(count)[:, None]
    col_ids = jnp.arange(count)[None, :]
    freqs = (row_ids + 1) // 2
    angle = 2.0 * jnp.pi * (freqs * col_ids % count).astype(jnp.float32) / count
    table = jnp.where(row_ids % 2 == 1, jnp.cos(angle), jnp.sin(angle))
    table = jnp.where(row_ids == 0, jnp.ones_like(table), table)
    edges = (row_ids == 0) | (row_ids == count - 1)
    scale = jnp.where(edges, jnp.sqrt(1.0 / count), jnp.sqrt(2.0 / count)).astype(jnp.float32)
    return (table * scale).astype(jnp.float32)

def respond(force, omega, zeta):
    steps = force.shape[1]
    lag = (jnp.arange(steps)[:, None] - jnp.arange(steps)[None, :]).astype(jnp.float32)
    later = lag >= 0.0
    lag_pos = jnp.maximum(lag, 0.0)
    decay = (omega * zeta)[:, None, None]
    damped = (omega * jnp.sqrt(1.0 - zeta * zeta))[:, None, None]
    kernel = jnp.where(later[None], jnp.exp(-decay * lag_pos) * jnp.sin(damped * lag_pos), 0.0)
    return jnp.einsum('mts,ms->mt', kernel, force, precision=lax.Precision.HIGHEST)

def reference(wake_field, sector_basis, block_index, phase_index, mode_shapes, residual_flex, mode_omega, mode_zeta, stress_map):
    flat = wake_field.reshape(BLOCKS * PH, ROWS).astype(jnp.float32)

    def project(basis):
        return jnp.dot(flat, basis.astype(jnp.float32).T, precision=lax.Precision.HIGHEST).astype(jnp.bfloat16)
    tables = lax.map(project, sector_basis)
    pairs = (block_index * PH + phase_index).astype(jnp.int32)
    picked = jax.vmap(lambda table, pair: table[pair])(tables, pairs)
    forcing = jnp.transpose(picked, (0, 2, 1))
    table_f = fourier(BLADES)
    harmonic = jnp.einsum('hs,snt->hnt', table_f, forcing.astype(jnp.float32), precision=lax.Precision.HIGHEST).astype(jnp.bfloat16)

    def answer(items):
        forced, shapes, flex, omega, zeta = items
        modal_force = jnp.dot(shapes, forced, preferred_element_type=jnp.float32)
        amplitude = respond(modal_force, omega, zeta)
        physical = jnp.einsum('mn,mt->nt', shapes.astype(jnp.float32), amplitude, precision=lax.Precision.HIGHEST)
        physical = physical + jnp.dot(flex, forced, preferred_element_type=jnp.float32)
        return physical.astype(jnp.bfloat16)
    physical = lax.map(answer, (harmonic, mode_shapes, residual_flex, mode_omega, mode_zeta))
    sectoral = jnp.einsum('hs,hnt->snt', table_f, physical.astype(jnp.float32), precision=lax.Precision.HIGHEST).astype(jnp.bfloat16)

    def recover(items):
        operator, motion = items
        return jnp.dot(operator, motion, preferred_element_type=jnp.float32).astype(jnp.bfloat16)
    return lax.map(recover, (stress_map, sectoral))
```

```python
import numpy as np
import jax
import jax.numpy as jnp
from jax import lax
from jax.experimental import pallas as pl
from jax.experimental.pallas import tpu as pltpu
from jax.sharding import Mesh, PartitionSpec as P

AXES = ("yl", "z", "c", "x", "yh")
SIZES = (2, 16, 2, 4, 2)
PLANE = ("yl", "c", "x", "yh")
YL, Z, C, D = 2, 16, 2, 8
PEERS = YL * C * D
BLADES, PH, NT, NB, MODES = YL * Z * C, 8, 256, 128, 40
HALF = 896
TS = NT // PEERS
TD = NT // D
BF = jnp.bfloat16
F32 = jnp.float32
HI = lax.Precision.HIGHEST


def fourier_table(count):
    h = np.arange(count)[:, None]
    s = np.arange(count)[None, :]
    angle = 2.0 * np.pi * ((((h + 1) // 2) * s) % count) / count
    table = np.where(h % 2 == 1, np.cos(angle), np.sin(angle))
    table = np.where(h == 0, 1.0, table)
    edges = (h == 0) | (h == count - 1)
    return table * np.where(edges, np.sqrt(1.0 / count), np.sqrt(2.0 / count))


FOURIER = fourier_table(BLADES)
FORWARD = np.ascontiguousarray(
    FOURIER.reshape(YL, Z, C, YL, Z, C).transpose(1, 4, 3, 5, 0, 2).reshape(Z, 1, 256)
).astype(np.float32)
INVERSE = np.ascontiguousarray(
    FOURIER.reshape(YL, Z, C, YL, Z, C).transpose(0, 2, 4, 1, 3, 5).reshape(YL * C * Z, 1, 64)
).astype(np.float32)


def dot_nt(a, b, **kw):
    return lax.dot_general(
        a, b, (((1,), (1,)), ((), ())), preferred_element_type=F32, **kw
    )


def project_kernel(pos, own_ref, other_ref, mine_ref, got_ref, index_ref, out_ref):
    core = pos[1]
    basis = jnp.concatenate([mine_ref[...], got_ref[0:NB, :]], axis=0)
    table = [
        dot_nt(ref[...].reshape(YL * Z * PH, HALF), basis).astype(BF)
        for ref in (own_ref, other_ref)
    ]
    pair = lax.broadcasted_iota(jnp.int32, (NT, YL * Z * PH), 1).astype(F32)
    theirs = got_ref[NB : NB + 16, 0:NT].astype(F32)
    picks = []
    for r in range(2):
        if r == 0:
            block, phase = index_ref[0:1, :], index_ref[1:2, :]
        else:
            block = theirs[0:1, :].astype(jnp.int32)
            phase = theirs[1:2, :].astype(jnp.int32)
        code = ((block >> 1) * PH + phase).astype(F32)
        here = (block & 1) == core
        codes = jnp.concatenate(
            [jnp.where(here, code, -1.0), jnp.where(here, -1.0, code)]
            + [jnp.zeros((6, NT), F32)],
            axis=0,
        ).T
        total = jnp.zeros((NT, NB), F32)
        for k in range(2):
            onehot = jnp.where(codes[:, k : k + 1] == pair, 1.0, 0.0).astype(BF)
            total += jnp.dot(
                onehot, table[k][:, r * NB : (r + 1) * NB], preferred_element_type=F32
            )
        picks.append(total.reshape(PEERS, TS, NB))
    out_ref[...] = jnp.concatenate(picks, axis=1).astype(BF)


def gather_sum_kernel(in_ref, out_ref):
    sums = {}
    for yl in range(YL):
        for c in range(C):
            total = None
            for d in range(D):
                part = in_ref[(yl * C + c) * D + d].astype(F32)
                total = part if total is None else total + part
            sums[yl, c] = total
    rows = [
        sums[yl, c][0:TS] + sums[1 - yl, c][TS : 2 * TS] for yl in range(YL) for c in range(C)
    ]
    block = jnp.concatenate(rows, axis=0).astype(BF)
    out_ref[...] = jnp.broadcast_to(block[None], out_ref.shape)


def forward_kernel(pos, table_ref, in_ref, out_ref):
    acc = [None] * 4
    for z in range(Z):
        block = in_ref[z].astype(F32)
        for q in range(4):
            part = block[q * TS : (q + 1) * TS]
            for h in range(4):
                term = part * table_ref[0, 0, (z * 4 + q) * 4 + h]
                acc[h] = term if acc[h] is None else acc[h] + term
    for h in range(4):
        out_ref[h * D : (h + 1) * D] = jnp.broadcast_to(acc[h].astype(BF)[None], (D, TS, NB))


def modal_kernel(pos, in_ref, shapes_ref, flex_ref, damp_ref, out_ref, hold_ref):
    force = in_ref[...].reshape(NT, NB)
    shapes = shapes_ref[...]
    real = dot_nt(shapes, force)
    imag = None
    damp = jnp.concatenate([damp_ref[...], jnp.zeros((6, MODES), F32)], axis=0).T
    omega, zeta = damp[:, 0:1], damp[:, 1:2]
    size = jnp.exp(-omega * zeta)
    angle = omega * jnp.sqrt(1.0 - zeta * zeta)
    pr, pi = size * jnp.cos(angle), size * jnp.sin(angle)
    lane = lax.broadcasted_iota(jnp.int32, (MODES, NT), 1)
    shift = 1
    while shift < NT:
        keep = lane >= shift
        sr = jnp.where(keep, pltpu.roll(real, shift, 1), 0.0)
        if imag is None:
            real, imag = real + pr * sr, pi * sr
        else:
            si = jnp.where(keep, pltpu.roll(imag, shift, 1), 0.0)
            real, imag = real + (pr * sr - pi * si), imag + (pr * si + pi * sr)
        pr, pi = pr * pr - pi * pi, 2.0 * pr * pi
        shift *= 2
    hold_ref[...] = lax.dot_general(
        imag,
        shapes.astype(F32),
        (((0,), (0,)), ((), ())),
        precision=HI,
        preferred_element_type=F32,
    ) + dot_nt(force, flex_ref[...])
    block = hold_ref[pl.ds(pl.multiple_of(pos[2] * TD, TD), TD), :].astype(BF)
    out_ref[...] = jnp.broadcast_to(block[None], out_ref.shape)


def inverse_kernel(pos, table_ref, in_ref, out_ref):
    acc = [None] * 4
    for z in range(Z):
        block = in_ref[z].astype(F32)
        for s in range(4):
            term = block * table_ref[0, 0, z * 4 + s]
            acc[s] = term if acc[s] is None else acc[s] + term
    for s in range(4):
        out_ref[s * D : (s + 1) * D] = jnp.broadcast_to(acc[s].astype(BF)[None], (D, TD, NB))


def stress_kernel(in_ref, map_ref, out_ref, motion_ref):
    @pl.when(pl.program_id(0) == 0)
    def _():
        total = None
        for q in range(YL * C):
            part = in_ref[q * D : (q + 1) * D].astype(F32)
            total = part if total is None else total + part
        motion_ref[...] = total.reshape(NT, NB).astype(BF)

    out_ref[...] = dot_nt(map_ref[...], motion_ref[...]).astype(BF)


def whole(shape):
    return pl.BlockSpec(shape, lambda *_: (0,) * len(shape))


def call(kernel, pos, out, in_specs, *args, scratch=()):
    return pl.pallas_call(
        kernel,
        out_shape=jax.ShapeDtypeStruct(out, BF),
        grid_spec=pltpu.PrefetchScalarGridSpec(
            num_scalar_prefetch=1,
            grid=(1,),
            in_specs=in_specs,
            out_specs=whole(out),
            scratch_shapes=list(scratch),
        ),
        compiler_params=pltpu.CompilerParams(vmem_limit_bytes=24 * 1024 * 1024),
    )(pos, *args)


def local(wake, basis, block_index, phase_index, shapes, flex, omega, zeta, stress_map):
    yl, z, c = lax.axis_index("yl"), lax.axis_index("z"), lax.axis_index("c")
    d = lax.axis_index("x") * 2 + lax.axis_index("yh")
    pos = jnp.stack([yl, c, d, z, (yl * C + c) * Z + z]).astype(jnp.int32)
    index = jnp.concatenate([block_index, phase_index], axis=0)

    send = lax.dynamic_slice(basis[0], (0, (1 - yl) * HALF), (NB, HALF))
    send = jnp.concatenate([send, jnp.pad(index.astype(BF), ((0, 14), (0, HALF - NT)))], axis=0)
    got = lax.ppermute(send, "yl", [(0, 1), (1, 0)])

    mine = jnp.transpose(wake[0].reshape(PH, YL, HALF), (1, 0, 2))
    mine = jnp.broadcast_to(mine[:, None], (YL, Z, PH, HALF)).reshape(YL * Z, PH, HALF)
    own = lax.all_to_all(mine, ("yl", "z"), 0, 0, tiled=True)
    other = lax.ppermute(own, "c", [(0, 1), (1, 0)])

    picked = call(
        project_kernel,
        pos,
        (PEERS, 2 * TS, NB),
        [
            whole((YL * Z, PH, HALF)),
            whole((YL * Z, PH, HALF)),
            pl.BlockSpec((NB, HALF), lambda i, p: (0, p[0])),
            whole((NB + 16, HALF)),
            whole((2, NT)),
        ],
        own,
        other,
        basis[0],
        got,
        index,
    )
    parts = lax.all_to_all(picked, PLANE, 0, 0, tiled=True)
    forcing = pl.pallas_call(
        gather_sum_kernel, out_shape=jax.ShapeDtypeStruct((Z, 4 * TS, NB), BF)
    )(parts)
    forcing = lax.all_to_all(forcing, "z", 0, 0, tiled=True)
    harmonic = call(
        forward_kernel,
        pos,
        (PEERS, TS, NB),
        [
            pl.BlockSpec((1, 1, 256), lambda i, p: (p[3], 0, 0), memory_space=pltpu.SMEM),
            whole((Z, 4 * TS, NB)),
        ],
        jnp.asarray(FORWARD),
        forcing,
    )
    harmonic = lax.all_to_all(harmonic, PLANE, 0, 0, tiled=True)
    physical = call(
        modal_kernel,
        pos,
        (Z, TD, NB),
        [whole((PEERS, TS, NB)), whole((MODES, NB)), whole((NB, NB)), whole((2, MODES))],
        harmonic,
        shapes[0],
        flex[0],
        jnp.concatenate([omega, zeta], axis=0),
        scratch=[pltpu.VMEM((NT, NB), F32)],
    )
    physical = lax.all_to_all(physical, "z", 0, 0, tiled=True)
    sectoral = call(
        inverse_kernel,
        pos,
        (PEERS, TD, NB),
        [
            pl.BlockSpec((1, 1, 64), lambda i, p: (p[4], 0, 0), memory_space=pltpu.SMEM),
            whole((Z, TD, NB)),
        ],
        jnp.asarray(INVERSE),
        physical,
    )
    sectoral = lax.all_to_all(sectoral, PLANE, 0, 0, tiled=True)
    rows = stress_map.shape[1]
    step = rows // 4
    stress = pl.pallas_call(
        stress_kernel,
        out_shape=jax.ShapeDtypeStruct((rows, NT), BF),
        grid=(rows // step,),
        in_specs=[
            whole((PEERS, TD, NB)),
            pl.BlockSpec((step, NB), lambda i: (i, 0)),
        ],
        out_specs=pl.BlockSpec((step, NT), lambda i: (i, 0)),
        scratch_shapes=[pltpu.VMEM((NT, NB), BF)],
    )(sectoral, stress_map[0])
    return stress[None]


def solution(mesh):
    sector, dof = ("yl", "z", "c"), ("x", "yh")
    return jax.shard_map(
        local,
        mesh=Mesh(mesh.devices.reshape(SIZES), AXES),
        in_specs=(
            P(sector, None, dof),
            P(sector, None, dof),
            P(sector, None),
            P(sector, None),
            P(sector, None, None),
            P(sector, None, None),
            P(sector, None),
            P(sector, None),
            P(sector, dof, None),
        ),
        out_specs=P(sector, dof, None),
        check_vma=False,
    )
```

```python
import numpy as np
import jax
import jax.numpy as jnp
from jax import lax
from jax.experimental import pallas as pl
from jax.experimental.pallas import tpu as pltpu
from jax.sharding import Mesh, PartitionSpec as P

AXES = ("yl", "z", "c", "x", "yh")
SIZES = (2, 16, 2, 4, 2)
PLANE = ("yl", "c", "x", "yh")
YL, Z, C, D = 2, 16, 2, 8
PEERS = YL * C * D
BLADES, PH, NT, NB, MODES = YL * Z * C, 8, 256, 128, 40
HALF = 896
TS = NT // PEERS
TD = NT // D
BF = jnp.bfloat16
F32 = jnp.float32
HI = lax.Precision.HIGHEST


def fourier_table(count):
    h = np.arange(count)[:, None]
    s = np.arange(count)[None, :]
    angle = 2.0 * np.pi * ((((h + 1) // 2) * s) % count) / count
    table = np.where(h % 2 == 1, np.cos(angle), np.sin(angle))
    table = np.where(h == 0, 1.0, table)
    edges = (h == 0) | (h == count - 1)
    return table * np.where(edges, np.sqrt(1.0 / count), np.sqrt(2.0 / count))


FOURIER = fourier_table(BLADES)
FORWARD = np.ascontiguousarray(
    FOURIER.reshape(YL, Z, C, YL, Z, C).transpose(1, 4, 3, 5, 0, 2).reshape(Z, 256)
).astype(np.float32)
INVERSE = np.ascontiguousarray(
    FOURIER.reshape(YL, Z, C, YL, Z, C).transpose(0, 2, 4, 1, 3, 5).reshape(YL * C * Z, 64)
).astype(np.float32)


def dot_nt(a, b, **kw):
    return lax.dot_general(
        a, b, (((1,), (1,)), ((), ())), preferred_element_type=F32, **kw
    )


def spread_kernel(in_ref, out_ref):
    for half in range(YL):
        part = in_ref[:, half * HALF : (half + 1) * HALF]
        out_ref[half * Z : (half + 1) * Z] = jnp.broadcast_to(part[None], (Z, PH, HALF))


def pack_kernel(pos, basis_ref, block_ref, phase_ref, near_ref, far_ref):
    index = jnp.concatenate(
        [block_ref[...].astype(F32), phase_ref[...].astype(F32), jnp.zeros((14, NT), F32)], axis=0
    )
    index = jnp.concatenate([index, jnp.zeros((16, HALF - NT), F32)], axis=1).astype(BF)
    for k, ref in enumerate((near_ref, far_ref)):
        half = (pos[0] + k) & 1
        ref[0:NB] = basis_ref[:, pl.ds(pl.multiple_of(half * HALF, 128), HALF)]
        ref[NB : NB + 16] = index


def project_kernel(pos, wake_ref, *refs):
    out_ref = refs[-1]
    basis = jnp.concatenate([ref[0:NB] for ref in refs[:4]], axis=0)
    table = dot_nt(wake_ref[...].reshape(YL * Z * PH, HALF), basis).astype(BF)
    pair = lax.broadcasted_iota(jnp.int32, (NT, YL * Z * PH), 1).astype(F32)
    codes = []
    for ref in refs[:4]:
        index = ref[NB : NB + 16, 0:NT].astype(F32)
        block, phase = index[0:1].astype(jnp.int32), index[1:2].astype(jnp.int32)
        code = ((block >> 1) * PH + phase).astype(F32)
        codes.append(jnp.where((block & 1) == pos[1], code, -1.0))
    codes = jnp.concatenate(codes + [jnp.zeros((4, NT), F32)], axis=0).T
    picks = []
    for r in range(4):
        onehot = jnp.where(codes[:, r : r + 1] == pair, 1.0, 0.0).astype(BF)
        part = jnp.dot(onehot, table[:, r * NB : (r + 1) * NB], preferred_element_type=F32)
        picks.append(part.reshape(PEERS, TS, NB))
    out_ref[...] = jnp.concatenate(picks, axis=1).astype(BF)


def gather_sum_kernel(in_ref, out_ref):
    sums = {}
    for yl in range(YL):
        for c in range(C):
            total = None
            for d in range(D):
                part = in_ref[(yl * C + c) * D + d].astype(F32)
                total = part if total is None else total + part
            sums[yl, c] = total
    rows = []
    for yl in range(YL):
        for c in range(C):
            total = None
            for y in range(YL):
                for k in range(C):
                    r = (yl ^ y) + 2 * (c ^ k)
                    part = sums[y, k][r * TS : (r + 1) * TS]
                    total = part if total is None else total + part
            rows.append(total)
    block = jnp.concatenate(rows, axis=0).astype(BF)
    out_ref[...] = jnp.broadcast_to(block[None], out_ref.shape)


def forward_kernel(table_ref, in_ref, out_ref):
    acc = [None] * 4
    for z in range(Z):
        block = in_ref[z].astype(F32)
        for q in range(4):
            part = block[q * TS : (q + 1) * TS]
            for h in range(4):
                term = part * table_ref[(z * 4 + q) * 4 + h]
                acc[h] = term if acc[h] is None else acc[h] + term
    for h in range(4):
        out_ref[h * D : (h + 1) * D] = jnp.broadcast_to(acc[h].astype(BF)[None], (D, TS, NB))


def modal_kernel(pos, in_ref, shapes_ref, flex_ref, damp_ref, out_ref, hold_ref):
    force = in_ref[...].reshape(NT, NB)
    shapes = shapes_ref[...]
    real = dot_nt(shapes, force)
    imag = None
    damp = jnp.concatenate([damp_ref[...], jnp.zeros((6, MODES), F32)], axis=0).T
    omega, zeta = damp[:, 0:1], damp[:, 1:2]
    size = jnp.exp(-omega * zeta)
    angle = omega * jnp.sqrt(1.0 - zeta * zeta)
    pr, pi = size * jnp.cos(angle), size * jnp.sin(angle)
    lane = lax.broadcasted_iota(jnp.int32, (MODES, NT), 1)
    shift = 1
    while shift < NT:
        keep = lane >= shift
        sr = jnp.where(keep, pltpu.roll(real, shift, 1), 0.0)
        if imag is None:
            real, imag = real + pr * sr, pi * sr
        else:
            si = jnp.where(keep, pltpu.roll(imag, shift, 1), 0.0)
            real, imag = real + (pr * sr - pi * si), imag + (pr * si + pi * sr)
        pr, pi = pr * pr - pi * pi, 2.0 * pr * pi
        shift *= 2
    hold_ref[...] = lax.dot_general(
        imag,
        shapes.astype(F32),
        (((0,), (0,)), ((), ())),
        precision=HI,
        preferred_element_type=F32,
    ) + dot_nt(force, flex_ref[...])
    block = hold_ref[pl.ds(pl.multiple_of(pos[2] * TD, TD), TD), :].astype(BF)
    out_ref[...] = jnp.broadcast_to(block[None], out_ref.shape)


def inverse_kernel(table_ref, in_ref, out_ref):
    acc = [None] * 4
    for z in range(Z):
        block = in_ref[z].astype(F32)
        for s in range(4):
            term = block * table_ref[z * 4 + s]
            acc[s] = term if acc[s] is None else acc[s] + term
    for s in range(4):
        out_ref[s * D : (s + 1) * D] = jnp.broadcast_to(acc[s].astype(BF)[None], (D, TD, NB))


CHUNKS = 4


def stress_kernel(in_ref, map_ref, out_ref, hold_ref, sems):
    total = None
    for q in range(YL * C):
        part = in_ref[q * D : (q + 1) * D].astype(F32)
        total = part if total is None else total + part
    motion = total.reshape(NT, NB).astype(BF)
    step = map_ref.shape[0] // CHUNKS
    copies = []
    for k in range(CHUNKS):
        rows = pl.ds(k * step, step)
        hold_ref[rows] = dot_nt(map_ref[rows], motion).astype(BF)
        copies.append(pltpu.make_async_copy(hold_ref.at[rows], out_ref.at[rows], sems.at[k]))
        copies[-1].start()
    for copy in copies:
        copy.wait()


VMEM = pl.BlockSpec(memory_space=pltpu.VMEM)
SMEM = pl.BlockSpec(memory_space=pltpu.SMEM)


def call(kernel, outs, specs, *args, out_specs=None, scratch=()):
    outs = [jax.ShapeDtypeStruct(shape, BF) for shape in outs]
    got = pl.pallas_call(
        kernel,
        out_shape=outs,
        in_specs=specs,
        out_specs=out_specs or [VMEM] * len(outs),
        scratch_shapes=list(scratch),
        compiler_params=pltpu.CompilerParams(vmem_limit_bytes=24 * 1024 * 1024),
    )(*args)
    return got[0] if len(outs) == 1 else got


def local(wake, basis, block_index, phase_index, shapes, flex, omega, zeta, stress_map):
    yl, z, c = lax.axis_index("yl"), lax.axis_index("z"), lax.axis_index("c")
    d = lax.axis_index("x") * 2 + lax.axis_index("yh")
    pos = jnp.stack([yl, c, d]).astype(jnp.int32)
    forward = lax.dynamic_slice(jnp.asarray(FORWARD), (z, 0), (1, 256)).reshape(256)
    inverse = lax.dynamic_slice(jnp.asarray(INVERSE), ((yl * C + c) * Z + z, 0), (1, 64)).reshape(64)
    damp = jnp.concatenate([omega, zeta], axis=0)

    spread = call(spread_kernel, [(YL * Z, PH, HALF)], [VMEM], wake[0])
    blocks = lax.all_to_all(spread, ("yl", "z"), 0, 0, tiled=True)

    near, far = call(
        pack_kernel,
        [(NB + 16, HALF)] * 2,
        [SMEM, VMEM, VMEM, VMEM],
        pos,
        basis[0],
        block_index,
        phase_index,
    )
    swap = [(0, 1), (1, 0)]
    by_yl = lax.ppermute(far, "yl", swap)
    by_c = lax.ppermute(near, "c", swap)
    by_both = lax.ppermute(far, ("yl", "c"), [(0, 3), (1, 2), (2, 1), (3, 0)])

    picked = call(
        project_kernel,
        [(PEERS, 4 * TS, NB)],
        [SMEM] + [VMEM] * 5,
        pos,
        blocks,
        near,
        by_yl,
        by_c,
        by_both,
    )
    parts = lax.all_to_all(picked, PLANE, 0, 0, tiled=True)
    forcing = call(gather_sum_kernel, [(Z, 4 * TS, NB)], [VMEM], parts)
    forcing = lax.all_to_all(forcing, "z", 0, 0, tiled=True)
    harmonic = call(forward_kernel, [(PEERS, TS, NB)], [SMEM, VMEM], forward, forcing)
    harmonic = lax.all_to_all(harmonic, PLANE, 0, 0, tiled=True)
    physical = call(
        modal_kernel,
        [(Z, TD, NB)],
        [SMEM] + [VMEM] * 4,
        pos,
        harmonic,
        shapes[0],
        flex[0],
        damp,
        scratch=[pltpu.VMEM((NT, NB), F32)],
    )
    physical = lax.all_to_all(physical, "z", 0, 0, tiled=True)
    sectoral = call(inverse_kernel, [(PEERS, TD, NB)], [SMEM, VMEM], inverse, physical)
    sectoral = lax.all_to_all(sectoral, PLANE, 0, 0, tiled=True)
    rows = stress_map.shape[1]
    stress = call(
        stress_kernel,
        [(rows, NT)],
        [VMEM, VMEM],
        sectoral,
        stress_map[0],
        out_specs=[pl.BlockSpec(memory_space=pl.ANY)],
        scratch=[pltpu.VMEM((rows, NT), BF), pltpu.SemaphoreType.DMA((CHUNKS,))],
    )
    return stress[None]


def solution(mesh):
    sector, dof = ("yl", "z", "c"), ("x", "yh")
    return jax.shard_map(
        local,
        mesh=Mesh(mesh.devices.reshape(SIZES), AXES),
        in_specs=(
            P(sector, None, dof),
            P(sector, None, dof),
            P(sector, None),
            P(sector, None),
            P(sector, None, None),
            P(sector, None, None),
            P(sector, None),
            P(sector, None),
            P(sector, dof, None),
        ),
        out_specs=P(sector, dof, None),
        check_vma=False,
    )
```

```python
import numpy as np
import jax
import jax.numpy as jnp
from jax import lax
from jax.experimental import pallas as pl
from jax.experimental.pallas import tpu as pltpu
from jax.sharding import Mesh, PartitionSpec as P

AXES = ("yl", "z", "c", "x", "yh")
SIZES = (2, 16, 2, 4, 2)
PLANE = ("yl", "c", "x", "yh")
YL, Z, C, D = 2, 16, 2, 8
PEERS = YL * C * D
BLADES, PH, NT, NB, MODES = YL * Z * C, 8, 256, 128, 40
HALF = 896
TS = NT // PEERS
BF = jnp.bfloat16
F32 = jnp.float32
HI = lax.Precision.HIGHEST


def fourier_table(count):
    h = np.arange(count)[:, None]
    s = np.arange(count)[None, :]
    angle = 2.0 * np.pi * ((((h + 1) // 2) * s) % count) / count
    table = np.where(h % 2 == 1, np.cos(angle), np.sin(angle))
    table = np.where(h == 0, 1.0, table)
    edges = (h == 0) | (h == count - 1)
    return table * np.where(edges, np.sqrt(1.0 / count), np.sqrt(2.0 / count))


FOURIER = fourier_table(BLADES).reshape(YL, Z, C, YL, Z, C)
EYE = np.eye(TS)


def halves(table):
    high = table.astype(np.float32).astype(BF)
    low = (table - high.astype(np.float64)).astype(np.float32).astype(BF)
    return np.stack([high, low], axis=1)


def forward_table():
    table = FOURIER.reshape(YL, D, 2, C, YL, Z, C).transpose(0, 3, 1, 2, 5, 4, 6)
    table = np.stack([table, table[:, :, :, ::-1]]).reshape(2, BLADES, BLADES)
    return np.einsum("pij,tu->pitju", table, EYE).reshape(2, BLADES * TS, BLADES * TS)


def inverse_table():
    table = FOURIER.reshape(YL, D, 2, C, YL, Z, C).transpose(5, 4, 6, 0, 3, 1, 2)
    table = np.stack([table[z] if z % 2 == 0 else table[z][..., ::-1] for z in range(Z)])
    table = table.reshape(Z, 4, BLADES)
    return np.einsum("zij,tu->zitju", table, EYE).reshape(Z, 4 * TS, BLADES * TS)


FORWARD = halves(forward_table())
INVERSE = halves(inverse_table())
PACK = 2 * MODES + NB


def dot_nt(a, b, **kw):
    return lax.dot_general(
        a, b, (((1,), (1,)), ((), ())), preferred_element_type=F32, **kw
    )


def spread_kernel(in_ref, out_ref):
    for half in range(YL):
        part = in_ref[:, half * HALF : (half + 1) * HALF]
        out_ref[half * Z : (half + 1) * Z] = jnp.broadcast_to(part[None], (Z, PH, HALF))


def pack_kernel(pos, basis_ref, block_ref, phase_ref, near_ref, far_ref):
    index = jnp.concatenate(
        [block_ref[...].astype(F32), phase_ref[...].astype(F32), jnp.zeros((14, NT), F32)], axis=0
    )
    index = jnp.concatenate([index, jnp.zeros((16, HALF - NT), F32)], axis=1).astype(BF)
    for k, ref in enumerate((near_ref, far_ref)):
        half = (pos[0] + k) & 1
        ref[0:NB] = basis_ref[:, pl.ds(pl.multiple_of(half * HALF, 128), HALF)]
        ref[NB : NB + 16] = index


def project_kernel(pos, kept_ref, wake_ref, *refs):
    out_ref = refs[-1]
    basis = jnp.concatenate([ref[0:NB] for ref in refs[:4]], axis=0)
    table = dot_nt(wake_ref[...].reshape(YL * Z * PH, HALF), basis).astype(BF)
    pair = lax.broadcasted_iota(jnp.int32, (NT, YL * Z * PH), 1).astype(F32)
    codes = []
    for ref in refs[:4]:
        index = ref[NB : NB + 16, 0:NT].astype(F32)
        block, phase = index[0:1].astype(jnp.int32), index[1:2].astype(jnp.int32)
        code = ((block >> 1) * PH + phase).astype(F32)
        codes.append(jnp.where((block & 1) == pos[1], code, -1.0))
    codes = jnp.concatenate(codes + [jnp.zeros((4, NT), F32)], axis=0).T
    picks = []
    for r in range(4):
        onehot = jnp.where(codes[:, r : r + 1] == pair, 1.0, 0.0).astype(BF)
        part = jnp.dot(onehot, table[:, r * NB : (r + 1) * NB], preferred_element_type=F32)
        picks.append(part.reshape(PEERS, TS, NB))
    out_ref[...] = jnp.concatenate(picks, axis=1).astype(BF)


def gather_sum_kernel(in_ref, out_ref):
    sums = {}
    for yl in range(YL):
        for c in range(C):
            total = None
            for d in range(D):
                part = in_ref[(yl * C + c) * D + d].astype(F32)
                total = part if total is None else total + part
            sums[yl, c] = total
    rows = []
    for yl in range(YL):
        for c in range(C):
            total = None
            for y in range(YL):
                for k in range(C):
                    r = (yl ^ y) + 2 * (c ^ k)
                    part = sums[y, k][r * TS : (r + 1) * TS]
                    total = part if total is None else total + part
            rows.append(total)
    block = jnp.concatenate(rows, axis=0).astype(BF)
    out_ref[...] = jnp.broadcast_to(block[None], out_ref.shape)


def fourier_sum(table_ref, in_ref):
    block = in_ref[...].reshape(BLADES * TS, NB)
    return sum(
        jnp.dot(table_ref[k], block, preferred_element_type=F32) for k in range(2)
    ).astype(BF)


def forward_kernel(table_ref, in_ref, kept_ref, out_ref):
    out_ref[...] = fourier_sum(table_ref, in_ref).reshape(PEERS, 2 * TS, NB)


def inverse_kernel(table_ref, in_ref, out_ref):
    block = fourier_sum(table_ref, in_ref)
    for s in range(4):
        part = block[s * TS : (s + 1) * TS]
        out_ref[s * D : (s + 1) * D] = jnp.broadcast_to(part[None], (D, TS, NB))


def parameter_kernel(shapes_ref, flex_ref, omega_ref, zeta_ref, out_ref):
    damp = jnp.concatenate([omega_ref[...], zeta_ref[...], jnp.zeros((6, MODES), F32)], axis=0).T
    omega, zeta = damp[:, 0:1], damp[:, 1:2]
    size = jnp.exp(-omega * zeta)
    angle = omega * jnp.sqrt(1.0 - zeta * zeta)
    real, imag = size * jnp.cos(angle), size * jnp.sin(angle)
    lane = lax.broadcasted_iota(jnp.int32, (MODES, NB), 1)
    powers = jnp.zeros((MODES, NB), F32)
    for k in range(8):
        powers = jnp.where(lane == 2 * k, real, jnp.where(lane == 2 * k + 1, imag, powers))
        real, imag = real * real - imag * imag, 2.0 * real * imag
    high = powers.astype(BF).astype(F32)
    middle = (powers - high).astype(BF).astype(F32)
    low = powers - high - middle
    terms = high + pltpu.roll(middle, 16, 1) + pltpu.roll(low, 32, 1)
    out_ref[...] = jnp.concatenate(
        [shapes_ref[...].astype(F32), terms, flex_ref[...].astype(F32)], axis=0
    ).astype(BF)


def respond(force, pack_ref):
    shapes = pack_ref[0 : 2 * MODES][0:MODES]
    terms = pack_ref[0 : 2 * MODES][MODES : 2 * MODES].astype(F32)
    powers = terms[:, 0:16] + terms[:, 16:32] + terms[:, 32:48]
    real = dot_nt(shapes, force)
    imag = None
    lane = lax.broadcasted_iota(jnp.int32, (MODES, NT), 1)
    for k in range(8):
        pr, pi = powers[:, 2 * k : 2 * k + 1], powers[:, 2 * k + 1 : 2 * k + 2]
        keep = lane >= 2**k
        sr = jnp.where(keep, pltpu.roll(real, 2**k, 1), 0.0)
        if imag is None:
            real, imag = real + pr * sr, pi * sr
        else:
            si = jnp.where(keep, pltpu.roll(imag, 2**k, 1), 0.0)
            real, imag = real + (pr * sr - pi * si), imag + (pr * si + pi * sr)
    return lax.dot_general(
        imag,
        shapes.astype(F32),
        (((0,), (0,)), ((), ())),
        precision=HI,
        preferred_element_type=F32,
    ) + dot_nt(force, pack_ref[2 * MODES : PACK])


def modal_kernel(in_ref, first_ref, second_ref, out_ref):
    parts = []
    for e, pack_ref in enumerate((first_ref, second_ref)):
        force = in_ref[...].astype(F32)[:, e * TS : (e + 1) * TS].reshape(NT, NB).astype(BF)
        parts.append(respond(force, pack_ref).reshape(PEERS, TS, NB))
    out_ref[...] = jnp.concatenate(parts, axis=1).astype(BF)


CHUNKS = 4


def stress_kernel(in_ref, map_ref, out_ref, hold_ref, sems):
    motion = in_ref[...].reshape(NT, NB)
    step = map_ref.shape[0] // CHUNKS
    copies = []
    for k in range(CHUNKS):
        rows = pl.ds(k * step, step)
        hold_ref[rows] = dot_nt(map_ref[rows], motion).astype(BF)
        copies.append(pltpu.make_async_copy(hold_ref.at[rows], out_ref.at[rows], sems.at[k]))
        copies[-1].start()
    for copy in copies:
        copy.wait()


VMEM = pl.BlockSpec(memory_space=pltpu.VMEM)
SMEM = pl.BlockSpec(memory_space=pltpu.SMEM)
HBM = pl.BlockSpec(memory_space=pl.ANY)


def call(kernel, outs, specs, *args, out_specs=None, scratch=()):
    outs = [jax.ShapeDtypeStruct(shape, BF) for shape in outs]
    got = pl.pallas_call(
        kernel,
        out_shape=outs,
        in_specs=specs,
        out_specs=out_specs or [VMEM] * len(outs),
        scratch_shapes=list(scratch),
        compiler_params=pltpu.CompilerParams(vmem_limit_bytes=24 * 1024 * 1024),
    )(*args)
    return got[0] if len(outs) == 1 else got


def local(wake, basis, block_index, phase_index, shapes, flex, omega, zeta, stress_map):
    yl, z, c = lax.axis_index("yl"), lax.axis_index("z"), lax.axis_index("c")
    pos = jnp.stack([yl, c]).astype(jnp.int32)
    forward = lax.dynamic_slice(
        jnp.asarray(FORWARD), (z & 1, 0, 0, 0), (1,) + FORWARD.shape[1:]
    )[0]
    inverse = lax.dynamic_slice(jnp.asarray(INVERSE), (z, 0, 0, 0), (1,) + INVERSE.shape[1:])[0]

    pack = call(parameter_kernel, [(PACK, NB)], [VMEM] * 4, shapes[0], flex[0], omega, zeta)
    route = [
        [(i * D + k, (2 * k + (i & 1 ^ e)) * D + i // 2) for i in range(Z) for k in range(D)]
        for e in range(2)
    ]
    first = lax.ppermute(pack, ("z", "x", "yh"), route[0])

    spread = call(spread_kernel, [(YL * Z, PH, HALF)], [VMEM], wake[0])
    blocks = lax.all_to_all(spread, ("yl", "z"), 0, 0, tiled=True)

    near, far = call(
        pack_kernel,
        [(NB + 16, HALF)] * 2,
        [SMEM, VMEM, VMEM, VMEM],
        pos,
        basis[0],
        block_index,
        phase_index,
    )
    swap = [(0, 1), (1, 0)]
    by_yl = lax.ppermute(far, "yl", swap)
    by_c = lax.ppermute(near, "c", swap)
    by_both = lax.ppermute(far, ("yl", "c"), [(0, 3), (1, 2), (2, 1), (3, 0)])

    picked = call(
        project_kernel,
        [(PEERS, 4 * TS, NB)],
        [SMEM, HBM] + [VMEM] * 5,
        pos,
        first,
        blocks,
        near,
        by_yl,
        by_c,
        by_both,
    )
    pack, picked = lax.optimization_barrier((pack, picked))
    second = lax.ppermute(pack, ("z", "x", "yh"), route[1])
    parts = lax.all_to_all(picked, PLANE, 0, 0, tiled=True)
    forcing = call(gather_sum_kernel, [(Z, 4 * TS, NB)], [VMEM], parts)
    forcing = lax.all_to_all(forcing, "z", 0, 0, tiled=True)
    harmonic = call(
        forward_kernel, [(PEERS, 2 * TS, NB)], [VMEM, VMEM, HBM], forward, forcing, second
    )
    harmonic = lax.all_to_all(harmonic, PLANE, 0, 0, tiled=True)
    physical = call(modal_kernel, [(PEERS, 2 * TS, NB)], [VMEM] * 3, harmonic, first, second)
    physical = lax.all_to_all(physical, PLANE, 0, 0, tiled=True)
    sectoral = call(inverse_kernel, [(PEERS, TS, NB)], [VMEM] * 2, inverse, physical)
    sectoral = lax.all_to_all(sectoral, PLANE, 0, 0, tiled=True)
    rows = stress_map.shape[1]
    stress = call(
        stress_kernel,
        [(rows, NT)],
        [VMEM, VMEM],
        sectoral,
        stress_map[0],
        out_specs=[HBM],
        scratch=[pltpu.VMEM((rows, NT), BF), pltpu.SemaphoreType.DMA((CHUNKS,))],
    )
    return stress[None]


def solution(mesh):
    sector, dof = ("yl", "z", "c"), ("x", "yh")
    return jax.shard_map(
        local,
        mesh=Mesh(mesh.devices.reshape(SIZES), AXES),
        in_specs=(
            P(sector, None, dof),
            P(sector, None, dof),
            P(sector, None),
            P(sector, None),
            P(sector, None, None),
            P(sector, None, None),
            P(sector, None),
            P(sector, None),
            P(sector, dof, None),
        ),
        out_specs=P(sector, dof, None),
        check_vma=False,
    )
```

```python
import numpy as np
import jax
import jax.numpy as jnp
from jax import lax
from jax.experimental import pallas as pl
from jax.experimental.pallas import tpu as pltpu
from jax.sharding import Mesh, PartitionSpec as P

AXES = ("yl", "z", "c", "x", "yh")
SIZES = (2, 16, 2, 4, 2)
PLANE = ("yl", "c", "x", "yh")
YL, Z, C, D = 2, 16, 2, 8
PEERS = YL * C * D
BLADES, PH, NT, NB, MODES = YL * Z * C, 8, 256, 128, 40
HALF = 896
TS = NT // PEERS
TD = NT // D
BF = jnp.bfloat16
F32 = jnp.float32
HI = lax.Precision.HIGHEST


def fourier_table(count):
    h = np.arange(count)[:, None]
    s = np.arange(count)[None, :]
    angle = 2.0 * np.pi * ((((h + 1) // 2) * s) % count) / count
    table = np.where(h % 2 == 1, np.cos(angle), np.sin(angle))
    table = np.where(h == 0, 1.0, table)
    edges = (h == 0) | (h == count - 1)
    return table * np.where(edges, np.sqrt(1.0 / count), np.sqrt(2.0 / count))


FOURIER = fourier_table(BLADES)


def forward_table():
    table = FOURIER.reshape(YL, Z, C, YL, Z, C).transpose(1, 0, 2, 4, 3, 5)
    table = np.einsum("zij,tu->zitju", table.reshape(Z, 4, BLADES), np.eye(TS))
    table = table.reshape(Z, 4 * TS, BLADES * TS).astype(np.float32)
    high = table.astype(BF)
    return np.stack([high, (table - high.astype(np.float32)).astype(BF)], axis=1)


FORWARD = forward_table()
INVERSE = np.ascontiguousarray(
    FOURIER.reshape(YL, Z, C, YL, Z, C).transpose(0, 2, 4, 1, 3, 5).reshape(YL * C * Z, 64)
).astype(np.float32)


def dot_nt(a, b, **kw):
    return lax.dot_general(
        a, b, (((1,), (1,)), ((), ())), preferred_element_type=F32, **kw
    )


def spread_kernel(in_ref, out_ref, sem):
    copies = []
    for half in range(YL):
        part = in_ref.at[:, pl.ds(half * HALF, HALF)]
        for z in range(Z):
            k = half * Z + z
            copies.append(pltpu.make_async_copy(part, out_ref.at[k], sem.at[k]))
            copies[-1].start()
    for copy in copies:
        copy.wait()


def pack_kernel(pos, basis_ref, block_ref, phase_ref, near_ref, far_ref):
    index = jnp.concatenate(
        [block_ref[...].astype(F32), phase_ref[...].astype(F32), jnp.zeros((14, NT), F32)], axis=0
    )
    index = jnp.concatenate([index, jnp.zeros((16, HALF - NT), F32)], axis=1).astype(BF)
    for k, ref in enumerate((near_ref, far_ref)):
        half = (pos[0] + k) & 1
        ref[0:NB] = basis_ref[:, pl.ds(pl.multiple_of(half * HALF, 128), HALF)]
        ref[NB : NB + 16] = index


def project_kernel(pos, wake_ref, *refs):
    out_ref = refs[-1]
    basis = jnp.concatenate([ref[0:NB] for ref in refs[:4]], axis=0)
    table = dot_nt(wake_ref[...].reshape(YL * Z * PH, HALF), basis).astype(BF)
    pair = lax.broadcasted_iota(jnp.int32, (NT, YL * Z * PH), 1).astype(F32)
    codes = []
    for ref in refs[:4]:
        index = ref[NB : NB + 16, 0:NT].astype(F32)
        block, phase = index[0:1].astype(jnp.int32), index[1:2].astype(jnp.int32)
        code = ((block >> 1) * PH + phase).astype(F32)
        codes.append(jnp.where((block & 1) == pos[1], code, -1.0))
    codes = jnp.concatenate(codes + [jnp.zeros((4, NT), F32)], axis=0).T
    picks = []
    for r in range(4):
        onehot = jnp.where(codes[:, r : r + 1] == pair, 1.0, 0.0).astype(BF)
        part = jnp.dot(onehot, table[:, r * NB : (r + 1) * NB], preferred_element_type=F32)
        picks.append(part.reshape(PEERS, TS, NB))
    out_ref[...] = jnp.concatenate(picks, axis=1).astype(BF)


def gather_sum_kernel(in_ref, out_ref):
    sums = {}
    for yl in range(YL):
        for c in range(C):
            total = None
            for d in range(D):
                part = in_ref[(yl * C + c) * D + d].astype(F32)
                total = part if total is None else total + part
            sums[yl, c] = total
    rows = []
    for yl in range(YL):
        for c in range(C):
            total = None
            for y in range(YL):
                for k in range(C):
                    r = (yl ^ y) + 2 * (c ^ k)
                    part = sums[y, k][r * TS : (r + 1) * TS]
                    total = part if total is None else total + part
            rows.append(total)
    block = jnp.concatenate(rows, axis=0).astype(BF)
    out_ref[...] = jnp.broadcast_to(block[None], out_ref.shape)


def forward_kernel(table_ref, in_ref, out_ref):
    block = in_ref[...].reshape(BLADES * TS, NB)
    block = sum(jnp.dot(table_ref[k], block, preferred_element_type=F32) for k in range(2))
    for h in range(4):
        part = block[h * TS : (h + 1) * TS].astype(BF)
        out_ref[h * D : (h + 1) * D] = jnp.broadcast_to(part[None], (D, TS, NB))


def powers_kernel(omega_ref, zeta_ref, out_ref):
    damp = jnp.concatenate([omega_ref[...], zeta_ref[...], jnp.zeros((6, MODES), F32)], axis=0).T
    omega, zeta = damp[:, 0:1], damp[:, 1:2]
    size = jnp.exp(-omega * zeta)
    angle = omega * jnp.sqrt(1.0 - zeta * zeta)
    real, imag = size * jnp.cos(angle), size * jnp.sin(angle)
    lane = lax.broadcasted_iota(jnp.int32, (MODES, NB), 1)
    powers = jnp.zeros((MODES, NB), F32)
    for k in range(8):
        powers = jnp.where(lane == 2 * k, real, jnp.where(lane == 2 * k + 1, imag, powers))
        real, imag = real * real - imag * imag, 2.0 * real * imag
    out_ref[...] = powers


def modal_kernel(pos, in_ref, shapes_ref, flex_ref, powers_ref, out_ref, hold_ref):
    force = in_ref[...].reshape(NT, NB)
    shapes = shapes_ref[...]
    hold_ref[...] = dot_nt(force, flex_ref[...])
    real = dot_nt(shapes, force)
    imag = None
    powers = powers_ref[...]
    lane = lax.broadcasted_iota(jnp.int32, (MODES, NT), 1)
    for k in range(8):
        pr, pi = powers[:, 2 * k : 2 * k + 1], powers[:, 2 * k + 1 : 2 * k + 2]
        keep = lane >= 2**k
        sr = jnp.where(keep, pltpu.roll(real, 2**k, 1), 0.0)
        if imag is None:
            real, imag = real + pr * sr, pi * sr
        else:
            si = jnp.where(keep, pltpu.roll(imag, 2**k, 1), 0.0)
            real, imag = real + (pr * sr - pi * si), imag + (pr * si + pi * sr)
    hold_ref[...] += lax.dot_general(
        imag,
        shapes.astype(F32),
        (((0,), (0,)), ((), ())),
        precision=HI,
        preferred_element_type=F32,
    )
    block = hold_ref[pl.ds(pl.multiple_of(pos[2] * TD, TD), TD), :].astype(BF)
    out_ref[...] = jnp.broadcast_to(block[None], out_ref.shape)


def inverse_kernel(table_ref, in_ref, out_ref):
    acc = [None] * 4
    for z in range(Z):
        block = in_ref[z].astype(F32)
        for s in range(4):
            term = block * table_ref[z * 4 + s]
            acc[s] = term if acc[s] is None else acc[s] + term
    for s in range(4):
        out_ref[s * D : (s + 1) * D] = jnp.broadcast_to(acc[s].astype(BF)[None], (D, TD, NB))


CHUNKS = 4


def stress_kernel(in_ref, map_ref, out_ref, hold_ref, sems):
    total = None
    for q in range(YL * C):
        part = in_ref[q * D : (q + 1) * D].astype(F32)
        total = part if total is None else total + part
    motion = total.reshape(NT, NB).astype(BF)
    step = map_ref.shape[0] // CHUNKS
    copies = []
    for k in range(CHUNKS):
        rows = pl.ds(k * step, step)
        hold_ref[rows] = dot_nt(map_ref[rows], motion).astype(BF)
        copies.append(pltpu.make_async_copy(hold_ref.at[rows], out_ref.at[rows], sems.at[k]))
        copies[-1].start()
    for copy in copies:
        copy.wait()


VMEM = pl.BlockSpec(memory_space=pltpu.VMEM)
SMEM = pl.BlockSpec(memory_space=pltpu.SMEM)
HBM = pl.BlockSpec(memory_space=pl.ANY)


def call(kernel, outs, specs, *args, out_specs=None, scratch=(), dtype=BF):
    outs = [jax.ShapeDtypeStruct(shape, dtype) for shape in outs]
    got = pl.pallas_call(
        kernel,
        out_shape=outs,
        in_specs=specs,
        out_specs=out_specs or [VMEM] * len(outs),
        scratch_shapes=list(scratch),
        compiler_params=pltpu.CompilerParams(vmem_limit_bytes=24 * 1024 * 1024),
    )(*args)
    return got[0] if len(outs) == 1 else got


def local(wake, basis, block_index, phase_index, shapes, flex, omega, zeta, stress_map):
    yl, z, c = lax.axis_index("yl"), lax.axis_index("z"), lax.axis_index("c")
    d = lax.axis_index("x") * 2 + lax.axis_index("yh")
    pos = jnp.stack([yl, c, d]).astype(jnp.int32)
    forward = lax.dynamic_slice(jnp.asarray(FORWARD), (z, 0, 0, 0), (1,) + FORWARD.shape[1:])[0]
    inverse = lax.dynamic_slice(jnp.asarray(INVERSE), ((yl * C + c) * Z + z, 0), (1, 64)).reshape(64)
    powers = call(powers_kernel, [(MODES, NB)], [VMEM] * 2, omega, zeta, dtype=F32)

    spread = call(
        spread_kernel,
        [(YL * Z, PH, HALF)],
        [HBM],
        wake[0],
        out_specs=[HBM],
        scratch=[pltpu.SemaphoreType.DMA((YL * Z,))],
    )
    blocks = lax.all_to_all(spread, ("yl", "z"), 0, 0, tiled=True)

    near, far = call(
        pack_kernel,
        [(NB + 16, HALF)] * 2,
        [SMEM, VMEM, VMEM, VMEM],
        pos,
        basis[0],
        block_index,
        phase_index,
    )
    swap = [(0, 1), (1, 0)]
    by_yl = lax.ppermute(far, "yl", swap)
    by_c = lax.ppermute(near, "c", swap)
    by_both = lax.ppermute(far, ("yl", "c"), [(0, 3), (1, 2), (2, 1), (3, 0)])

    picked = call(
        project_kernel,
        [(PEERS, 4 * TS, NB)],
        [SMEM] + [VMEM] * 5,
        pos,
        blocks,
        near,
        by_yl,
        by_c,
        by_both,
    )
    parts = lax.all_to_all(picked, PLANE, 0, 0, tiled=True)
    forcing = call(gather_sum_kernel, [(Z, 4 * TS, NB)], [VMEM], parts)
    forcing = lax.all_to_all(forcing, "z", 0, 0, tiled=True)
    harmonic = call(forward_kernel, [(PEERS, TS, NB)], [VMEM, VMEM], forward, forcing)
    harmonic = lax.all_to_all(harmonic, PLANE, 0, 0, tiled=True)
    physical = call(
        modal_kernel,
        [(Z, TD, NB)],
        [SMEM] + [VMEM] * 4,
        pos,
        harmonic,
        shapes[0],
        flex[0],
        powers,
        scratch=[pltpu.VMEM((NT, NB), F32)],
    )
    physical = lax.all_to_all(physical, "z", 0, 0, tiled=True)
    sectoral = call(inverse_kernel, [(PEERS, TD, NB)], [SMEM, VMEM], inverse, physical)
    sectoral = lax.all_to_all(sectoral, PLANE, 0, 0, tiled=True)
    rows = stress_map.shape[1]
    stress = call(
        stress_kernel,
        [(rows, NT)],
        [VMEM, VMEM],
        sectoral,
        stress_map[0],
        out_specs=[HBM],
        scratch=[pltpu.VMEM((rows, NT), BF), pltpu.SemaphoreType.DMA((CHUNKS,))],
    )
    return stress[None]


def solution(mesh):
    sector, dof = ("yl", "z", "c"), ("x", "yh")
    return jax.shard_map(
        local,
        mesh=Mesh(mesh.devices.reshape(SIZES), AXES),
        in_specs=(
            P(sector, None, dof),
            P(sector, None, dof),
            P(sector, None),
            P(sector, None),
            P(sector, None, None),
            P(sector, None, None),
            P(sector, None),
            P(sector, None),
            P(sector, dof, None),
        ),
        out_specs=P(sector, dof, None),
        check_vma=False,
    )
```

```python
import numpy as np
import jax
import jax.numpy as jnp
from jax import lax
from jax.experimental import pallas as pl
from jax.experimental.pallas import tpu as pltpu
from jax.sharding import Mesh, PartitionSpec as P

AXES = ("yl", "z", "c", "x", "yh")
SIZES = (2, 16, 2, 4, 2)
PLANE = ("yl", "c", "x", "yh")
YL, Z, C, D = 2, 16, 2, 8
PEERS = YL * C * D
BLADES, PH, NT, NB, MODES = YL * Z * C, 8, 256, 128, 40
HALF = 896
TS = NT // PEERS
TD = NT // D
BF = jnp.bfloat16
F32 = jnp.float32
HI = lax.Precision.HIGHEST


def fourier_table(count):
    h = np.arange(count)[:, None]
    s = np.arange(count)[None, :]
    angle = 2.0 * np.pi * ((((h + 1) // 2) * s) % count) / count
    table = np.where(h % 2 == 1, np.cos(angle), np.sin(angle))
    table = np.where(h == 0, 1.0, table)
    edges = (h == 0) | (h == count - 1)
    return table * np.where(edges, np.sqrt(1.0 / count), np.sqrt(2.0 / count))


FOURIER = fourier_table(BLADES)


def forward_table():
    table = FOURIER.reshape(YL, Z, C, YL, Z, C).transpose(1, 0, 2, 4, 3, 5)
    table = np.einsum("zij,tu->zitju", table.reshape(Z, 4, BLADES), np.eye(TS))
    table = table.reshape(Z, 4 * TS, BLADES * TS).astype(np.float32)
    high = table.astype(BF)
    return np.stack([high, (table - high.astype(np.float32)).astype(BF)], axis=1)


FORWARD = forward_table()
INVERSE = np.ascontiguousarray(
    FOURIER.reshape(YL, Z, C, YL, Z, C).transpose(0, 2, 4, 1, 3, 5).reshape(YL * C * Z, 64)
).astype(np.float32)


def dot_nt(a, b, **kw):
    return lax.dot_general(
        a, b, (((1,), (1,)), ((), ())), preferred_element_type=F32, **kw
    )


def spread_kernel(in_ref, out_ref, sem):
    copies = []
    for half in range(YL):
        part = in_ref.at[:, pl.ds(half * HALF, HALF)]
        for z in range(Z):
            k = half * Z + z
            copies.append(pltpu.make_async_copy(part, out_ref.at[k], sem.at[k]))
            copies[-1].start()
    for copy in copies:
        copy.wait()


def pack_kernel(pos, basis_ref, block_ref, phase_ref, near_ref, far_ref):
    index = jnp.concatenate(
        [block_ref[...].astype(F32), phase_ref[...].astype(F32), jnp.zeros((14, NT), F32)], axis=0
    )
    index = jnp.concatenate([index, jnp.zeros((16, HALF - NT), F32)], axis=1).astype(BF)
    for k, ref in enumerate((near_ref, far_ref)):
        half = (pos[0] + k) & 1
        ref[0:NB] = basis_ref[:, pl.ds(pl.multiple_of(half * HALF, 128), HALF)]
        ref[NB : NB + 16] = index


def project_kernel(pos, wake_ref, *refs):
    out_ref = refs[-1]
    basis = jnp.concatenate([ref[0:NB] for ref in refs[:4]], axis=0)
    table = dot_nt(wake_ref[...].reshape(YL * Z * PH, HALF), basis).astype(BF)
    pair = lax.broadcasted_iota(jnp.int32, (NT, YL * Z * PH), 1).astype(F32)
    codes = []
    for ref in refs[:4]:
        index = ref[NB : NB + 16, 0:NT].astype(F32)
        block, phase = index[0:1].astype(jnp.int32), index[1:2].astype(jnp.int32)
        code = ((block >> 1) * PH + phase).astype(F32)
        codes.append(jnp.where((block & 1) == pos[1], code, -1.0))
    codes = jnp.concatenate(codes + [jnp.zeros((4, NT), F32)], axis=0).T
    picks = []
    for r in range(4):
        onehot = jnp.where(codes[:, r : r + 1] == pair, 1.0, 0.0).astype(BF)
        part = jnp.dot(onehot, table[:, r * NB : (r + 1) * NB], preferred_element_type=F32)
        picks.append(part.reshape(PEERS, TS, NB))
    out_ref[...] = jnp.concatenate(picks, axis=1).astype(BF)


def gather_sum_kernel(in_ref, out_ref):
    sums = {}
    for yl in range(YL):
        for c in range(C):
            total = None
            for d in range(D):
                part = in_ref[(yl * C + c) * D + d].astype(F32)
                total = part if total is None else total + part
            sums[yl, c] = total
    rows = []
    for yl in range(YL):
        for c in range(C):
            total = None
            for y in range(YL):
                for k in range(C):
                    r = (yl ^ y) + 2 * (c ^ k)
                    part = sums[y, k][r * TS : (r + 1) * TS]
                    total = part if total is None else total + part
            rows.append(total)
    block = jnp.concatenate(rows, axis=0).astype(BF)
    out_ref[...] = jnp.broadcast_to(block[None], out_ref.shape)


def forward_kernel(table_ref, in_ref, out_ref):
    block = in_ref[...].reshape(BLADES * TS, NB)
    block = sum(jnp.dot(table_ref[k], block, preferred_element_type=F32) for k in range(2))
    for h in range(4):
        part = block[h * TS : (h + 1) * TS].astype(BF)
        out_ref[h * D : (h + 1) * D] = jnp.broadcast_to(part[None], (D, TS, NB))


def powers_kernel(omega_ref, zeta_ref, out_ref):
    damp = jnp.concatenate([omega_ref[...], zeta_ref[...], jnp.zeros((6, MODES), F32)], axis=0).T
    omega, zeta = damp[:, 0:1], damp[:, 1:2]
    size = jnp.exp(-omega * zeta)
    angle = omega * jnp.sqrt(1.0 - zeta * zeta)
    real, imag = size * jnp.cos(angle), size * jnp.sin(angle)
    lane = lax.broadcasted_iota(jnp.int32, (MODES, NB), 1)
    powers = jnp.zeros((MODES, NB), F32)
    for k in range(8):
        powers = jnp.where(lane == 2 * k, real, jnp.where(lane == 2 * k + 1, imag, powers))
        real, imag = real * real - imag * imag, 2.0 * real * imag
    out_ref[...] = powers


def modal_kernel(pos, in_ref, shapes_ref, flex_ref, powers_ref, out_ref):
    shapes = shapes_ref[...]
    real = dot_nt(shapes, in_ref[...].reshape(NT, NB))
    rows = in_ref[pl.ds(pos[2] * (TD // TS), TD // TS)].reshape(TD, NB)
    direct = dot_nt(rows, flex_ref[...])
    imag = None
    powers = powers_ref[...]
    lane = lax.broadcasted_iota(jnp.int32, (MODES, NT), 1)
    for k in range(8):
        pr, pi = powers[:, 2 * k : 2 * k + 1], powers[:, 2 * k + 1 : 2 * k + 2]
        keep = lane >= 2**k
        sr = jnp.where(keep, pltpu.roll(real, 2**k, 1), 0.0)
        if imag is None:
            real, imag = real + pr * sr, pi * sr
        else:
            si = jnp.where(keep, pltpu.roll(imag, 2**k, 1), 0.0)
            real, imag = real + (pr * sr - pi * si), imag + (pr * si + pi * sr)
    own = pltpu.roll(imag, lax.rem(NT - pos[2] * TD, NT), 1)[:, 0:128]
    high = own.astype(BF).astype(F32)
    amplitude = jnp.concatenate([high, own - high], axis=0).T[0:TD].astype(BF)
    modal = jnp.dot(
        amplitude, jnp.concatenate([shapes, shapes], axis=0), preferred_element_type=F32
    )
    out_ref[...] = jnp.broadcast_to((modal + direct).astype(BF)[None], out_ref.shape)


def inverse_kernel(table_ref, in_ref, out_ref):
    acc = [None] * 4
    for z in range(Z):
        block = in_ref[z].astype(F32)
        for s in range(4):
            term = block * table_ref[z * 4 + s]
            acc[s] = term if acc[s] is None else acc[s] + term
    for s in range(4):
        out_ref[s * D : (s + 1) * D] = jnp.broadcast_to(acc[s].astype(BF)[None], (D, TD, NB))


CHUNKS = 4


def stress_kernel(in_ref, map_ref, out_ref, hold_ref, sems):
    total = None
    for q in range(YL * C):
        part = in_ref[q * D : (q + 1) * D].astype(F32)
        total = part if total is None else total + part
    motion = total.reshape(NT, NB).astype(BF)
    step = map_ref.shape[0] // CHUNKS
    copies = []
    for k in range(CHUNKS):
        rows = pl.ds(k * step, step)
        hold_ref[rows] = dot_nt(map_ref[rows], motion).astype(BF)
        copies.append(pltpu.make_async_copy(hold_ref.at[rows], out_ref.at[rows], sems.at[k]))
        copies[-1].start()
    for copy in copies:
        copy.wait()


VMEM = pl.BlockSpec(memory_space=pltpu.VMEM)
SMEM = pl.BlockSpec(memory_space=pltpu.SMEM)
HBM = pl.BlockSpec(memory_space=pl.ANY)


def call(kernel, outs, specs, *args, out_specs=None, scratch=(), dtype=BF):
    outs = [jax.ShapeDtypeStruct(shape, dtype) for shape in outs]
    got = pl.pallas_call(
        kernel,
        out_shape=outs,
        in_specs=specs,
        out_specs=out_specs or [VMEM] * len(outs),
        scratch_shapes=list(scratch),
        compiler_params=pltpu.CompilerParams(vmem_limit_bytes=24 * 1024 * 1024),
    )(*args)
    return got[0] if len(outs) == 1 else got


def local(wake, basis, block_index, phase_index, shapes, flex, omega, zeta, stress_map):
    yl, z, c = lax.axis_index("yl"), lax.axis_index("z"), lax.axis_index("c")
    d = lax.axis_index("x") * 2 + lax.axis_index("yh")
    pos = jnp.stack([yl, c, d]).astype(jnp.int32)
    forward = lax.dynamic_slice(jnp.asarray(FORWARD), (z, 0, 0, 0), (1,) + FORWARD.shape[1:])[0]
    inverse = lax.dynamic_slice(jnp.asarray(INVERSE), ((yl * C + c) * Z + z, 0), (1, 64)).reshape(64)
    powers = call(powers_kernel, [(MODES, NB)], [VMEM] * 2, omega, zeta, dtype=F32)

    spread = call(
        spread_kernel,
        [(YL * Z, PH, HALF)],
        [pl.BlockSpec(memory_space=pltpu.HBM)],
        wake[0],
        out_specs=[HBM],
        scratch=[pltpu.SemaphoreType.DMA((YL * Z,))],
    )
    blocks = lax.all_to_all(spread, ("yl", "z"), 0, 0, tiled=True)

    near, far = call(
        pack_kernel,
        [(NB + 16, HALF)] * 2,
        [SMEM, VMEM, VMEM, VMEM],
        pos,
        basis[0],
        block_index,
        phase_index,
    )
    swap = [(0, 1), (1, 0)]
    by_yl = lax.ppermute(far, "yl", swap)
    by_c = lax.ppermute(near, "c", swap)
    by_both = lax.ppermute(by_yl, "c", swap)
    near, forward, inverse, powers = lax.optimization_barrier((near, forward, inverse, powers))

    picked = call(
        project_kernel,
        [(PEERS, 4 * TS, NB)],
        [SMEM] + [VMEM] * 5,
        pos,
        blocks,
        near,
        by_yl,
        by_c,
        by_both,
    )
    parts = lax.all_to_all(picked, PLANE, 0, 0, tiled=True)
    forcing = call(gather_sum_kernel, [(Z, 4 * TS, NB)], [VMEM], parts)
    forcing = lax.all_to_all(forcing, "z", 0, 0, tiled=True)
    harmonic = call(forward_kernel, [(PEERS, TS, NB)], [VMEM, VMEM], forward, forcing)
    harmonic = lax.all_to_all(harmonic, PLANE, 0, 0, tiled=True)
    physical = call(
        modal_kernel,
        [(Z, TD, NB)],
        [SMEM] + [VMEM] * 4,
        pos,
        harmonic,
        shapes[0],
        flex[0],
        powers,
    )
    physical = lax.all_to_all(physical, "z", 0, 0, tiled=True)
    sectoral = call(inverse_kernel, [(PEERS, TD, NB)], [SMEM, VMEM], inverse, physical)
    sectoral = lax.all_to_all(sectoral, PLANE, 0, 0, tiled=True)
    rows = stress_map.shape[1]
    stress = call(
        stress_kernel,
        [(rows, NT)],
        [VMEM, VMEM],
        sectoral,
        stress_map[0],
        out_specs=[HBM],
        scratch=[pltpu.VMEM((rows, NT), BF), pltpu.SemaphoreType.DMA((CHUNKS,))],
    )
    return stress[None]


def solution(mesh):
    sector, dof = ("yl", "z", "c"), ("x", "yh")
    return jax.shard_map(
        local,
        mesh=Mesh(mesh.devices.reshape(SIZES), AXES),
        in_specs=(
            P(sector, None, dof),
            P(sector, None, dof),
            P(sector, None),
            P(sector, None),
            P(sector, None, None),
            P(sector, None, None),
            P(sector, None),
            P(sector, None),
            P(sector, dof, None),
        ),
        out_specs=P(sector, dof, None),
        check_vma=False,
    )
```

```python
import numpy as np
import jax
import jax.numpy as jnp
from jax import lax
from jax.experimental import pallas as pl
from jax.experimental.pallas import tpu as pltpu
from jax.sharding import Mesh, PartitionSpec as P

AXES = ("yl", "z", "c", "x", "yh")
SIZES = (2, 16, 2, 4, 2)
PLANE = ("yl", "c", "x", "yh")
YL, Z, C, D = 2, 16, 2, 8
PEERS = YL * C * D
BLADES, PH, NT, NB, MODES = YL * Z * C, 8, 256, 128, 40
HALF = 896
TS = NT // PEERS
TD = NT // D
BF = jnp.bfloat16
F32 = jnp.float32
HI = lax.Precision.HIGHEST


def fourier_table(count):
    h = np.arange(count)[:, None]
    s = np.arange(count)[None, :]
    angle = 2.0 * np.pi * ((((h + 1) // 2) * s) % count) / count
    table = np.where(h % 2 == 1, np.cos(angle), np.sin(angle))
    table = np.where(h == 0, 1.0, table)
    edges = (h == 0) | (h == count - 1)
    return table * np.where(edges, np.sqrt(1.0 / count), np.sqrt(2.0 / count))


FOURIER = fourier_table(BLADES)


def forward_table():
    table = FOURIER.reshape(YL, Z, C, YL, Z, C).transpose(1, 0, 2, 4, 3, 5)
    table = np.einsum("zij,tu->zitju", table.reshape(Z, 4, BLADES), np.eye(TS))
    table = table.reshape(Z, 4 * TS, BLADES * TS).astype(np.float32)
    high = table.astype(BF)
    return np.stack([high, (table - high.astype(np.float32)).astype(BF)], axis=1)


FORWARD = forward_table()


def inverse_table():
    table = FOURIER.reshape(YL, Z, C, YL, Z, C).transpose(0, 2, 4, 3, 5, 1)
    table = np.einsum("dij,tu->ditju", table.reshape(BLADES, 4, Z), np.eye(TS))
    table = table.reshape(BLADES, 4 * TS, Z * TS).astype(np.float32)
    high = table.astype(BF)
    return np.stack([high, (table - high.astype(np.float32)).astype(BF)], axis=1)


INVERSE = inverse_table()


def dot_nt(a, b, **kw):
    return lax.dot_general(
        a, b, (((1,), (1,)), ((), ())), preferred_element_type=F32, **kw
    )


def spread_kernel(in_ref, out_ref, sem):
    copies = []
    for half in range(YL):
        part = in_ref.at[:, pl.ds(half * HALF, HALF)]
        for z in range(Z):
            k = half * Z + z
            copies.append(pltpu.make_async_copy(part, out_ref.at[k], sem.at[k]))
            copies[-1].start()
    for copy in copies:
        copy.wait()


def pack_kernel(pos, basis_ref, block_ref, phase_ref, near_ref, far_ref):
    index = jnp.concatenate(
        [block_ref[...].astype(F32), phase_ref[...].astype(F32), jnp.zeros((14, NT), F32)], axis=0
    )
    index = jnp.concatenate([index, jnp.zeros((16, HALF - NT), F32)], axis=1).astype(BF)
    for k, ref in enumerate((near_ref, far_ref)):
        half = (pos[0] + k) & 1
        ref[0:NB] = basis_ref[:, pl.ds(pl.multiple_of(half * HALF, 128), HALF)]
        ref[NB : NB + 16] = index


def select_kernel(pos, *refs):
    basis_ref, onehot_ref = refs[4:]
    codes = []
    for r, ref in enumerate(refs[:4]):
        basis_ref[r * NB : (r + 1) * NB] = ref[0:NB]
        index = ref[NB : NB + 16, 0:NT].astype(F32)
        block, phase = index[0:1].astype(jnp.int32), index[1:2].astype(jnp.int32)
        code = ((block >> 1) * PH + phase).astype(F32)
        codes.append(jnp.where((block & 1) == pos[1], code, -1.0))
    codes = jnp.concatenate(codes + [jnp.zeros((4, NT), F32)], axis=0).T
    pair = lax.broadcasted_iota(jnp.int32, (NT, YL * Z * PH), 1).astype(F32)
    for r in range(4):
        onehot_ref[r] = jnp.where(codes[:, r : r + 1] == pair, 1.0, 0.0).astype(BF)


def project_kernel(wake_ref, basis_ref, onehot_ref, out_ref):
    table = dot_nt(wake_ref[...].reshape(YL * Z * PH, HALF), basis_ref[...]).astype(BF)
    picks = []
    for r in range(4):
        part = jnp.dot(
            onehot_ref[r], table[:, r * NB : (r + 1) * NB], preferred_element_type=F32
        )
        picks.append(part.reshape(PEERS, TS, NB))
    out_ref[...] = jnp.concatenate(picks, axis=1).astype(BF)


def gather_sum_kernel(in_ref, out_ref):
    sums = {}
    for yl in range(YL):
        for c in range(C):
            total = None
            for d in range(D):
                part = in_ref[(yl * C + c) * D + d].astype(F32)
                total = part if total is None else total + part
            sums[yl, c] = total
    rows = []
    for yl in range(YL):
        for c in range(C):
            total = None
            for y in range(YL):
                for k in range(C):
                    r = (yl ^ y) + 2 * (c ^ k)
                    part = sums[y, k][r * TS : (r + 1) * TS]
                    total = part if total is None else total + part
            rows.append(total)
    block = jnp.concatenate(rows, axis=0).astype(BF)
    out_ref[...] = jnp.broadcast_to(block[None], out_ref.shape)


def forward_kernel(table_ref, in_ref, out_ref):
    block = in_ref[...].reshape(BLADES * TS, NB)
    block = sum(jnp.dot(table_ref[k], block, preferred_element_type=F32) for k in range(2))
    for h in range(4):
        part = block[h * TS : (h + 1) * TS].astype(BF)
        out_ref[h * D : (h + 1) * D] = jnp.broadcast_to(part[None], (D, TS, NB))


def powers_kernel(omega_ref, zeta_ref, out_ref):
    damp = jnp.concatenate([omega_ref[...], zeta_ref[...], jnp.zeros((6, MODES), F32)], axis=0).T
    omega, zeta = damp[:, 0:1], damp[:, 1:2]
    size = jnp.exp(-omega * zeta)
    angle = omega * jnp.sqrt(1.0 - zeta * zeta)
    real, imag = size * jnp.cos(angle), size * jnp.sin(angle)
    lane = lax.broadcasted_iota(jnp.int32, (MODES, NB), 1)
    powers = jnp.zeros((MODES, NB), F32)
    for k in range(8):
        powers = jnp.where(lane == 2 * k, real, jnp.where(lane == 2 * k + 1, imag, powers))
        real, imag = real * real - imag * imag, 2.0 * real * imag
    out_ref[...] = powers


def modal_kernel(pos, in_ref, shapes_ref, flex_ref, powers_ref, out_ref):
    shapes = shapes_ref[...]
    real = dot_nt(shapes, in_ref[...].reshape(NT, NB))
    rows = in_ref[pl.ds(pos[2] * (TD // TS), TD // TS)].reshape(TD, NB)
    direct = dot_nt(rows, flex_ref[...])
    imag = None
    powers = powers_ref[...]
    lane = lax.broadcasted_iota(jnp.int32, (MODES, NT), 1)
    for k in range(8):
        pr, pi = powers[:, 2 * k : 2 * k + 1], powers[:, 2 * k + 1 : 2 * k + 2]
        keep = lane >= 2**k
        sr = jnp.where(keep, pltpu.roll(real, 2**k, 1), 0.0)
        if imag is None:
            real, imag = real + pr * sr, pi * sr
        else:
            si = jnp.where(keep, pltpu.roll(imag, 2**k, 1), 0.0)
            real, imag = real + (pr * sr - pi * si), imag + (pr * si + pi * sr)
    own = pltpu.roll(imag, lax.rem(NT - pos[2] * TD, NT), 1)[:, 0:128]
    high = own.astype(BF).astype(F32)
    amplitude = jnp.concatenate([high, own - high], axis=0).T[0:TD].astype(BF)
    modal = jnp.dot(
        amplitude, jnp.concatenate([shapes, shapes], axis=0), preferred_element_type=F32
    )
    out_ref[...] = jnp.broadcast_to((modal + direct).astype(BF)[None], out_ref.shape)


def inverse_kernel(table_ref, in_ref, out_ref):
    block = in_ref[...].astype(F32)
    parts = []
    for g in range(TD // TS):
        part = block[:, g * TS : (g + 1) * TS].reshape(Z * TS, NB).astype(BF)
        parts.append(
            sum(jnp.dot(table_ref[k], part, preferred_element_type=F32) for k in range(2))
        )
    for s in range(4):
        part = jnp.concatenate([p[s * TS : (s + 1) * TS] for p in parts], axis=0).astype(BF)
        out_ref[s * D : (s + 1) * D] = jnp.broadcast_to(part[None], (D, TD, NB))


CHUNKS = 4


def stress_kernel(in_ref, map_ref, out_ref, hold_ref, sems):
    total = None
    for q in range(YL * C):
        part = in_ref[q * D : (q + 1) * D].astype(F32)
        total = part if total is None else total + part
    motion = total.reshape(NT, NB).astype(BF)
    step = map_ref.shape[0] // CHUNKS
    copies = []
    for k in range(CHUNKS):
        rows = pl.ds(k * step, step)
        hold_ref[rows] = dot_nt(map_ref[rows], motion).astype(BF)
        copies.append(pltpu.make_async_copy(hold_ref.at[rows], out_ref.at[rows], sems.at[k]))
        copies[-1].start()
    for copy in copies:
        copy.wait()


VMEM = pl.BlockSpec(memory_space=pltpu.VMEM)
SMEM = pl.BlockSpec(memory_space=pltpu.SMEM)
HBM = pl.BlockSpec(memory_space=pl.ANY)


def call(kernel, outs, specs, *args, out_specs=None, scratch=(), dtype=BF, vmem=24):
    outs = [jax.ShapeDtypeStruct(shape, dtype) for shape in outs]
    got = pl.pallas_call(
        kernel,
        out_shape=outs,
        in_specs=specs,
        out_specs=out_specs or [VMEM] * len(outs),
        scratch_shapes=list(scratch),
        compiler_params=pltpu.CompilerParams(vmem_limit_bytes=vmem * 1024 * 1024),
    )(*args)
    return got[0] if len(outs) == 1 else got


def local(wake, basis, block_index, phase_index, shapes, flex, omega, zeta, stress_map):
    yl, z, c = lax.axis_index("yl"), lax.axis_index("z"), lax.axis_index("c")
    d = lax.axis_index("x") * 2 + lax.axis_index("yh")
    pos = jnp.stack([yl, c, d]).astype(jnp.int32)
    forward = lax.dynamic_slice(jnp.asarray(FORWARD), (z, 0, 0, 0), (1,) + FORWARD.shape[1:])[0]
    inverse = lax.dynamic_slice(
        jnp.asarray(INVERSE), ((yl * C + c) * Z + z, 0, 0, 0), (1,) + INVERSE.shape[1:]
    )[0]
    powers = call(powers_kernel, [(MODES, NB)], [VMEM] * 2, omega, zeta, dtype=F32)

    spread = call(
        spread_kernel,
        [(YL * Z, PH, HALF)],
        [HBM],
        wake[0],
        out_specs=[HBM],
        vmem=60,
        scratch=[pltpu.SemaphoreType.DMA((YL * Z,))],
    )
    blocks = lax.all_to_all(spread, ("yl", "z"), 0, 0, tiled=True)

    near, far = call(
        pack_kernel,
        [(NB + 16, HALF)] * 2,
        [SMEM, VMEM, VMEM, VMEM],
        pos,
        basis[0],
        block_index,
        phase_index,
    )
    swap = [(0, 1), (1, 0)]
    by_yl = lax.ppermute(far, "yl", swap)
    by_c = lax.ppermute(near, "c", swap)
    by_both = lax.ppermute(by_yl, "c", swap)
    near, forward, inverse, powers = lax.optimization_barrier((near, forward, inverse, powers))

    joined, onehot = call(
        select_kernel,
        [(4 * NB, HALF), (4, NT, YL * Z * PH)],
        [SMEM] + [VMEM] * 4,
        pos,
        near,
        by_yl,
        by_c,
        by_both,
    )
    picked = call(project_kernel, [(PEERS, 4 * TS, NB)], [VMEM] * 3, blocks, joined, onehot)
    parts = lax.all_to_all(picked, PLANE, 0, 0, tiled=True)
    forcing = call(gather_sum_kernel, [(Z, 4 * TS, NB)], [VMEM], parts)
    forcing = lax.all_to_all(forcing, "z", 0, 0, tiled=True)
    harmonic = call(forward_kernel, [(PEERS, TS, NB)], [VMEM, VMEM], forward, forcing)
    harmonic = lax.all_to_all(harmonic, PLANE, 0, 0, tiled=True)
    physical = call(
        modal_kernel,
        [(Z, TD, NB)],
        [SMEM] + [VMEM] * 4,
        pos,
        harmonic,
        shapes[0],
        flex[0],
        powers,
    )
    physical = lax.all_to_all(physical, "z", 0, 0, tiled=True)
    sectoral = call(inverse_kernel, [(PEERS, TD, NB)], [VMEM] * 2, inverse, physical)
    sectoral = lax.all_to_all(sectoral, PLANE, 0, 0, tiled=True)
    rows = stress_map.shape[1]
    stress = call(
        stress_kernel,
        [(rows, NT)],
        [VMEM, VMEM],
        sectoral,
        stress_map[0],
        out_specs=[HBM],
        scratch=[pltpu.VMEM((rows, NT), BF), pltpu.SemaphoreType.DMA((CHUNKS,))],
    )
    return stress[None]


def solution(mesh):
    sector, dof = ("yl", "z", "c"), ("x", "yh")
    return jax.shard_map(
        local,
        mesh=Mesh(mesh.devices.reshape(SIZES), AXES),
        in_specs=(
            P(sector, None, dof),
            P(sector, None, dof),
            P(sector, None),
            P(sector, None),
            P(sector, None, None),
            P(sector, None, None),
            P(sector, None),
            P(sector, None),
            P(sector, dof, None),
        ),
        out_specs=P(sector, dof, None),
        check_vma=False,
    )
```

```python
import numpy as np
import jax
import jax.numpy as jnp
from jax import lax
from jax.experimental import pallas as pl
from jax.experimental.pallas import tpu as pltpu
from jax.sharding import Mesh, PartitionSpec as P

AXES = ("yl", "z", "c", "x", "yh")
SIZES = (2, 16, 2, 4, 2)
PLANE = ("yl", "c", "x", "yh")
YL, Z, C, D = 2, 16, 2, 8
PEERS = YL * C * D
BLADES, PH, NT, NB, MODES = YL * Z * C, 8, 256, 128, 40
HALF = 896
TS = NT // PEERS
TD = NT // D
BF = jnp.bfloat16
F32 = jnp.float32
HI = lax.Precision.HIGHEST


def fourier_table(count):
    h = np.arange(count)[:, None]
    s = np.arange(count)[None, :]
    angle = 2.0 * np.pi * ((((h + 1) // 2) * s) % count) / count
    table = np.where(h % 2 == 1, np.cos(angle), np.sin(angle))
    table = np.where(h == 0, 1.0, table)
    edges = (h == 0) | (h == count - 1)
    return table * np.where(edges, np.sqrt(1.0 / count), np.sqrt(2.0 / count))


FOURIER = fourier_table(BLADES)


def forward_table():
    table = FOURIER.reshape(YL, Z, C, YL, Z, C).transpose(1, 0, 2, 4, 3, 5)
    table = np.einsum("zij,tu->zitju", table.reshape(Z, 4, BLADES), np.eye(TS))
    table = table.reshape(Z, 4 * TS, BLADES * TS).astype(np.float32)
    high = table.astype(BF)
    return np.stack([high, (table - high.astype(np.float32)).astype(BF)], axis=1)


FORWARD = forward_table()


def inverse_table():
    table = FOURIER.reshape(YL, Z, C, YL, Z, C).transpose(0, 2, 4, 3, 5, 1)
    table = np.einsum("dij,tu->ditju", table.reshape(BLADES, 4, Z), np.eye(TS))
    table = table.reshape(BLADES, 4 * TS, Z * TS).astype(np.float32)
    high = table.astype(BF)
    return np.stack([high, (table - high.astype(np.float32)).astype(BF)], axis=1)


INVERSE = inverse_table()


def dot_nt(a, b, **kw):
    return lax.dot_general(
        a, b, (((1,), (1,)), ((), ())), preferred_element_type=F32, **kw
    )


def spread_kernel(in_ref, out_ref, wake_ref, hold_ref, sems):
    copy = pltpu.make_async_copy(in_ref, wake_ref, sems.at[YL])
    copy.start()
    copy.wait()
    copies = []
    for half in range(YL):
        rows = pl.ds(half * Z, Z)
        part = wake_ref[:, half * HALF : (half + 1) * HALF]
        hold_ref[rows] = jnp.broadcast_to(part[None], (Z, PH, HALF))
        copies.append(pltpu.make_async_copy(hold_ref.at[rows], out_ref.at[rows], sems.at[half]))
        copies[-1].start()
    for copy in copies:
        copy.wait()


def pack_kernel(pos, basis_ref, block_ref, phase_ref, near_ref, far_ref):
    index = jnp.concatenate(
        [block_ref[...].astype(F32), phase_ref[...].astype(F32), jnp.zeros((14, NT), F32)], axis=0
    )
    index = jnp.concatenate([index, jnp.zeros((16, HALF - NT), F32)], axis=1).astype(BF)
    for k, ref in enumerate((near_ref, far_ref)):
        half = (pos[0] + k) & 1
        ref[0:NB] = basis_ref[:, pl.ds(pl.multiple_of(half * HALF, 128), HALF)]
        ref[NB : NB + 16] = index


def select_kernel(pos, *refs):
    basis_ref, onehot_ref = refs[4:]
    codes = []
    for r, ref in enumerate(refs[:4]):
        basis_ref[r * NB : (r + 1) * NB] = ref[0:NB]
        index = ref[NB : NB + 16, 0:NT].astype(F32)
        block, phase = index[0:1].astype(jnp.int32), index[1:2].astype(jnp.int32)
        code = ((block >> 1) * PH + phase).astype(F32)
        codes.append(jnp.where((block & 1) == pos[1], code, -1.0))
    codes = jnp.concatenate(codes + [jnp.zeros((4, NT), F32)], axis=0).T
    pair = lax.broadcasted_iota(jnp.int32, (NT, YL * Z * PH), 1).astype(F32)
    for r in range(4):
        onehot_ref[r] = jnp.where(codes[:, r : r + 1] == pair, 1.0, 0.0).astype(BF)


def project_kernel(wake_ref, basis_ref, onehot_ref, out_ref):
    table = dot_nt(wake_ref[...].reshape(YL * Z * PH, HALF), basis_ref[...]).astype(BF)
    picks = []
    for r in range(4):
        part = jnp.dot(
            onehot_ref[r], table[:, r * NB : (r + 1) * NB], preferred_element_type=F32
        )
        picks.append(part.reshape(PEERS, TS, NB))
    out_ref[...] = jnp.concatenate(picks, axis=1).astype(BF)


def gather_sum_kernel(in_ref, out_ref):
    sums = {}
    for yl in range(YL):
        for c in range(C):
            total = None
            for d in range(D):
                part = in_ref[(yl * C + c) * D + d].astype(F32)
                total = part if total is None else total + part
            sums[yl, c] = total
    rows = []
    for yl in range(YL):
        for c in range(C):
            total = None
            for y in range(YL):
                for k in range(C):
                    r = (yl ^ y) + 2 * (c ^ k)
                    part = sums[y, k][r * TS : (r + 1) * TS]
                    total = part if total is None else total + part
            rows.append(total)
    block = jnp.concatenate(rows, axis=0).astype(BF)
    out_ref[...] = jnp.broadcast_to(block[None], out_ref.shape)


def forward_kernel(table_ref, in_ref, out_ref):
    block = in_ref[...].reshape(BLADES * TS, NB)
    block = sum(jnp.dot(table_ref[k], block, preferred_element_type=F32) for k in range(2))
    for h in range(4):
        part = block[h * TS : (h + 1) * TS].astype(BF)
        out_ref[h * D : (h + 1) * D] = jnp.broadcast_to(part[None], (D, TS, NB))


def powers_kernel(omega_ref, zeta_ref, out_ref):
    damp = jnp.concatenate([omega_ref[...], zeta_ref[...], jnp.zeros((6, MODES), F32)], axis=0).T
    omega, zeta = damp[:, 0:1], damp[:, 1:2]
    size = jnp.exp(-omega * zeta)
    angle = omega * jnp.sqrt(1.0 - zeta * zeta)
    real, imag = size * jnp.cos(angle), size * jnp.sin(angle)
    lane = lax.broadcasted_iota(jnp.int32, (MODES, NB), 1)
    powers = jnp.zeros((MODES, NB), F32)
    for k in range(8):
        powers = jnp.where(lane == 2 * k, real, jnp.where(lane == 2 * k + 1, imag, powers))
        real, imag = real * real - imag * imag, 2.0 * real * imag
    out_ref[...] = powers


def modal_kernel(pos, in_ref, shapes_ref, flex_ref, powers_ref, out_ref):
    shapes = shapes_ref[...]
    real = dot_nt(shapes, in_ref[...].reshape(NT, NB))
    rows = in_ref[pl.ds(pos[2] * (TD // TS), TD // TS)].reshape(TD, NB)
    direct = dot_nt(rows, flex_ref[...])
    imag = None
    powers = powers_ref[...]
    lane = lax.broadcasted_iota(jnp.int32, (MODES, NT), 1)
    for k in range(8):
        pr, pi = powers[:, 2 * k : 2 * k + 1], powers[:, 2 * k + 1 : 2 * k + 2]
        keep = lane >= 2**k
        sr = jnp.where(keep, pltpu.roll(real, 2**k, 1), 0.0)
        if imag is None:
            real, imag = real + pr * sr, pi * sr
        else:
            si = jnp.where(keep, pltpu.roll(imag, 2**k, 1), 0.0)
            real, imag = real + (pr * sr - pi * si), imag + (pr * si + pi * sr)
    own = pltpu.roll(imag, lax.rem(NT - pos[2] * TD, NT), 1)[:, 0:128]
    high = own.astype(BF).astype(F32)
    amplitude = jnp.concatenate([high, own - high], axis=0).T[0:TD].astype(BF)
    modal = jnp.dot(
        amplitude, jnp.concatenate([shapes, shapes], axis=0), preferred_element_type=F32
    )
    out_ref[...] = jnp.broadcast_to((modal + direct).astype(BF)[None], out_ref.shape)


def inverse_kernel(table_ref, in_ref, out_ref):
    block = in_ref[...].astype(F32)
    parts = []
    for g in range(TD // TS):
        part = block[:, g * TS : (g + 1) * TS].reshape(Z * TS, NB).astype(BF)
        parts.append(
            sum(jnp.dot(table_ref[k], part, preferred_element_type=F32) for k in range(2))
        )
    for s in range(4):
        part = jnp.concatenate([p[s * TS : (s + 1) * TS] for p in parts], axis=0).astype(BF)
        out_ref[s * D : (s + 1) * D] = jnp.broadcast_to(part[None], (D, TD, NB))


CHUNKS = 4


def stress_kernel(in_ref, map_ref, out_ref, hold_ref, sems):
    total = None
    for q in range(YL * C):
        part = in_ref[q * D : (q + 1) * D].astype(F32)
        total = part if total is None else total + part
    motion = total.reshape(NT, NB).astype(BF)
    step = map_ref.shape[0] // CHUNKS
    copies = []
    for k in range(CHUNKS):
        rows = pl.ds(k * step, step)
        hold_ref[rows] = dot_nt(map_ref[rows], motion).astype(BF)
        copies.append(pltpu.make_async_copy(hold_ref.at[rows], out_ref.at[rows], sems.at[k]))
        copies[-1].start()
    for copy in copies:
        copy.wait()


VMEM = pl.BlockSpec(memory_space=pltpu.VMEM)
SMEM = pl.BlockSpec(memory_space=pltpu.SMEM)
HBM = pl.BlockSpec(memory_space=pl.ANY)


def call(kernel, outs, specs, *args, out_specs=None, scratch=(), dtype=BF, vmem=24):
    outs = [jax.ShapeDtypeStruct(shape, dtype) for shape in outs]
    got = pl.pallas_call(
        kernel,
        out_shape=outs,
        in_specs=specs,
        out_specs=out_specs or [VMEM] * len(outs),
        scratch_shapes=list(scratch),
        compiler_params=pltpu.CompilerParams(vmem_limit_bytes=vmem * 1024 * 1024),
    )(*args)
    return got[0] if len(outs) == 1 else got


def local(wake, basis, block_index, phase_index, shapes, flex, omega, zeta, stress_map):
    yl, z, c = lax.axis_index("yl"), lax.axis_index("z"), lax.axis_index("c")
    d = lax.axis_index("x") * 2 + lax.axis_index("yh")
    pos = jnp.stack([yl, c, d]).astype(jnp.int32)
    forward = lax.dynamic_slice(jnp.asarray(FORWARD), (z, 0, 0, 0), (1,) + FORWARD.shape[1:])[0]
    inverse = lax.dynamic_slice(
        jnp.asarray(INVERSE), ((yl * C + c) * Z + z, 0, 0, 0), (1,) + INVERSE.shape[1:]
    )[0]
    powers = call(powers_kernel, [(MODES, NB)], [VMEM] * 2, omega, zeta, dtype=F32)

    spread = call(
        spread_kernel,
        [(YL * Z, PH, HALF)],
        [HBM],
        wake[0],
        out_specs=[HBM],
        vmem=60,
        scratch=[
            pltpu.VMEM((PH, YL * HALF), BF),
            pltpu.VMEM((YL * Z, PH, HALF), BF),
            pltpu.SemaphoreType.DMA((YL + 1,)),
        ],
    )
    blocks = lax.all_to_all(spread, ("yl", "z"), 0, 0, tiled=True)

    near, far = call(
        pack_kernel,
        [(NB + 16, HALF)] * 2,
        [SMEM, VMEM, VMEM, VMEM],
        pos,
        basis[0],
        block_index,
        phase_index,
    )
    swap = [(0, 1), (1, 0)]
    by_yl = lax.ppermute(far, "yl", swap)
    by_c = lax.ppermute(near, "c", swap)
    by_both = lax.ppermute(by_yl, "c", swap)
    near, forward, inverse, powers = lax.optimization_barrier((near, forward, inverse, powers))

    joined, onehot = call(
        select_kernel,
        [(4 * NB, HALF), (4, NT, YL * Z * PH)],
        [SMEM] + [VMEM] * 4,
        pos,
        near,
        by_yl,
        by_c,
        by_both,
    )
    picked = call(project_kernel, [(PEERS, 4 * TS, NB)], [VMEM] * 3, blocks, joined, onehot)
    parts = lax.all_to_all(picked, PLANE, 0, 0, tiled=True)
    forcing = call(gather_sum_kernel, [(Z, 4 * TS, NB)], [VMEM], parts)
    forcing = lax.all_to_all(forcing, "z", 0, 0, tiled=True)
    harmonic = call(forward_kernel, [(PEERS, TS, NB)], [VMEM, VMEM], forward, forcing)
    harmonic = lax.all_to_all(harmonic, PLANE, 0, 0, tiled=True)
    physical = call(
        modal_kernel,
        [(Z, TD, NB)],
        [SMEM] + [VMEM] * 4,
        pos,
        harmonic,
        shapes[0],
        flex[0],
        powers,
    )
    physical = lax.all_to_all(physical, "z", 0, 0, tiled=True)
    sectoral = call(inverse_kernel, [(PEERS, TD, NB)], [VMEM] * 2, inverse, physical)
    sectoral = lax.all_to_all(sectoral, PLANE, 0, 0, tiled=True)
    rows = stress_map.shape[1]
    stress = call(
        stress_kernel,
        [(rows, NT)],
        [VMEM, VMEM],
        sectoral,
        stress_map[0],
        out_specs=[HBM],
        scratch=[pltpu.VMEM((rows, NT), BF), pltpu.SemaphoreType.DMA((CHUNKS,))],
    )
    return stress[None]


def solution(mesh):
    sector, dof = ("yl", "z", "c"), ("x", "yh")
    return jax.shard_map(
        local,
        mesh=Mesh(mesh.devices.reshape(SIZES), AXES),
        in_specs=(
            P(sector, None, dof),
            P(sector, None, dof),
            P(sector, None),
            P(sector, None),
            P(sector, None, None),
            P(sector, None, None),
            P(sector, None),
            P(sector, None),
            P(sector, dof, None),
        ),
        out_specs=P(sector, dof, None),
        check_vma=False,
    )
```

```python
import numpy as np
import jax
import jax.numpy as jnp
from jax import lax
from jax.experimental import pallas as pl
from jax.experimental.pallas import tpu as pltpu
from jax.sharding import Mesh, PartitionSpec as P

AXES = ("yl", "z", "c", "x", "yh")
SIZES = (2, 16, 2, 4, 2)
PLANE = ("yl", "c", "x", "yh")
YL, Z, C, D = 2, 16, 2, 8
PEERS = YL * C * D
BLADES, PH, NT, NB, MODES = YL * Z * C, 8, 256, 128, 40
HALF = 896
TS = NT // PEERS
TD = NT // D
BF = jnp.bfloat16
F32 = jnp.float32
HI = lax.Precision.HIGHEST


def fourier_table(count):
    h = np.arange(count)[:, None]
    s = np.arange(count)[None, :]
    angle = 2.0 * np.pi * ((((h + 1) // 2) * s) % count) / count
    table = np.where(h % 2 == 1, np.cos(angle), np.sin(angle))
    table = np.where(h == 0, 1.0, table)
    edges = (h == 0) | (h == count - 1)
    return table * np.where(edges, np.sqrt(1.0 / count), np.sqrt(2.0 / count))


FOURIER = fourier_table(BLADES)


def forward_table():
    table = FOURIER.reshape(YL, Z, C, YL, Z, C).transpose(1, 0, 2, 4, 3, 5)
    table = np.einsum("zij,tu->zitju", table.reshape(Z, 4, BLADES), np.eye(TS))
    table = table.reshape(Z, 4 * TS, BLADES * TS).astype(np.float32)
    high = table.astype(BF)
    return np.stack([high, (table - high.astype(np.float32)).astype(BF)], axis=1)


FORWARD = forward_table()


def inverse_table():
    table = FOURIER.reshape(YL, Z, C, YL, Z, C).transpose(0, 2, 4, 3, 5, 1)
    table = np.einsum("dij,tu->ditju", table.reshape(BLADES, 4, Z), np.eye(TS))
    table = table.reshape(BLADES, 4 * TS, Z * TS).astype(np.float32)
    high = table.astype(BF)
    return np.stack([high, (table - high.astype(np.float32)).astype(BF)], axis=1)


INVERSE = inverse_table()


def dot_nt(a, b, **kw):
    return lax.dot_general(
        a, b, (((1,), (1,)), ((), ())), preferred_element_type=F32, **kw
    )


def spread_kernel(in_ref, out_ref, wake_ref, hold_ref, sems):
    copy = pltpu.make_async_copy(in_ref, wake_ref, sems.at[YL])
    copy.start()
    copy.wait()
    copies = []
    for half in range(YL):
        rows = pl.ds(half * Z, Z)
        part = wake_ref[:, half * HALF : (half + 1) * HALF]
        hold_ref[rows] = jnp.broadcast_to(part[None], (Z, PH, HALF))
        copies.append(pltpu.make_async_copy(hold_ref.at[rows], out_ref.at[rows], sems.at[half]))
        copies[-1].start()
    for copy in copies:
        copy.wait()


def pack_kernel(pos, basis_ref, block_ref, phase_ref, near_ref, far_ref):
    index = jnp.concatenate(
        [block_ref[...].astype(F32), phase_ref[...].astype(F32), jnp.zeros((14, NT), F32)], axis=0
    )
    index = jnp.concatenate([index, jnp.zeros((16, HALF - NT), F32)], axis=1).astype(BF)
    for k, ref in enumerate((near_ref, far_ref)):
        half = (pos[0] + k) & 1
        ref[0:NB] = basis_ref[:, pl.ds(pl.multiple_of(half * HALF, 128), HALF)]
        ref[NB : NB + 16] = index


def select_kernel(pos, *refs):
    basis_ref, onehot_ref = refs[4:]
    codes = []
    for r, ref in enumerate(refs[:4]):
        basis_ref[r * NB : (r + 1) * NB] = ref[0:NB]
        index = ref[NB : NB + 16, 0:NT].astype(F32)
        block, phase = index[0:1].astype(jnp.int32), index[1:2].astype(jnp.int32)
        code = ((block >> 1) * PH + phase).astype(F32)
        codes.append(jnp.where((block & 1) == pos[1], code, -1.0))
    codes = jnp.concatenate(codes + [jnp.zeros((4, NT), F32)], axis=0).T
    pair = lax.broadcasted_iota(jnp.int32, (NT, YL * Z * PH), 1).astype(F32)
    for r in range(4):
        onehot_ref[r] = jnp.where(codes[:, r : r + 1] == pair, 1.0, 0.0).astype(BF)


def project_kernel(wake_ref, basis_ref, onehot_ref, out_ref):
    table = dot_nt(wake_ref[...].reshape(YL * Z * PH, HALF), basis_ref[...]).astype(BF)
    picks = []
    for r in range(4):
        part = jnp.dot(
            onehot_ref[r], table[:, r * NB : (r + 1) * NB], preferred_element_type=F32
        )
        picks.append(part.reshape(PEERS, TS, NB))
    out_ref[...] = jnp.concatenate(picks, axis=1).astype(BF)


def gather_sum_kernel(in_ref, out_ref):
    sums = {}
    for yl in range(YL):
        for c in range(C):
            total = None
            for d in range(D):
                part = in_ref[(yl * C + c) * D + d].astype(F32)
                total = part if total is None else total + part
            sums[yl, c] = total
    rows = []
    for yl in range(YL):
        for c in range(C):
            total = None
            for y in range(YL):
                for k in range(C):
                    r = (yl ^ y) + 2 * (c ^ k)
                    part = sums[y, k][r * TS : (r + 1) * TS]
                    total = part if total is None else total + part
            rows.append(total)
    block = jnp.concatenate(rows, axis=0).astype(BF)
    out_ref[...] = jnp.broadcast_to(block[None], out_ref.shape)


def forward_kernel(table_ref, in_ref, out_ref):
    block = in_ref[...].reshape(BLADES * TS, NB)
    block = sum(jnp.dot(table_ref[k], block, preferred_element_type=F32) for k in range(2))
    for h in range(4):
        part = block[h * TS : (h + 1) * TS].astype(BF)
        out_ref[h * D : (h + 1) * D] = jnp.broadcast_to(part[None], (D, TS, NB))


def powers_kernel(omega_ref, zeta_ref, out_ref):
    omega, zeta = omega_ref[...], zeta_ref[...]
    size = jnp.exp(-omega * zeta)
    angle = omega * jnp.sqrt(1.0 - zeta * zeta)
    real, imag = size * jnp.cos(angle), size * jnp.sin(angle)
    out_ref[...] = jnp.zeros_like(out_ref)
    for k in range(8):
        out_ref[2 * k : 2 * k + 1, 0:MODES] = real
        out_ref[2 * k + 1 : 2 * k + 2, 0:MODES] = imag
        real, imag = real * real - imag * imag, 2.0 * real * imag


def modal_kernel(pos, in_ref, shapes_ref, flex_ref, powers_ref, out_ref, hold_ref):
    shapes = jnp.concatenate(
        [shapes_ref[...].astype(F32), jnp.zeros((NB - MODES, NB), F32)], axis=0
    ).astype(BF)
    real = dot_nt(in_ref[...].reshape(NT, NB), shapes)
    imag = jnp.zeros_like(real)
    row = lax.broadcasted_iota(jnp.int32, (NT, NB), 0)
    for k in range(8):
        s = 2**k
        pr, pi = powers_ref[2 * k : 2 * k + 1, :], powers_ref[2 * k + 1 : 2 * k + 2, :]
        if s < 8:
            sr = jnp.where(row >= s, pltpu.roll(real, s, 0), 0.0)
            if k == 0:
                real, imag = real + pr * sr, pi * sr
            else:
                si = jnp.where(row >= s, pltpu.roll(imag, s, 0), 0.0)
                real, imag = real + (pr * sr - pi * si), imag + (pr * si + pi * sr)
        else:
            sr, si = real[: NT - s], imag[: NT - s]
            real = jnp.concatenate([real[:s], real[s:] + (pr * sr - pi * si)], axis=0)
            imag = jnp.concatenate([imag[:s], imag[s:] + (pr * si + pi * sr)], axis=0)
    hold_ref[...] = imag
    own = hold_ref[pl.ds(pl.multiple_of(pos[2] * TD, TD), TD), :]
    high = own.astype(BF)
    low = (own - high.astype(F32)).astype(BF)
    rows = in_ref[pl.ds(pos[2] * (TD // TS), TD // TS)].reshape(TD, NB)
    total = (
        jnp.dot(high, shapes, preferred_element_type=F32)
        + jnp.dot(low, shapes, preferred_element_type=F32)
        + dot_nt(rows, flex_ref[...])
    )
    out_ref[...] = jnp.broadcast_to(total.astype(BF)[None], out_ref.shape)


def inverse_kernel(table_ref, in_ref, out_ref):
    block = in_ref[...].astype(F32)
    parts = []
    for g in range(TD // TS):
        part = block[:, g * TS : (g + 1) * TS].reshape(Z * TS, NB).astype(BF)
        parts.append(
            sum(jnp.dot(table_ref[k], part, preferred_element_type=F32) for k in range(2))
        )
    for s in range(4):
        part = jnp.concatenate([p[s * TS : (s + 1) * TS] for p in parts], axis=0).astype(BF)
        out_ref[s * D : (s + 1) * D] = jnp.broadcast_to(part[None], (D, TD, NB))


CHUNKS = 8


def stress_kernel(in_ref, map_ref, out_ref, hold_ref, sems):
    total = None
    for q in range(YL * C):
        part = in_ref[q * D : (q + 1) * D].astype(F32)
        total = part if total is None else total + part
    motion = total.reshape(NT, NB).astype(BF)
    step = map_ref.shape[0] // CHUNKS
    copies = []
    for k in range(CHUNKS):
        rows = pl.ds(k * step, step)
        hold_ref[rows] = dot_nt(map_ref[rows], motion).astype(BF)
        copies.append(pltpu.make_async_copy(hold_ref.at[rows], out_ref.at[rows], sems.at[k]))
        copies[-1].start()
    for copy in copies:
        copy.wait()


VMEM = pl.BlockSpec(memory_space=pltpu.VMEM)
SMEM = pl.BlockSpec(memory_space=pltpu.SMEM)
HBM = pl.BlockSpec(memory_space=pl.ANY)


def call(kernel, outs, specs, *args, out_specs=None, scratch=(), dtype=BF, vmem=24):
    outs = [jax.ShapeDtypeStruct(shape, dtype) for shape in outs]
    got = pl.pallas_call(
        kernel,
        out_shape=outs,
        in_specs=specs,
        out_specs=out_specs or [VMEM] * len(outs),
        scratch_shapes=list(scratch),
        compiler_params=pltpu.CompilerParams(vmem_limit_bytes=vmem * 1024 * 1024),
    )(*args)
    return got[0] if len(outs) == 1 else got


def local(wake, basis, block_index, phase_index, shapes, flex, omega, zeta, stress_map):
    yl, z, c = lax.axis_index("yl"), lax.axis_index("z"), lax.axis_index("c")
    d = lax.axis_index("x") * 2 + lax.axis_index("yh")
    pos = jnp.stack([yl, c, d]).astype(jnp.int32)
    forward = lax.dynamic_slice(jnp.asarray(FORWARD), (z, 0, 0, 0), (1,) + FORWARD.shape[1:])[0]
    inverse = lax.dynamic_slice(
        jnp.asarray(INVERSE), ((yl * C + c) * Z + z, 0, 0, 0), (1,) + INVERSE.shape[1:]
    )[0]
    powers = call(powers_kernel, [(16, NB)], [VMEM] * 2, omega, zeta, dtype=F32)

    spread = call(
        spread_kernel,
        [(YL * Z, PH, HALF)],
        [HBM],
        wake[0],
        out_specs=[HBM],
        vmem=60,
        scratch=[
            pltpu.VMEM((PH, YL * HALF), BF),
            pltpu.VMEM((YL * Z, PH, HALF), BF),
            pltpu.SemaphoreType.DMA((YL + 1,)),
        ],
    )
    blocks = lax.all_to_all(spread, ("yl", "z"), 0, 0, tiled=True)

    near, far = call(
        pack_kernel,
        [(NB + 16, HALF)] * 2,
        [SMEM, VMEM, VMEM, VMEM],
        pos,
        basis[0],
        block_index,
        phase_index,
    )
    swap = [(0, 1), (1, 0)]
    by_yl = lax.ppermute(far, "yl", swap)
    by_c = lax.ppermute(near, "c", swap)
    by_both = lax.ppermute(by_yl, "c", swap)
    near, forward, inverse, powers = lax.optimization_barrier((near, forward, inverse, powers))

    joined, onehot = call(
        select_kernel,
        [(4 * NB, HALF), (4, NT, YL * Z * PH)],
        [SMEM] + [VMEM] * 4,
        pos,
        near,
        by_yl,
        by_c,
        by_both,
    )
    picked = call(project_kernel, [(PEERS, 4 * TS, NB)], [VMEM] * 3, blocks, joined, onehot)
    parts = lax.all_to_all(picked, PLANE, 0, 0, tiled=True)
    forcing = call(gather_sum_kernel, [(Z, 4 * TS, NB)], [VMEM], parts)
    forcing = lax.all_to_all(forcing, "z", 0, 0, tiled=True)
    harmonic = call(forward_kernel, [(PEERS, TS, NB)], [VMEM, VMEM], forward, forcing)
    harmonic = lax.all_to_all(harmonic, PLANE, 0, 0, tiled=True)
    physical = call(
        modal_kernel,
        [(Z, TD, NB)],
        [SMEM] + [VMEM] * 4,
        pos,
        harmonic,
        shapes[0],
        flex[0],
        powers,
        scratch=[pltpu.VMEM((NT, NB), F32)],
    )
    physical = lax.all_to_all(physical, "z", 0, 0, tiled=True)
    sectoral = call(inverse_kernel, [(PEERS, TD, NB)], [VMEM] * 2, inverse, physical)
    sectoral = lax.all_to_all(sectoral, PLANE, 0, 0, tiled=True)
    rows = stress_map.shape[1]
    stress = call(
        stress_kernel,
        [(rows, NT)],
        [VMEM, VMEM],
        sectoral,
        stress_map[0],
        out_specs=[HBM],
        scratch=[pltpu.VMEM((rows, NT), BF), pltpu.SemaphoreType.DMA((CHUNKS,))],
    )
    return stress[None]


def solution(mesh):
    sector, dof = ("yl", "z", "c"), ("x", "yh")
    return jax.shard_map(
        local,
        mesh=Mesh(mesh.devices.reshape(SIZES), AXES),
        in_specs=(
            P(sector, None, dof),
            P(sector, None, dof),
            P(sector, None),
            P(sector, None),
            P(sector, None, None),
            P(sector, None, None),
            P(sector, None),
            P(sector, None),
            P(sector, dof, None),
        ),
        out_specs=P(sector, dof, None),
        check_vma=False,
    )
```

```python
import numpy as np
import jax
import jax.numpy as jnp
from jax import lax
from jax.experimental import pallas as pl
from jax.experimental.pallas import tpu as pltpu
from jax.sharding import Mesh, PartitionSpec as P

AXES = ("yl", "z", "c", "x", "yh")
SIZES = (2, 16, 2, 4, 2)
PLANE = ("yl", "c", "x", "yh")
YL, Z, C, D = 2, 16, 2, 8
PEERS = YL * C * D
BLADES, PH, NT, NB, MODES = YL * Z * C, 8, 256, 128, 40
HALF = 896
TS = NT // PEERS
TD = NT // D
BF = jnp.bfloat16
F32 = jnp.float32
HI = lax.Precision.HIGHEST


def fourier_table(count):
    h = np.arange(count)[:, None]
    s = np.arange(count)[None, :]
    angle = 2.0 * np.pi * ((((h + 1) // 2) * s) % count) / count
    table = np.where(h % 2 == 1, np.cos(angle), np.sin(angle))
    table = np.where(h == 0, 1.0, table)
    edges = (h == 0) | (h == count - 1)
    return table * np.where(edges, np.sqrt(1.0 / count), np.sqrt(2.0 / count))


FOURIER = fourier_table(BLADES)


SHIFT = ((0, 1, -1, 2, -2, 3, -3, 4), (8, -7, 7, -6, 6, -5, 5, -4))
PACK = 48 + NB


def halves(table, axis):
    table = table.astype(np.float32)
    high = table.astype(BF)
    return np.stack([high, (table - high.astype(np.float32)).astype(BF)], axis=axis)


def forward_table():
    table = FOURIER.reshape(BLADES, YL, Z, C).transpose(0, 2, 1, 3).reshape(BLADES, BLADES)
    table = np.einsum("ij,tu->itju", table, np.eye(TS))
    return halves(table.reshape(BLADES * TS, BLADES * TS), 0)


def inverse_table():
    table = FOURIER.reshape(YL, Z, C, YL, Z, C)
    rows = []
    for z in range(Z):
        source = (z + np.array(SHIFT).T) % Z
        part = table[:, source][..., z, :]
        rows.append(part.transpose(4, 5, 0, 3, 1, 2).reshape(4, BLADES))
    table = np.einsum("zij,tu->zitju", np.stack(rows), np.eye(TS))
    return halves(table.reshape(Z, 4 * TS, BLADES * TS), 1)


FORWARD = forward_table()
INVERSE = inverse_table()


def dot_nt(a, b, **kw):
    return lax.dot_general(
        a, b, (((1,), (1,)), ((), ())), preferred_element_type=F32, **kw
    )


def spread_kernel(in_ref, out_ref, wake_ref, hold_ref, sems):
    copy = pltpu.make_async_copy(in_ref, wake_ref, sems.at[YL])
    copy.start()
    copy.wait()
    copies = []
    for half in range(YL):
        rows = pl.ds(half * Z, Z)
        part = wake_ref[:, half * HALF : (half + 1) * HALF]
        hold_ref[rows] = jnp.broadcast_to(part[None], (Z, PH, HALF))
        copies.append(pltpu.make_async_copy(hold_ref.at[rows], out_ref.at[rows], sems.at[half]))
        copies[-1].start()
    for copy in copies:
        copy.wait()


def pack_kernel(pos, basis_ref, block_ref, phase_ref, near_ref, far_ref):
    index = jnp.concatenate(
        [block_ref[...].astype(F32), phase_ref[...].astype(F32), jnp.zeros((14, NT), F32)], axis=0
    )
    index = jnp.concatenate([index, jnp.zeros((16, HALF - NT), F32)], axis=1).astype(BF)
    for k, ref in enumerate((near_ref, far_ref)):
        half = (pos[0] + k) & 1
        ref[0:NB] = basis_ref[:, pl.ds(pl.multiple_of(half * HALF, 128), HALF)]
        ref[NB : NB + 16] = index


def select_kernel(pos, *refs):
    basis_ref, onehot_ref = refs[4:]
    codes = []
    for r, ref in enumerate(refs[:4]):
        basis_ref[r * NB : (r + 1) * NB] = ref[0:NB]
        index = ref[NB : NB + 16, 0:NT].astype(F32)
        block, phase = index[0:1].astype(jnp.int32), index[1:2].astype(jnp.int32)
        code = ((block >> 1) * PH + phase).astype(F32)
        codes.append(jnp.where((block & 1) == pos[1], code, -1.0))
    codes = jnp.concatenate(codes + [jnp.zeros((4, NT), F32)], axis=0).T
    pair = lax.broadcasted_iota(jnp.int32, (NT, YL * Z * PH), 1).astype(F32)
    for r in range(4):
        onehot_ref[r] = jnp.where(codes[:, r : r + 1] == pair, 1.0, 0.0).astype(BF)


def project_kernel(wake_ref, basis_ref, onehot_ref, out_ref):
    table = dot_nt(wake_ref[...].reshape(YL * Z * PH, HALF), basis_ref[...]).astype(BF)
    picks = []
    for r in range(4):
        part = jnp.dot(
            onehot_ref[r], table[:, r * NB : (r + 1) * NB], preferred_element_type=F32
        )
        picks.append(part.reshape(PEERS, TS, NB))
    out_ref[...] = jnp.concatenate(picks, axis=1).astype(BF)


def gather_sum_kernel(in_ref, kept_ref, out_ref):
    sums = {}
    for yl in range(YL):
        for c in range(C):
            total = None
            for d in range(D):
                part = in_ref[(yl * C + c) * D + d].astype(F32)
                total = part if total is None else total + part
            sums[yl, c] = total
    rows = []
    for yl in range(YL):
        for c in range(C):
            total = None
            for y in range(YL):
                for k in range(C):
                    r = (yl ^ y) + 2 * (c ^ k)
                    part = sums[y, k][r * TS : (r + 1) * TS]
                    total = part if total is None else total + part
            rows.append(total)
    block = jnp.concatenate(rows, axis=0).astype(BF)
    out_ref[...] = jnp.broadcast_to(block[None], out_ref.shape)


def fourier_sum(table_ref, in_ref):
    block = in_ref[...].reshape(BLADES * TS, NB)
    return sum(jnp.dot(table_ref[k], block, preferred_element_type=F32) for k in range(2))


def forward_kernel(pos, table_ref, in_ref, shapes_ref, out_ref, hold_ref):
    hold_ref[...] = fourier_sum(table_ref, in_ref).reshape(BLADES, TS, NB)
    for yl in range(YL):
        for c in range(C):
            for d in range(D):
                parts = [
                    hold_ref[yl * Z * C + ((pos[2] + SHIFT[e][d] + Z) & (Z - 1)) * C + c]
                    for e in range(2)
                ]
                out_ref[(yl * C + c) * D + d] = jnp.concatenate(parts, axis=0).astype(BF)


def parameter_kernel(shapes_ref, flex_ref, omega_ref, zeta_ref, out_ref):
    rows = []
    for ref in (omega_ref, zeta_ref):
        value = ref[...]
        high = value.astype(BF).astype(F32)
        middle = (value - high).astype(BF).astype(F32)
        rows += [high, middle, value - high - middle]
    rows = jnp.concatenate(rows + [jnp.zeros((2, MODES), F32)], axis=0)
    rows = jnp.concatenate([rows, jnp.zeros((8, NB - MODES), F32)], axis=1)
    out_ref[...] = jnp.concatenate(
        [shapes_ref[...].astype(F32), rows, flex_ref[...].astype(F32)], axis=0
    ).astype(BF)


def prepare_kernel(first_ref, second_ref, shapes_ref, powers_ref):
    packs = [ref[0:48].astype(F32) for ref in (first_ref, second_ref)]
    none = jnp.zeros((64, NB), F32)
    rest = jnp.zeros((64 - MODES, NB), F32)
    shapes_ref[0] = jnp.concatenate([packs[0][0:MODES], rest, none], axis=0).astype(BF)
    shapes_ref[1] = jnp.concatenate([none, packs[1][0:MODES], rest], axis=0).astype(BF)
    damp = []
    for row in (MODES, MODES + 3):
        parts = [p[row : row + 1] + p[row + 1 : row + 2] + p[row + 2 : row + 3] for p in packs]
        damp.append(jnp.concatenate([p[:, 0:64] for p in parts], axis=1))
    omega, zeta = damp
    size = jnp.exp(-omega * zeta)
    angle = omega * jnp.sqrt(1.0 - zeta * zeta)
    real, imag = size * jnp.cos(angle), size * jnp.sin(angle)
    for k in range(8):
        powers_ref[2 * k : 2 * k + 1] = real
        powers_ref[2 * k + 1 : 2 * k + 2] = imag
        real, imag = real * real - imag * imag, 2.0 * real * imag


def modal_kernel(in_ref, first_ref, second_ref, shapes_ref, powers_ref, out_ref):
    block = in_ref[...].astype(F32)
    force = [block[:, e * TS : (e + 1) * TS].reshape(NT, NB).astype(BF) for e in range(2)]
    real = dot_nt(force[0], shapes_ref[0]) + dot_nt(force[1], shapes_ref[1])
    imag = jnp.zeros_like(real)
    row = lax.broadcasted_iota(jnp.int32, (NT, NB), 0)
    for k in range(8):
        s = 2**k
        pr, pi = powers_ref[2 * k : 2 * k + 1, :], powers_ref[2 * k + 1 : 2 * k + 2, :]
        if s < 8:
            sr = jnp.where(row >= s, pltpu.roll(real, s, 0), 0.0)
            if k == 0:
                real, imag = real + pr * sr, pi * sr
            else:
                si = jnp.where(row >= s, pltpu.roll(imag, s, 0), 0.0)
                real, imag = real + (pr * sr - pi * si), imag + (pr * si + pi * sr)
        else:
            sr, si = real[: NT - s], imag[: NT - s]
            real = jnp.concatenate([real[:s], real[s:] + (pr * sr - pi * si)], axis=0)
            imag = jnp.concatenate([imag[:s], imag[s:] + (pr * si + pi * sr)], axis=0)
    high = imag.astype(BF)
    low = (imag - high.astype(F32)).astype(BF)
    parts = []
    for e, ref in enumerate((first_ref, second_ref)):
        total = (
            jnp.dot(high, shapes_ref[e], preferred_element_type=F32)
            + jnp.dot(low, shapes_ref[e], preferred_element_type=F32)
            + dot_nt(force[e], ref[48:PACK])
        )
        parts.append(total.reshape(PEERS, TS, NB))
    out_ref[...] = jnp.concatenate(parts, axis=1).astype(BF)


def inverse_kernel(table_ref, in_ref, out_ref):
    block = fourier_sum(table_ref, in_ref).astype(BF)
    for s in range(4):
        part = block[s * TS : (s + 1) * TS]
        out_ref[s * D : (s + 1) * D] = jnp.broadcast_to(part[None], (D, TS, NB))


CHUNKS = 8


def stress_kernel(in_ref, map_ref, out_ref, hold_ref, sems):
    motion = in_ref[...].reshape(NT, NB)
    step = map_ref.shape[0] // CHUNKS
    copies = []
    for k in range(CHUNKS):
        rows = pl.ds(k * step, step)
        hold_ref[rows] = dot_nt(map_ref[rows], motion).astype(BF)
        copies.append(pltpu.make_async_copy(hold_ref.at[rows], out_ref.at[rows], sems.at[k]))
        copies[-1].start()
    for copy in copies:
        copy.wait()


VMEM = pl.BlockSpec(memory_space=pltpu.VMEM)
SMEM = pl.BlockSpec(memory_space=pltpu.SMEM)
HBM = pl.BlockSpec(memory_space=pl.ANY)


def call(kernel, outs, specs, *args, out_specs=None, scratch=(), dtypes=(BF, BF), vmem=24):
    outs = [jax.ShapeDtypeStruct(shape, dtype) for shape, dtype in zip(outs, dtypes)]
    got = pl.pallas_call(
        kernel,
        out_shape=outs,
        in_specs=specs,
        out_specs=out_specs or [VMEM] * len(outs),
        scratch_shapes=list(scratch),
        compiler_params=pltpu.CompilerParams(vmem_limit_bytes=vmem * 1024 * 1024),
    )(*args)
    return got[0] if len(outs) == 1 else got


def local(wake, basis, block_index, phase_index, shapes, flex, omega, zeta, stress_map):
    yl, z, c = lax.axis_index("yl"), lax.axis_index("z"), lax.axis_index("c")
    pos = jnp.stack([yl, c, z]).astype(jnp.int32)
    inverse = lax.dynamic_slice(jnp.asarray(INVERSE), (z, 0, 0, 0), (1,) + INVERSE.shape[1:])[0]
    pack = call(parameter_kernel, [(PACK, NB)], [VMEM] * 4, shapes[0], flex[0], omega, zeta)
    route = [
        [(i * D + k, (i - SHIFT[e][k]) % Z * D + k) for i in range(Z) for k in range(D)]
        for e in range(2)
    ]

    spread = call(
        spread_kernel,
        [(YL * Z, PH, HALF)],
        [HBM],
        wake[0],
        out_specs=[HBM],
        vmem=60,
        scratch=[
            pltpu.VMEM((PH, YL * HALF), BF),
            pltpu.VMEM((YL * Z, PH, HALF), BF),
            pltpu.SemaphoreType.DMA((YL + 1,)),
        ],
    )
    blocks = lax.all_to_all(spread, ("yl", "z"), 0, 0, tiled=True)

    near, far = call(
        pack_kernel,
        [(NB + 16, HALF)] * 2,
        [SMEM, VMEM, VMEM, VMEM],
        pos,
        basis[0],
        block_index,
        phase_index,
    )
    swap = [(0, 1), (1, 0)]
    by_yl = lax.ppermute(far, "yl", swap)
    by_c = lax.ppermute(near, "c", swap)
    by_both = lax.ppermute(by_yl, "c", swap)
    near, inverse, pack = lax.optimization_barrier((near, inverse, pack))

    joined, onehot = call(
        select_kernel,
        [(4 * NB, HALF), (4, NT, YL * Z * PH)],
        [SMEM] + [VMEM] * 4,
        pos,
        near,
        by_yl,
        by_c,
        by_both,
    )
    picked = call(project_kernel, [(PEERS, 4 * TS, NB)], [VMEM] * 3, blocks, joined, onehot)
    column = ("z", "x", "yh")
    pack, picked = lax.optimization_barrier((pack, picked))
    first = lax.ppermute(pack, column, route[0])
    parts = lax.all_to_all(picked, PLANE, 0, 0, tiled=True)
    forcing = call(gather_sum_kernel, [(Z, 4 * TS, NB)], [VMEM, HBM], parts, first)
    pack, forcing = lax.optimization_barrier((pack, forcing))
    second = lax.ppermute(pack, column, route[1])
    spreads, powers = call(
        prepare_kernel, [(2, NB, NB), (16, NB)], [VMEM] * 2, first, second, dtypes=(BF, F32)
    )
    forcing = lax.all_to_all(forcing, "z", 0, 0, tiled=True)
    harmonic = call(
        forward_kernel,
        [(PEERS, 2 * TS, NB)],
        [SMEM, VMEM, VMEM, HBM],
        pos,
        jnp.asarray(FORWARD),
        forcing,
        spreads,
        scratch=[pltpu.VMEM((BLADES, TS, NB), F32)],
    )
    harmonic = lax.all_to_all(harmonic, PLANE, 0, 0, tiled=True)
    physical = call(
        modal_kernel,
        [(PEERS, 2 * TS, NB)],
        [VMEM] * 5,
        harmonic,
        first,
        second,
        spreads,
        powers,
    )
    physical = lax.all_to_all(physical, PLANE, 0, 0, tiled=True)
    sectoral = call(inverse_kernel, [(PEERS, TS, NB)], [VMEM] * 2, inverse, physical)
    sectoral = lax.all_to_all(sectoral, PLANE, 0, 0, tiled=True)
    rows = stress_map.shape[1]
    stress = call(
        stress_kernel,
        [(rows, NT)],
        [VMEM, VMEM],
        sectoral,
        stress_map[0],
        out_specs=[HBM],
        scratch=[pltpu.VMEM((rows, NT), BF), pltpu.SemaphoreType.DMA((CHUNKS,))],
    )
    return stress[None]


def solution(mesh):
    sector, dof = ("yl", "z", "c"), ("x", "yh")
    return jax.shard_map(
        local,
        mesh=Mesh(mesh.devices.reshape(SIZES), AXES),
        in_specs=(
            P(sector, None, dof),
            P(sector, None, dof),
            P(sector, None),
            P(sector, None),
            P(sector, None, None),
            P(sector, None, None),
            P(sector, None),
            P(sector, None),
            P(sector, dof, None),
        ),
        out_specs=P(sector, dof, None),
        check_vma=False,
    )
```

```python
import numpy as np
import jax
import jax.numpy as jnp
from jax import lax
from jax.experimental import pallas as pl
from jax.experimental.pallas import tpu as pltpu
from jax.sharding import Mesh, PartitionSpec as P

AXES = ("yl", "z", "c", "x", "yh")
SIZES = (2, 16, 2, 4, 2)
PLANE = ("yl", "c", "x", "yh")
YL, Z, C, D = 2, 16, 2, 8
PEERS = YL * C * D
BLADES, PH, NT, NB, MODES = YL * Z * C, 8, 256, 128, 40
HALF = 896
TS = NT // PEERS
TD = NT // D
BF = jnp.bfloat16
F32 = jnp.float32
HI = lax.Precision.HIGHEST


def fourier_table(count):
    h = np.arange(count)[:, None]
    s = np.arange(count)[None, :]
    angle = 2.0 * np.pi * ((((h + 1) // 2) * s) % count) / count
    table = np.where(h % 2 == 1, np.cos(angle), np.sin(angle))
    table = np.where(h == 0, 1.0, table)
    edges = (h == 0) | (h == count - 1)
    return table * np.where(edges, np.sqrt(1.0 / count), np.sqrt(2.0 / count))


FOURIER = fourier_table(BLADES)


SHIFT = ((0, 1, -1, 2, -2, 3, -3, 4), (8, -7, 7, -6, 6, -5, 5, -4))
HOPS = (SHIFT[0], (4, -3, 3, -2, 2, -1, 1, 0), (4, -4, 4, -4, 4, -4, 4, -4))
PACK = 48 + NB


def halves(table, axis):
    table = table.astype(np.float32)
    high = table.astype(BF)
    return np.stack([high, (table - high.astype(np.float32)).astype(BF)], axis=axis)


def forward_table():
    table = FOURIER.reshape(BLADES, YL, Z, C).transpose(0, 2, 1, 3).reshape(BLADES, BLADES)
    table = np.einsum("ij,tu->itju", table, np.eye(TS))
    return halves(table.reshape(BLADES * TS, BLADES * TS), 0)


def inverse_table():
    table = FOURIER.reshape(YL, Z, C, YL, Z, C)
    rows = []
    for z in range(Z):
        source = (z + np.array(SHIFT).T) % Z
        part = table[:, source][..., z, :]
        rows.append(part.transpose(4, 5, 0, 3, 1, 2).reshape(4, BLADES))
    table = np.einsum("zij,tu->zitju", np.stack(rows), np.eye(TS))
    return halves(table.reshape(Z, 4 * TS, BLADES * TS), 1)


FORWARD = forward_table()
INVERSE = inverse_table()


def dot_nt(a, b, **kw):
    return lax.dot_general(
        a, b, (((1,), (1,)), ((), ())), preferred_element_type=F32, **kw
    )


def spread_kernel(in_ref, out_ref, wake_ref, hold_ref, sems):
    copy = pltpu.make_async_copy(in_ref, wake_ref, sems.at[YL])
    copy.start()
    copy.wait()
    copies = []
    for half in range(YL):
        rows = pl.ds(half * Z, Z)
        part = wake_ref[:, half * HALF : (half + 1) * HALF]
        hold_ref[rows] = jnp.broadcast_to(part[None], (Z, PH, HALF))
        copies.append(pltpu.make_async_copy(hold_ref.at[rows], out_ref.at[rows], sems.at[half]))
        copies[-1].start()
    for copy in copies:
        copy.wait()


def pack_kernel(pos, basis_ref, block_ref, phase_ref, near_ref, far_ref):
    index = jnp.concatenate(
        [block_ref[...].astype(F32), phase_ref[...].astype(F32), jnp.zeros((14, NT), F32)], axis=0
    )
    index = jnp.concatenate([index, jnp.zeros((16, HALF - NT), F32)], axis=1).astype(BF)
    for k, ref in enumerate((near_ref, far_ref)):
        half = (pos[0] + k) & 1
        ref[0:NB] = basis_ref[:, pl.ds(pl.multiple_of(half * HALF, 128), HALF)]
        ref[NB : NB + 16] = index


def select_kernel(pos, *refs):
    basis_ref, onehot_ref = refs[4:]
    codes = []
    for r, ref in enumerate(refs[:4]):
        basis_ref[r * NB : (r + 1) * NB] = ref[0:NB]
        index = ref[NB : NB + 16, 0:NT].astype(F32)
        block, phase = index[0:1].astype(jnp.int32), index[1:2].astype(jnp.int32)
        code = ((block >> 1) * PH + phase).astype(F32)
        codes.append(jnp.where((block & 1) == pos[1], code, -1.0))
    codes = jnp.concatenate(codes + [jnp.zeros((4, NT), F32)], axis=0).T
    pair = lax.broadcasted_iota(jnp.int32, (NT, YL * Z * PH), 1).astype(F32)
    for r in range(4):
        onehot_ref[r] = jnp.where(codes[:, r : r + 1] == pair, 1.0, 0.0).astype(BF)


def project_kernel(wake_ref, basis_ref, onehot_ref, out_ref):
    table = dot_nt(wake_ref[...].reshape(YL * Z * PH, HALF), basis_ref[...]).astype(BF)
    picks = []
    for r in range(4):
        part = jnp.dot(
            onehot_ref[r], table[:, r * NB : (r + 1) * NB], preferred_element_type=F32
        )
        picks.append(part.reshape(PEERS, TS, NB))
    out_ref[...] = jnp.concatenate(picks, axis=1).astype(BF)


def gather_sum_kernel(in_ref, first_ref, middle_ref, out_ref):
    sums = {}
    for yl in range(YL):
        for c in range(C):
            total = None
            for d in range(D):
                part = in_ref[(yl * C + c) * D + d].astype(F32)
                total = part if total is None else total + part
            sums[yl, c] = total
    rows = []
    for yl in range(YL):
        for c in range(C):
            total = None
            for y in range(YL):
                for k in range(C):
                    r = (yl ^ y) + 2 * (c ^ k)
                    part = sums[y, k][r * TS : (r + 1) * TS]
                    total = part if total is None else total + part
            rows.append(total)
    block = jnp.concatenate(rows, axis=0).astype(BF)
    out_ref[...] = jnp.broadcast_to(block[None], out_ref.shape)


def fourier_sum(table_ref, in_ref):
    block = in_ref[...].reshape(BLADES * TS, NB)
    return sum(jnp.dot(table_ref[k], block, preferred_element_type=F32) for k in range(2))


def forward_kernel(pos, table_ref, in_ref, shapes_ref, out_ref, hold_ref):
    hold_ref[...] = fourier_sum(table_ref, in_ref).reshape(BLADES, TS, NB)
    for yl in range(YL):
        for c in range(C):
            for d in range(D):
                parts = [
                    hold_ref[yl * Z * C + ((pos[2] + SHIFT[e][d] + Z) & (Z - 1)) * C + c]
                    for e in range(2)
                ]
                out_ref[(yl * C + c) * D + d] = jnp.concatenate(parts, axis=0).astype(BF)


def parameter_kernel(shapes_ref, flex_ref, omega_ref, zeta_ref, out_ref):
    rows = []
    for ref in (omega_ref, zeta_ref):
        value = ref[...]
        high = value.astype(BF).astype(F32)
        middle = (value - high).astype(BF).astype(F32)
        rows += [high, middle, value - high - middle]
    rows = jnp.concatenate(rows + [jnp.zeros((2, MODES), F32)], axis=0)
    rows = jnp.concatenate([rows, jnp.zeros((8, NB - MODES), F32)], axis=1)
    out_ref[...] = jnp.concatenate(
        [shapes_ref[...].astype(F32), rows, flex_ref[...].astype(F32)], axis=0
    ).astype(BF)


def prepare_kernel(first_ref, second_ref, shapes_ref, powers_ref):
    packs = [ref[0:48].astype(F32) for ref in (first_ref, second_ref)]
    none = jnp.zeros((64, NB), F32)
    rest = jnp.zeros((64 - MODES, NB), F32)
    shapes_ref[0] = jnp.concatenate([packs[0][0:MODES], rest, none], axis=0).astype(BF)
    shapes_ref[1] = jnp.concatenate([none, packs[1][0:MODES], rest], axis=0).astype(BF)
    damp = []
    for row in (MODES, MODES + 3):
        parts = [p[row : row + 1] + p[row + 1 : row + 2] + p[row + 2 : row + 3] for p in packs]
        damp.append(jnp.concatenate([p[:, 0:64] for p in parts], axis=1))
    omega, zeta = damp
    size = jnp.exp(-omega * zeta)
    angle = omega * jnp.sqrt(1.0 - zeta * zeta)
    real, imag = size * jnp.cos(angle), size * jnp.sin(angle)
    for k in range(8):
        powers_ref[2 * k : 2 * k + 1] = real
        powers_ref[2 * k + 1 : 2 * k + 2] = imag
        real, imag = real * real - imag * imag, 2.0 * real * imag


def modal_kernel(in_ref, first_ref, second_ref, shapes_ref, powers_ref, out_ref):
    block = in_ref[...].astype(F32)
    force = [block[:, e * TS : (e + 1) * TS].reshape(NT, NB).astype(BF) for e in range(2)]
    real = dot_nt(force[0], shapes_ref[0]) + dot_nt(force[1], shapes_ref[1])
    imag = jnp.zeros_like(real)
    row = lax.broadcasted_iota(jnp.int32, (NT, NB), 0)
    for k in range(8):
        s = 2**k
        pr, pi = powers_ref[2 * k : 2 * k + 1, :], powers_ref[2 * k + 1 : 2 * k + 2, :]
        if s < 8:
            sr = jnp.where(row >= s, pltpu.roll(real, s, 0), 0.0)
            if k == 0:
                real, imag = real + pr * sr, pi * sr
            else:
                si = jnp.where(row >= s, pltpu.roll(imag, s, 0), 0.0)
                real, imag = real + (pr * sr - pi * si), imag + (pr * si + pi * sr)
        else:
            sr, si = real[: NT - s], imag[: NT - s]
            real = jnp.concatenate([real[:s], real[s:] + (pr * sr - pi * si)], axis=0)
            imag = jnp.concatenate([imag[:s], imag[s:] + (pr * si + pi * sr)], axis=0)
    high = imag.astype(BF)
    low = (imag - high.astype(F32)).astype(BF)
    parts = []
    for e, ref in enumerate((first_ref, second_ref)):
        total = (
            jnp.dot(high, shapes_ref[e], preferred_element_type=F32)
            + jnp.dot(low, shapes_ref[e], preferred_element_type=F32)
            + dot_nt(force[e], ref[48:PACK])
        )
        parts.append(total.reshape(PEERS, TS, NB))
    out_ref[...] = jnp.concatenate(parts, axis=1).astype(BF)


def inverse_kernel(table_ref, in_ref, out_ref):
    block = fourier_sum(table_ref, in_ref).astype(BF)
    for s in range(4):
        part = block[s * TS : (s + 1) * TS]
        out_ref[s * D : (s + 1) * D] = jnp.broadcast_to(part[None], (D, TS, NB))


CHUNKS = 8


def stress_kernel(in_ref, map_ref, out_ref, hold_ref, sems):
    motion = in_ref[...].reshape(NT, NB)
    step = map_ref.shape[0] // CHUNKS
    copies = []
    for k in range(CHUNKS):
        rows = pl.ds(k * step, step)
        hold_ref[rows] = dot_nt(map_ref[rows], motion).astype(BF)
        copies.append(pltpu.make_async_copy(hold_ref.at[rows], out_ref.at[rows], sems.at[k]))
        copies[-1].start()
    for copy in copies:
        copy.wait()


VMEM = pl.BlockSpec(memory_space=pltpu.VMEM)
SMEM = pl.BlockSpec(memory_space=pltpu.SMEM)
HBM = pl.BlockSpec(memory_space=pl.ANY)


def call(kernel, outs, specs, *args, out_specs=None, scratch=(), dtypes=(BF, BF), vmem=24):
    outs = [jax.ShapeDtypeStruct(shape, dtype) for shape, dtype in zip(outs, dtypes)]
    got = pl.pallas_call(
        kernel,
        out_shape=outs,
        in_specs=specs,
        out_specs=out_specs or [VMEM] * len(outs),
        scratch_shapes=list(scratch),
        compiler_params=pltpu.CompilerParams(vmem_limit_bytes=vmem * 1024 * 1024),
    )(*args)
    return got[0] if len(outs) == 1 else got


def local(wake, basis, block_index, phase_index, shapes, flex, omega, zeta, stress_map):
    yl, z, c = lax.axis_index("yl"), lax.axis_index("z"), lax.axis_index("c")
    pos = jnp.stack([yl, c, z]).astype(jnp.int32)
    inverse = lax.dynamic_slice(jnp.asarray(INVERSE), (z, 0, 0, 0), (1,) + INVERSE.shape[1:])[0]
    pack = call(parameter_kernel, [(PACK, NB)], [VMEM] * 4, shapes[0], flex[0], omega, zeta)
    route = [
        [(i * D + k, (i - hops[k]) % Z * D + k) for i in range(Z) for k in range(D)]
        for hops in HOPS
    ]

    spread = call(
        spread_kernel,
        [(YL * Z, PH, HALF)],
        [HBM],
        wake[0],
        out_specs=[HBM],
        vmem=60,
        scratch=[
            pltpu.VMEM((PH, YL * HALF), BF),
            pltpu.VMEM((YL * Z, PH, HALF), BF),
            pltpu.SemaphoreType.DMA((YL + 1,)),
        ],
    )
    blocks = lax.all_to_all(spread, ("yl", "z"), 0, 0, tiled=True)

    near, far = call(
        pack_kernel,
        [(NB + 16, HALF)] * 2,
        [SMEM, VMEM, VMEM, VMEM],
        pos,
        basis[0],
        block_index,
        phase_index,
    )
    swap = [(0, 1), (1, 0)]
    by_yl = lax.ppermute(far, "yl", swap)
    by_c = lax.ppermute(near, "c", swap)
    by_both = lax.ppermute(by_yl, "c", swap)
    near, inverse, pack = lax.optimization_barrier((near, inverse, pack))

    joined, onehot = call(
        select_kernel,
        [(4 * NB, HALF), (4, NT, YL * Z * PH)],
        [SMEM] + [VMEM] * 4,
        pos,
        near,
        by_yl,
        by_c,
        by_both,
    )
    picked = call(project_kernel, [(PEERS, 4 * TS, NB)], [VMEM] * 3, blocks, joined, onehot)
    column = ("z", "x", "yh")
    pack, picked = lax.optimization_barrier((pack, picked))
    first = lax.ppermute(pack, column, route[0])
    middle = lax.ppermute(pack, column, route[1])
    parts = lax.all_to_all(picked, PLANE, 0, 0, tiled=True)
    forcing = call(gather_sum_kernel, [(Z, 4 * TS, NB)], [VMEM, HBM, HBM], parts, first, middle)
    middle, forcing = lax.optimization_barrier((middle, forcing))
    second = lax.ppermute(middle, column, route[2])
    spreads, powers = call(
        prepare_kernel, [(2, NB, NB), (16, NB)], [VMEM] * 2, first, second, dtypes=(BF, F32)
    )
    forcing = lax.all_to_all(forcing, "z", 0, 0, tiled=True)
    harmonic = call(
        forward_kernel,
        [(PEERS, 2 * TS, NB)],
        [SMEM, VMEM, VMEM, HBM],
        pos,
        jnp.asarray(FORWARD),
        forcing,
        spreads,
        scratch=[pltpu.VMEM((BLADES, TS, NB), F32)],
    )
    harmonic = lax.all_to_all(harmonic, PLANE, 0, 0, tiled=True)
    physical = call(
        modal_kernel,
        [(PEERS, 2 * TS, NB)],
        [VMEM] * 5,
        harmonic,
        first,
        second,
        spreads,
        powers,
    )
    physical = lax.all_to_all(physical, PLANE, 0, 0, tiled=True)
    sectoral = call(inverse_kernel, [(PEERS, TS, NB)], [VMEM] * 2, inverse, physical)
    sectoral = lax.all_to_all(sectoral, PLANE, 0, 0, tiled=True)
    rows = stress_map.shape[1]
    stress = call(
        stress_kernel,
        [(rows, NT)],
        [VMEM, VMEM],
        sectoral,
        stress_map[0],
        out_specs=[HBM],
        scratch=[pltpu.VMEM((rows, NT), BF), pltpu.SemaphoreType.DMA((CHUNKS,))],
    )
    return stress[None]


def solution(mesh):
    sector, dof = ("yl", "z", "c"), ("x", "yh")
    return jax.shard_map(
        local,
        mesh=Mesh(mesh.devices.reshape(SIZES), AXES),
        in_specs=(
            P(sector, None, dof),
            P(sector, None, dof),
            P(sector, None),
            P(sector, None),
            P(sector, None, None),
            P(sector, None, None),
            P(sector, None),
            P(sector, None),
            P(sector, dof, None),
        ),
        out_specs=P(sector, dof, None),
        check_vma=False,
    )
```

```python
import numpy as np
import jax
import jax.numpy as jnp
from jax import lax
from jax.experimental import pallas as pl
from jax.experimental.pallas import tpu as pltpu
from jax.sharding import Mesh, PartitionSpec as P

AXES = ("yl", "z", "c", "x", "yh")
SIZES = (2, 16, 2, 4, 2)
PLANE = ("yl", "c", "x", "yh")
YL, Z, C, D = 2, 16, 2, 8
PEERS = YL * C * D
BLADES, PH, NT, NB, MODES = YL * Z * C, 8, 256, 128, 40
COLS = 1792
TS = NT // PEERS
TD = NT // D
BF = jnp.bfloat16
F32 = jnp.float32
HI = lax.Precision.HIGHEST


def fourier_table(count):
    h = np.arange(count)[:, None]
    s = np.arange(count)[None, :]
    angle = 2.0 * np.pi * ((((h + 1) // 2) * s) % count) / count
    table = np.where(h % 2 == 1, np.cos(angle), np.sin(angle))
    table = np.where(h == 0, 1.0, table)
    edges = (h == 0) | (h == count - 1)
    return table * np.where(edges, np.sqrt(1.0 / count), np.sqrt(2.0 / count))


FOURIER = fourier_table(BLADES)


def forward_table():
    table = FOURIER.reshape(YL, Z, C, YL, Z, C).transpose(1, 0, 2, 4, 3, 5)
    table = np.einsum("zij,tu->zitju", table.reshape(Z, 4, BLADES), np.eye(TS))
    table = table.reshape(Z, 4 * TS, BLADES * TS).astype(np.float32)
    high = table.astype(BF)
    return np.stack([high, (table - high.astype(np.float32)).astype(BF)], axis=1)


FORWARD = forward_table()


def inverse_table():
    table = FOURIER.reshape(YL, Z, C, YL, Z, C).transpose(0, 2, 4, 3, 5, 1)
    table = np.einsum("dij,tu->ditju", table.reshape(BLADES, 4, Z), np.eye(TS))
    table = table.reshape(BLADES, 4 * TS, Z * TS).astype(np.float32)
    high = table.astype(BF)
    return np.stack([high, (table - high.astype(np.float32)).astype(BF)], axis=1)


INVERSE = inverse_table()


def dot_nt(a, b, **kw):
    return lax.dot_general(
        a, b, (((1,), (1,)), ((), ())), preferred_element_type=F32, **kw
    )


def spread_kernel(in_ref, out_ref, wake_ref, hold_ref, sems):
    copy = pltpu.make_async_copy(in_ref, wake_ref, sems.at[2])
    copy.start()
    copy.wait()
    copies = []
    for k in range(2):
        rows = pl.ds(k * Z // 2, Z // 2)
        hold_ref[rows] = jnp.broadcast_to(wake_ref[...][None], (Z // 2, PH, COLS))
        copies.append(pltpu.make_async_copy(hold_ref.at[rows], out_ref.at[rows], sems.at[k]))
        copies[-1].start()
    for copy in copies:
        copy.wait()


def pack_kernel(basis_ref, block_ref, phase_ref, out_ref):
    index = jnp.concatenate(
        [block_ref[...].astype(F32), phase_ref[...].astype(F32), jnp.zeros((14, NT), F32)], axis=0
    )
    index = jnp.concatenate([index, jnp.zeros((16, COLS - NT), F32)], axis=1).astype(BF)
    out_ref[0:NB] = basis_ref[...]
    out_ref[NB : NB + 16] = index


def select_kernel(pos, *refs):
    basis_ref, onehot_ref = refs[4:]
    codes = []
    for r, ref in enumerate(refs[:4]):
        basis_ref[r * NB : (r + 1) * NB] = ref[0:NB]
        index = ref[NB : NB + 16, 0:NT].astype(F32)
        block, phase = index[0:1].astype(jnp.int32), index[1:2].astype(jnp.int32)
        code = (((block >> 1) & (Z - 1)) * PH + phase).astype(F32)
        here = ((block & 1) == pos[1]) & ((block >> 5) == pos[0])
        codes.append(jnp.where(here, code, -1.0))
    codes = jnp.concatenate(codes + [jnp.zeros((4, NT), F32)], axis=0).T
    pair = lax.broadcasted_iota(jnp.int32, (NT, Z * PH), 1).astype(F32)
    for r in range(4):
        onehot_ref[r] = jnp.where(codes[:, r : r + 1] == pair, 1.0, 0.0).astype(BF)


def project_kernel(wake_ref, basis_ref, onehot_ref, out_ref):
    table = dot_nt(wake_ref[...].reshape(Z * PH, COLS), basis_ref[...]).astype(BF)
    picks = []
    for r in range(4):
        part = jnp.dot(
            onehot_ref[r], table[:, r * NB : (r + 1) * NB], preferred_element_type=F32
        )
        picks.append(part.reshape(PEERS, TS, NB))
    out_ref[...] = jnp.concatenate(picks, axis=1).astype(BF)


def gather_sum_kernel(in_ref, out_ref):
    sums = {}
    for yl in range(YL):
        for c in range(C):
            total = None
            for d in range(D):
                part = in_ref[(yl * C + c) * D + d].astype(F32)
                total = part if total is None else total + part
            sums[yl, c] = total
    rows = []
    for yl in range(YL):
        for c in range(C):
            total = None
            for y in range(YL):
                for k in range(C):
                    r = (yl ^ y) + 2 * (c ^ k)
                    part = sums[y, k][r * TS : (r + 1) * TS]
                    total = part if total is None else total + part
            rows.append(total)
    block = jnp.concatenate(rows, axis=0).astype(BF)
    out_ref[...] = jnp.broadcast_to(block[None], out_ref.shape)


def forward_kernel(table_ref, in_ref, out_ref):
    block = in_ref[...].reshape(BLADES * TS, NB)
    block = sum(jnp.dot(table_ref[k], block, preferred_element_type=F32) for k in range(2))
    for h in range(4):
        part = block[h * TS : (h + 1) * TS].astype(BF)
        out_ref[h * D : (h + 1) * D] = jnp.broadcast_to(part[None], (D, TS, NB))


def powers_kernel(omega_ref, zeta_ref, out_ref):
    omega, zeta = omega_ref[...], zeta_ref[...]
    size = jnp.exp(-omega * zeta)
    angle = omega * jnp.sqrt(1.0 - zeta * zeta)
    real, imag = size * jnp.cos(angle), size * jnp.sin(angle)
    out_ref[...] = jnp.zeros_like(out_ref)
    for k in range(8):
        out_ref[2 * k : 2 * k + 1, 0:MODES] = real
        out_ref[2 * k + 1 : 2 * k + 2, 0:MODES] = imag
        real, imag = real * real - imag * imag, 2.0 * real * imag


def modal_kernel(pos, in_ref, shapes_ref, flex_ref, powers_ref, out_ref, hold_ref):
    shapes = jnp.concatenate(
        [shapes_ref[...].astype(F32), jnp.zeros((NB - MODES, NB), F32)], axis=0
    ).astype(BF)
    real = dot_nt(in_ref[...].reshape(NT, NB), shapes)
    imag = jnp.zeros_like(real)
    row = lax.broadcasted_iota(jnp.int32, (NT, NB), 0)
    for k in range(8):
        s = 2**k
        pr, pi = powers_ref[2 * k : 2 * k + 1, :], powers_ref[2 * k + 1 : 2 * k + 2, :]
        if s < 8:
            sr = jnp.where(row >= s, pltpu.roll(real, s, 0), 0.0)
            if k == 0:
                real, imag = real + pr * sr, pi * sr
            else:
                si = jnp.where(row >= s, pltpu.roll(imag, s, 0), 0.0)
                real, imag = real + (pr * sr - pi * si), imag + (pr * si + pi * sr)
        else:
            sr, si = real[: NT - s], imag[: NT - s]
            real = jnp.concatenate([real[:s], real[s:] + (pr * sr - pi * si)], axis=0)
            imag = jnp.concatenate([imag[:s], imag[s:] + (pr * si + pi * sr)], axis=0)
    hold_ref[...] = imag
    own = hold_ref[pl.ds(pl.multiple_of(pos[2] * TD, TD), TD), :]
    high = own.astype(BF)
    low = (own - high.astype(F32)).astype(BF)
    rows = in_ref[pl.ds(pos[2] * (TD // TS), TD // TS)].reshape(TD, NB)
    total = (
        jnp.dot(high, shapes, preferred_element_type=F32)
        + jnp.dot(low, shapes, preferred_element_type=F32)
        + dot_nt(rows, flex_ref[...])
    )
    out_ref[...] = jnp.broadcast_to(total.astype(BF)[None], out_ref.shape)


def inverse_kernel(table_ref, in_ref, out_ref):
    block = in_ref[...].astype(F32)
    parts = []
    for g in range(TD // TS):
        part = block[:, g * TS : (g + 1) * TS].reshape(Z * TS, NB).astype(BF)
        parts.append(
            sum(jnp.dot(table_ref[k], part, preferred_element_type=F32) for k in range(2))
        )
    for s in range(4):
        part = jnp.concatenate([p[s * TS : (s + 1) * TS] for p in parts], axis=0).astype(BF)
        out_ref[s * D : (s + 1) * D] = jnp.broadcast_to(part[None], (D, TD, NB))


CHUNKS = 8


def stress_kernel(in_ref, map_ref, out_ref, hold_ref, sems):
    total = None
    for q in range(YL * C):
        part = in_ref[q * D : (q + 1) * D].astype(F32)
        total = part if total is None else total + part
    motion = total.reshape(NT, NB).astype(BF)
    step = map_ref.shape[0] // CHUNKS
    copies = []
    for k in range(CHUNKS):
        rows = pl.ds(k * step, step)
        hold_ref[rows] = dot_nt(map_ref[rows], motion).astype(BF)
        copies.append(pltpu.make_async_copy(hold_ref.at[rows], out_ref.at[rows], sems.at[k]))
        copies[-1].start()
    for copy in copies:
        copy.wait()


VMEM = pl.BlockSpec(memory_space=pltpu.VMEM)
SMEM = pl.BlockSpec(memory_space=pltpu.SMEM)
HBM = pl.BlockSpec(memory_space=pl.ANY)


def call(kernel, outs, specs, *args, out_specs=None, scratch=(), dtype=BF, vmem=24):
    outs = [jax.ShapeDtypeStruct(shape, dtype) for shape in outs]
    got = pl.pallas_call(
        kernel,
        out_shape=outs,
        in_specs=specs,
        out_specs=out_specs or [VMEM] * len(outs),
        scratch_shapes=list(scratch),
        compiler_params=pltpu.CompilerParams(vmem_limit_bytes=vmem * 1024 * 1024),
    )(*args)
    return got[0] if len(outs) == 1 else got


def local(wake, basis, block_index, phase_index, shapes, flex, omega, zeta, stress_map):
    yl, z, c = lax.axis_index("yl"), lax.axis_index("z"), lax.axis_index("c")
    d = lax.axis_index("x") * 2 + lax.axis_index("yh")
    pos = jnp.stack([yl, c, d]).astype(jnp.int32)
    forward = lax.dynamic_slice(jnp.asarray(FORWARD), (z, 0, 0, 0), (1,) + FORWARD.shape[1:])[0]
    inverse = lax.dynamic_slice(
        jnp.asarray(INVERSE), ((yl * C + c) * Z + z, 0, 0, 0), (1,) + INVERSE.shape[1:]
    )[0]
    powers = call(powers_kernel, [(16, NB)], [VMEM] * 2, omega, zeta, dtype=F32)

    spread = call(
        spread_kernel,
        [(Z, PH, COLS)],
        [HBM],
        wake[0],
        out_specs=[HBM],
        vmem=60,
        scratch=[
            pltpu.VMEM((PH, COLS), BF),
            pltpu.VMEM((Z, PH, COLS), BF),
            pltpu.SemaphoreType.DMA((3,)),
        ],
    )
    blocks = lax.all_to_all(spread, "z", 0, 0, tiled=True)

    near = call(pack_kernel, [(NB + 16, COLS)], [VMEM] * 3, basis[0], block_index, phase_index)
    swap = [(0, 1), (1, 0)]
    by_yl = lax.ppermute(near, "yl", swap)
    by_c = lax.ppermute(near, "c", swap)
    by_both = lax.ppermute(by_yl, "c", swap)
    near, forward, inverse, powers = lax.optimization_barrier((near, forward, inverse, powers))

    joined, onehot = call(
        select_kernel,
        [(4 * NB, COLS), (4, NT, Z * PH)],
        [SMEM] + [VMEM] * 4,
        pos,
        near,
        by_yl,
        by_c,
        by_both,
    )
    picked = call(project_kernel, [(PEERS, 4 * TS, NB)], [VMEM] * 3, blocks, joined, onehot)
    parts = lax.all_to_all(picked, PLANE, 0, 0, tiled=True)
    forcing = call(gather_sum_kernel, [(Z, 4 * TS, NB)], [VMEM], parts)
    forcing = lax.all_to_all(forcing, "z", 0, 0, tiled=True)
    harmonic = call(forward_kernel, [(PEERS, TS, NB)], [VMEM, VMEM], forward, forcing)
    harmonic = lax.all_to_all(harmonic, PLANE, 0, 0, tiled=True)
    physical = call(
        modal_kernel,
        [(Z, TD, NB)],
        [SMEM] + [VMEM] * 4,
        pos,
        harmonic,
        shapes[0],
        flex[0],
        powers,
        scratch=[pltpu.VMEM((NT, NB), F32)],
    )
    physical = lax.all_to_all(physical, "z", 0, 0, tiled=True)
    sectoral = call(inverse_kernel, [(PEERS, TD, NB)], [VMEM] * 2, inverse, physical)
    sectoral = lax.all_to_all(sectoral, PLANE, 0, 0, tiled=True)
    rows = stress_map.shape[1]
    stress = call(
        stress_kernel,
        [(rows, NT)],
        [VMEM, VMEM],
        sectoral,
        stress_map[0],
        out_specs=[HBM],
        scratch=[pltpu.VMEM((rows, NT), BF), pltpu.SemaphoreType.DMA((CHUNKS,))],
    )
    return stress[None]


def solution(mesh):
    sector, dof = ("yl", "z", "c"), ("x", "yh")
    return jax.shard_map(
        local,
        mesh=Mesh(mesh.devices.reshape(SIZES), AXES),
        in_specs=(
            P(sector, None, dof),
            P(sector, None, dof),
            P(sector, None),
            P(sector, None),
            P(sector, None, None),
            P(sector, None, None),
            P(sector, None),
            P(sector, None),
            P(sector, dof, None),
        ),
        out_specs=P(sector, dof, None),
        check_vma=False,
    )
```

```python
import numpy as np
import jax
import jax.numpy as jnp
from jax import lax
from jax.experimental import pallas as pl
from jax.experimental.pallas import tpu as pltpu
from jax.sharding import Mesh, PartitionSpec as P

AXES = ("yl", "z", "c", "x", "yh")
SIZES = (2, 16, 2, 4, 2)
PLANE = ("yl", "c", "x", "yh")
YL, Z, C, D = 2, 16, 2, 8
PEERS = YL * C * D
BLADES, PH, NT, NB, MODES = YL * Z * C, 8, 256, 128, 40
COLS = 1792
TS = NT // PEERS
TD = NT // D
BF = jnp.bfloat16
F32 = jnp.float32
HI = lax.Precision.HIGHEST


def fourier_table(count):
    h = np.arange(count)[:, None]
    s = np.arange(count)[None, :]
    angle = 2.0 * np.pi * ((((h + 1) // 2) * s) % count) / count
    table = np.where(h % 2 == 1, np.cos(angle), np.sin(angle))
    table = np.where(h == 0, 1.0, table)
    edges = (h == 0) | (h == count - 1)
    return table * np.where(edges, np.sqrt(1.0 / count), np.sqrt(2.0 / count))


FOURIER = fourier_table(BLADES)


def forward_table():
    table = FOURIER.reshape(YL, Z, C, YL, Z, C).transpose(1, 0, 2, 4, 3, 5)
    table = np.einsum("zij,tu->zitju", table.reshape(Z, 4, BLADES), np.eye(TS))
    table = table.reshape(Z, 4 * TS, BLADES * TS).astype(np.float32)
    high = table.astype(BF)
    return np.stack([high, (table - high.astype(np.float32)).astype(BF)], axis=1)


FORWARD = forward_table()


def inverse_table():
    table = FOURIER.reshape(YL, Z, C, YL, Z, C).transpose(0, 2, 4, 3, 5, 1)
    table = np.einsum("dij,tu->ditju", table.reshape(BLADES, 4, Z), np.eye(TS))
    table = table.reshape(BLADES, 4 * TS, Z * TS).astype(np.float32)
    high = table.astype(BF)
    return np.stack([high, (table - high.astype(np.float32)).astype(BF)], axis=1)


INVERSE = inverse_table()


def dot_nt(a, b, **kw):
    return lax.dot_general(
        a, b, (((1,), (1,)), ((), ())), preferred_element_type=F32, **kw
    )


def spread_kernel(in_ref, out_ref, wake_ref, hold_ref, sems):
    copy = pltpu.make_async_copy(in_ref, wake_ref, sems.at[2])
    copy.start()
    copy.wait()
    copies = []
    for k in range(2):
        rows = pl.ds(k * Z // 2, Z // 2)
        hold_ref[rows] = jnp.broadcast_to(wake_ref[...][None], (Z // 2, PH, COLS))
        copies.append(pltpu.make_async_copy(hold_ref.at[rows], out_ref.at[rows], sems.at[k]))
        copies[-1].start()
    for copy in copies:
        copy.wait()


def pack_kernel(basis_ref, block_ref, phase_ref, out_ref):
    index = jnp.concatenate(
        [block_ref[...].astype(F32), phase_ref[...].astype(F32), jnp.zeros((14, NT), F32)], axis=0
    )
    index = jnp.concatenate([index, jnp.zeros((16, COLS - NT), F32)], axis=1).astype(BF)
    out_ref[0:NB] = basis_ref[...]
    out_ref[NB : NB + 16] = index


def project_kernel(pos, wake_ref, *refs):
    out_ref = refs[4]
    wake = wake_ref[...].reshape(Z * PH, COLS)
    codes = []
    for ref in refs[:4]:
        index = ref[NB : NB + 16, 0:NT].astype(F32)
        block, phase = index[0:1].astype(jnp.int32), index[1:2].astype(jnp.int32)
        code = (((block >> 1) & (Z - 1)) * PH + phase).astype(F32)
        here = ((block & 1) == pos[1]) & ((block >> 5) == pos[0])
        codes.append(jnp.where(here, code, -1.0))
    codes = jnp.concatenate(codes + [jnp.zeros((4, NT), F32)], axis=0).T
    pair = lax.broadcasted_iota(jnp.int32, (NT, Z * PH), 1).astype(F32)
    picks = []
    for r, ref in enumerate(refs[:4]):
        table = dot_nt(wake, ref[0:NB]).astype(BF)
        onehot = jnp.where(codes[:, r : r + 1] == pair, 1.0, 0.0).astype(BF)
        part = jnp.dot(onehot, table, preferred_element_type=F32)
        picks.append(part.reshape(PEERS, TS, NB))
    out_ref[...] = jnp.concatenate(picks, axis=1).astype(BF)


def gather_sum_kernel(in_ref, out_ref):
    sums = {}
    for yl in range(YL):
        for c in range(C):
            total = None
            for d in range(D):
                part = in_ref[(yl * C + c) * D + d].astype(F32)
                total = part if total is None else total + part
            sums[yl, c] = total
    rows = []
    for yl in range(YL):
        for c in range(C):
            total = None
            for y in range(YL):
                for k in range(C):
                    r = (yl ^ y) + 2 * (c ^ k)
                    part = sums[y, k][r * TS : (r + 1) * TS]
                    total = part if total is None else total + part
            rows.append(total)
    block = jnp.concatenate(rows, axis=0).astype(BF)
    out_ref[...] = jnp.broadcast_to(block[None], out_ref.shape)


def forward_kernel(table_ref, in_ref, out_ref):
    block = in_ref[...].reshape(BLADES * TS, NB)
    block = sum(jnp.dot(table_ref[k], block, preferred_element_type=F32) for k in range(2))
    for h in range(4):
        part = block[h * TS : (h + 1) * TS].astype(BF)
        out_ref[h * D : (h + 1) * D] = jnp.broadcast_to(part[None], (D, TS, NB))


def powers_kernel(omega_ref, zeta_ref, out_ref):
    omega, zeta = omega_ref[...], zeta_ref[...]
    size = jnp.exp(-omega * zeta)
    angle = omega * jnp.sqrt(1.0 - zeta * zeta)
    real, imag = size * jnp.cos(angle), size * jnp.sin(angle)
    out_ref[...] = jnp.zeros_like(out_ref)
    for k in range(8):
        out_ref[2 * k : 2 * k + 1, 0:MODES] = real
        out_ref[2 * k + 1 : 2 * k + 2, 0:MODES] = imag
        real, imag = real * real - imag * imag, 2.0 * real * imag


def modal_kernel(pos, in_ref, shapes_ref, flex_ref, powers_ref, out_ref, hold_ref):
    shapes = jnp.concatenate(
        [shapes_ref[...].astype(F32), jnp.zeros((NB - MODES, NB), F32)], axis=0
    ).astype(BF)
    real = dot_nt(in_ref[...].reshape(NT, NB), shapes)
    imag = jnp.zeros_like(real)
    row = lax.broadcasted_iota(jnp.int32, (NT, NB), 0)
    for k in range(8):
        s = 2**k
        pr, pi = powers_ref[2 * k : 2 * k + 1, :], powers_ref[2 * k + 1 : 2 * k + 2, :]
        if s < 8:
            sr = jnp.where(row >= s, pltpu.roll(real, s, 0), 0.0)
            if k == 0:
                real, imag = real + pr * sr, pi * sr
            else:
                si = jnp.where(row >= s, pltpu.roll(imag, s, 0), 0.0)
                real, imag = real + (pr * sr - pi * si), imag + (pr * si + pi * sr)
        else:
            sr, si = real[: NT - s], imag[: NT - s]
            real = jnp.concatenate([real[:s], real[s:] + (pr * sr - pi * si)], axis=0)
            imag = jnp.concatenate([imag[:s], imag[s:] + (pr * si + pi * sr)], axis=0)
    hold_ref[...] = imag
    own = hold_ref[pl.ds(pl.multiple_of(pos[2] * TD, TD), TD), :]
    high = own.astype(BF)
    low = (own - high.astype(F32)).astype(BF)
    rows = in_ref[pl.ds(pos[2] * (TD // TS), TD // TS)].reshape(TD, NB)
    total = (
        jnp.dot(high, shapes, preferred_element_type=F32)
        + jnp.dot(low, shapes, preferred_element_type=F32)
        + dot_nt(rows, flex_ref[...])
    )
    out_ref[...] = jnp.broadcast_to(total.astype(BF)[None], out_ref.shape)


def inverse_kernel(table_ref, in_ref, out_ref):
    block = in_ref[...].astype(F32)
    parts = []
    for g in range(TD // TS):
        part = block[:, g * TS : (g + 1) * TS].reshape(Z * TS, NB).astype(BF)
        parts.append(
            sum(jnp.dot(table_ref[k], part, preferred_element_type=F32) for k in range(2))
        )
    for s in range(4):
        part = jnp.concatenate([p[s * TS : (s + 1) * TS] for p in parts], axis=0).astype(BF)
        out_ref[s * D : (s + 1) * D] = jnp.broadcast_to(part[None], (D, TD, NB))


CHUNKS = 8


def stress_kernel(in_ref, map_ref, out_ref, hold_ref, sems):
    total = None
    for q in range(YL * C):
        part = in_ref[q * D : (q + 1) * D].astype(F32)
        total = part if total is None else total + part
    motion = total.reshape(NT, NB).astype(BF)
    step = map_ref.shape[0] // CHUNKS
    copies = []
    for k in range(CHUNKS):
        rows = pl.ds(k * step, step)
        hold_ref[rows] = dot_nt(map_ref[rows], motion).astype(BF)
        copies.append(pltpu.make_async_copy(hold_ref.at[rows], out_ref.at[rows], sems.at[k]))
        copies[-1].start()
    for copy in copies:
        copy.wait()


VMEM = pl.BlockSpec(memory_space=pltpu.VMEM)
SMEM = pl.BlockSpec(memory_space=pltpu.SMEM)
HBM = pl.BlockSpec(memory_space=pl.ANY)


def call(kernel, outs, specs, *args, out_specs=None, scratch=(), dtype=BF, vmem=24):
    outs = [jax.ShapeDtypeStruct(shape, dtype) for shape in outs]
    got = pl.pallas_call(
        kernel,
        out_shape=outs,
        in_specs=specs,
        out_specs=out_specs or [VMEM] * len(outs),
        scratch_shapes=list(scratch),
        compiler_params=pltpu.CompilerParams(vmem_limit_bytes=vmem * 1024 * 1024),
    )(*args)
    return got[0] if len(outs) == 1 else got


def local(wake, basis, block_index, phase_index, shapes, flex, omega, zeta, stress_map):
    yl, z, c = lax.axis_index("yl"), lax.axis_index("z"), lax.axis_index("c")
    d = lax.axis_index("x") * 2 + lax.axis_index("yh")
    pos = jnp.stack([yl, c, d]).astype(jnp.int32)
    forward = lax.dynamic_slice(jnp.asarray(FORWARD), (z, 0, 0, 0), (1,) + FORWARD.shape[1:])[0]
    inverse = lax.dynamic_slice(
        jnp.asarray(INVERSE), ((yl * C + c) * Z + z, 0, 0, 0), (1,) + INVERSE.shape[1:]
    )[0]
    powers = call(powers_kernel, [(16, NB)], [VMEM] * 2, omega, zeta, dtype=F32)

    spread = call(
        spread_kernel,
        [(Z, PH, COLS)],
        [HBM],
        wake[0],
        out_specs=[HBM],
        vmem=60,
        scratch=[
            pltpu.VMEM((PH, COLS), BF),
            pltpu.VMEM((Z, PH, COLS), BF),
            pltpu.SemaphoreType.DMA((3,)),
        ],
    )
    blocks = lax.all_to_all(spread, "z", 0, 0, tiled=True)

    near = call(pack_kernel, [(NB + 16, COLS)], [VMEM] * 3, basis[0], block_index, phase_index)
    swap = [(0, 1), (1, 0)]
    by_yl = lax.ppermute(near, "yl", swap)
    by_c = lax.ppermute(near, "c", swap)
    by_both = lax.ppermute(by_yl, "c", swap)
    near, forward, inverse, powers = lax.optimization_barrier((near, forward, inverse, powers))

    picked = call(
        project_kernel,
        [(PEERS, 4 * TS, NB)],
        [SMEM] + [VMEM] * 5,
        pos,
        blocks,
        near,
        by_yl,
        by_c,
        by_both,
    )
    parts = lax.all_to_all(picked, PLANE, 0, 0, tiled=True)
    forcing = call(gather_sum_kernel, [(Z, 4 * TS, NB)], [VMEM], parts)
    forcing = lax.all_to_all(forcing, "z", 0, 0, tiled=True)
    harmonic = call(forward_kernel, [(PEERS, TS, NB)], [VMEM, VMEM], forward, forcing)
    harmonic = lax.all_to_all(harmonic, PLANE, 0, 0, tiled=True)
    physical = call(
        modal_kernel,
        [(Z, TD, NB)],
        [SMEM] + [VMEM] * 4,
        pos,
        harmonic,
        shapes[0],
        flex[0],
        powers,
        scratch=[pltpu.VMEM((NT, NB), F32)],
    )
    physical = lax.all_to_all(physical, "z", 0, 0, tiled=True)
    sectoral = call(inverse_kernel, [(PEERS, TD, NB)], [VMEM] * 2, inverse, physical)
    sectoral = lax.all_to_all(sectoral, PLANE, 0, 0, tiled=True)
    rows = stress_map.shape[1]
    stress = call(
        stress_kernel,
        [(rows, NT)],
        [VMEM, VMEM],
        sectoral,
        stress_map[0],
        out_specs=[HBM],
        scratch=[pltpu.VMEM((rows, NT), BF), pltpu.SemaphoreType.DMA((CHUNKS,))],
    )
    return stress[None]


def solution(mesh):
    sector, dof = ("yl", "z", "c"), ("x", "yh")
    return jax.shard_map(
        local,
        mesh=Mesh(mesh.devices.reshape(SIZES), AXES),
        in_specs=(
            P(sector, None, dof),
            P(sector, None, dof),
            P(sector, None),
            P(sector, None),
            P(sector, None, None),
            P(sector, None, None),
            P(sector, None),
            P(sector, None),
            P(sector, dof, None),
        ),
        out_specs=P(sector, dof, None),
        check_vma=False,
    )
```

```python
import numpy as np
import jax
import jax.numpy as jnp
from jax import lax
from jax.experimental import pallas as pl
from jax.experimental.pallas import tpu as pltpu
from jax.sharding import Mesh, PartitionSpec as P

AXES = ("yl", "z", "c", "x", "yh")
SIZES = (2, 16, 2, 4, 2)
PLANE = ("yl", "c", "x", "yh")
YL, Z, C, D = 2, 16, 2, 8
PEERS = YL * C * D
BLADES, PH, NT, NB, MODES = YL * Z * C, 8, 256, 128, 40
COLS = 1792
TS = NT // PEERS
TD = NT // D
BF = jnp.bfloat16
F32 = jnp.float32
HI = lax.Precision.HIGHEST


def fourier_table(count):
    h = np.arange(count)[:, None]
    s = np.arange(count)[None, :]
    angle = 2.0 * np.pi * ((((h + 1) // 2) * s) % count) / count
    table = np.where(h % 2 == 1, np.cos(angle), np.sin(angle))
    table = np.where(h == 0, 1.0, table)
    edges = (h == 0) | (h == count - 1)
    return table * np.where(edges, np.sqrt(1.0 / count), np.sqrt(2.0 / count))


FOURIER = fourier_table(BLADES)


def forward_table():
    table = FOURIER.reshape(YL, Z, C, YL, Z, C).transpose(1, 0, 2, 4, 3, 5)
    table = np.einsum("zij,tu->zitju", table.reshape(Z, 4, BLADES), np.eye(TS))
    table = table.reshape(Z, 4 * TS, BLADES * TS).astype(np.float32)
    high = table.astype(BF)
    return np.stack([high, (table - high.astype(np.float32)).astype(BF)], axis=1)


FORWARD = forward_table()


def inverse_table():
    table = FOURIER.reshape(YL, Z, C, YL, Z, C).transpose(0, 2, 4, 3, 5, 1)
    table = np.einsum("dij,tu->ditju", table.reshape(BLADES, 4, Z), np.eye(TS))
    table = table.reshape(BLADES, 4 * TS, Z * TS).astype(np.float32)
    high = table.astype(BF)
    return np.stack([high, (table - high.astype(np.float32)).astype(BF)], axis=1)


INVERSE = inverse_table()


def dot_nt(a, b, **kw):
    return lax.dot_general(
        a, b, (((1,), (1,)), ((), ())), preferred_element_type=F32, **kw
    )


def spread_kernel(in_ref, out_ref, wake_ref, hold_ref, sems):
    copy = pltpu.make_async_copy(in_ref, wake_ref, sems.at[2])
    copy.start()
    copy.wait()
    copies = []
    for k in range(2):
        rows = pl.ds(k * Z // 2, Z // 2)
        hold_ref[rows] = jnp.broadcast_to(wake_ref[...][None], (Z // 2, PH, COLS))
        copies.append(pltpu.make_async_copy(hold_ref.at[rows], out_ref.at[rows], sems.at[k]))
        copies[-1].start()
    for copy in copies:
        copy.wait()


def pack_kernel(basis_ref, block_ref, phase_ref, out_ref):
    index = jnp.concatenate(
        [block_ref[...].astype(F32), phase_ref[...].astype(F32), jnp.zeros((14, NT), F32)], axis=0
    )
    index = jnp.concatenate([index, jnp.zeros((16, COLS - NT), F32)], axis=1).astype(BF)
    out_ref[0:NB] = basis_ref[...]
    out_ref[NB : NB + 16] = index


def select_kernel(pos, *refs):
    onehot_ref = refs[4]
    codes = []
    for ref in refs[:4]:
        index = ref[NB : NB + 16, 0:NT].astype(F32)
        block, phase = index[0:1].astype(jnp.int32), index[1:2].astype(jnp.int32)
        code = (((block >> 1) & (Z - 1)) * PH + phase).astype(F32)
        here = ((block & 1) == pos[1]) & ((block >> 5) == pos[0])
        codes.append(jnp.where(here, code, -1.0))
    codes = jnp.concatenate(codes + [jnp.zeros((4, NT), F32)], axis=0).T
    pair = lax.broadcasted_iota(jnp.int32, (NT, Z * PH), 1).astype(F32)
    for r in range(4):
        onehot_ref[r] = jnp.where(codes[:, r : r + 1] == pair, 1.0, 0.0).astype(BF)


def project_kernel(wake_ref, onehot_ref, *refs):
    out_ref = refs[4]
    wake = wake_ref[...].reshape(Z * PH, COLS)
    picks = []
    for r, ref in enumerate(refs[:4]):
        table = dot_nt(wake, ref[0:NB]).astype(BF)
        part = jnp.dot(onehot_ref[r], table, preferred_element_type=F32)
        picks.append(part.reshape(PEERS, TS, NB))
    out_ref[...] = jnp.concatenate(picks, axis=1).astype(BF)


def gather_sum_kernel(in_ref, out_ref):
    sums = {}
    for yl in range(YL):
        for c in range(C):
            total = None
            for d in range(D):
                part = in_ref[(yl * C + c) * D + d].astype(F32)
                total = part if total is None else total + part
            sums[yl, c] = total
    rows = []
    for yl in range(YL):
        for c in range(C):
            total = None
            for y in range(YL):
                for k in range(C):
                    r = (yl ^ y) + 2 * (c ^ k)
                    part = sums[y, k][r * TS : (r + 1) * TS]
                    total = part if total is None else total + part
            rows.append(total)
    block = jnp.concatenate(rows, axis=0).astype(BF)
    out_ref[...] = jnp.broadcast_to(block[None], out_ref.shape)


def forward_kernel(table_ref, in_ref, out_ref):
    block = in_ref[...].reshape(BLADES * TS, NB)
    block = sum(jnp.dot(table_ref[k], block, preferred_element_type=F32) for k in range(2))
    for h in range(4):
        part = block[h * TS : (h + 1) * TS].astype(BF)
        out_ref[h * D : (h + 1) * D] = jnp.broadcast_to(part[None], (D, TS, NB))


def powers_kernel(omega_ref, zeta_ref, out_ref):
    omega, zeta = omega_ref[...], zeta_ref[...]
    size = jnp.exp(-omega * zeta)
    angle = omega * jnp.sqrt(1.0 - zeta * zeta)
    real, imag = size * jnp.cos(angle), size * jnp.sin(angle)
    out_ref[...] = jnp.zeros_like(out_ref)
    for k in range(8):
        out_ref[2 * k : 2 * k + 1, 0:MODES] = real
        out_ref[2 * k + 1 : 2 * k + 2, 0:MODES] = imag
        real, imag = real * real - imag * imag, 2.0 * real * imag


def modal_kernel(pos, in_ref, shapes_ref, flex_ref, powers_ref, out_ref, hold_ref):
    shapes = jnp.concatenate(
        [shapes_ref[...].astype(F32), jnp.zeros((NB - MODES, NB), F32)], axis=0
    ).astype(BF)
    real = dot_nt(in_ref[...].reshape(NT, NB), shapes)
    imag = jnp.zeros_like(real)
    row = lax.broadcasted_iota(jnp.int32, (NT, NB), 0)
    for k in range(8):
        s = 2**k
        pr, pi = powers_ref[2 * k : 2 * k + 1, :], powers_ref[2 * k + 1 : 2 * k + 2, :]
        if s < 8:
            sr = jnp.where(row >= s, pltpu.roll(real, s, 0), 0.0)
            if k == 0:
                real, imag = real + pr * sr, pi * sr
            else:
                si = jnp.where(row >= s, pltpu.roll(imag, s, 0), 0.0)
                real, imag = real + (pr * sr - pi * si), imag + (pr * si + pi * sr)
        else:
            sr, si = real[: NT - s], imag[: NT - s]
            real = jnp.concatenate([real[:s], real[s:] + (pr * sr - pi * si)], axis=0)
            imag = jnp.concatenate([imag[:s], imag[s:] + (pr * si + pi * sr)], axis=0)
    hold_ref[...] = imag
    own = hold_ref[pl.ds(pl.multiple_of(pos[2] * TD, TD), TD), :]
    high = own.astype(BF)
    low = (own - high.astype(F32)).astype(BF)
    rows = in_ref[pl.ds(pos[2] * (TD // TS), TD // TS)].reshape(TD, NB)
    total = (
        jnp.dot(high, shapes, preferred_element_type=F32)
        + jnp.dot(low, shapes, preferred_element_type=F32)
        + dot_nt(rows, flex_ref[...])
    )
    out_ref[...] = jnp.broadcast_to(total.astype(BF)[None], out_ref.shape)


def inverse_kernel(table_ref, in_ref, out_ref):
    block = in_ref[...].astype(F32)
    parts = []
    for g in range(TD // TS):
        part = block[:, g * TS : (g + 1) * TS].reshape(Z * TS, NB).astype(BF)
        parts.append(
            sum(jnp.dot(table_ref[k], part, preferred_element_type=F32) for k in range(2))
        )
    for s in range(4):
        part = jnp.concatenate([p[s * TS : (s + 1) * TS] for p in parts], axis=0).astype(BF)
        out_ref[s * D : (s + 1) * D] = jnp.broadcast_to(part[None], (D, TD, NB))


CHUNKS = 8


def stress_kernel(in_ref, map_ref, out_ref, hold_ref, sems):
    total = None
    for q in range(YL * C):
        part = in_ref[q * D : (q + 1) * D].astype(F32)
        total = part if total is None else total + part
    motion = total.reshape(NT, NB).astype(BF)
    step = map_ref.shape[0] // CHUNKS
    copies = []
    for k in range(CHUNKS):
        rows = pl.ds(k * step, step)
        hold_ref[rows] = dot_nt(map_ref[rows], motion).astype(BF)
        copies.append(pltpu.make_async_copy(hold_ref.at[rows], out_ref.at[rows], sems.at[k]))
        copies[-1].start()
    for copy in copies:
        copy.wait()


VMEM = pl.BlockSpec(memory_space=pltpu.VMEM)
SMEM = pl.BlockSpec(memory_space=pltpu.SMEM)
HBM = pl.BlockSpec(memory_space=pl.ANY)


def call(kernel, outs, specs, *args, out_specs=None, scratch=(), dtype=BF, vmem=24):
    outs = [jax.ShapeDtypeStruct(shape, dtype) for shape in outs]
    got = pl.pallas_call(
        kernel,
        out_shape=outs,
        in_specs=specs,
        out_specs=out_specs or [VMEM] * len(outs),
        scratch_shapes=list(scratch),
        compiler_params=pltpu.CompilerParams(vmem_limit_bytes=vmem * 1024 * 1024),
    )(*args)
    return got[0] if len(outs) == 1 else got


def local(wake, basis, block_index, phase_index, shapes, flex, omega, zeta, stress_map):
    yl, z, c = lax.axis_index("yl"), lax.axis_index("z"), lax.axis_index("c")
    d = lax.axis_index("x") * 2 + lax.axis_index("yh")
    pos = jnp.stack([yl, c, d]).astype(jnp.int32)
    forward = lax.dynamic_slice(jnp.asarray(FORWARD), (z, 0, 0, 0), (1,) + FORWARD.shape[1:])[0]
    inverse = lax.dynamic_slice(
        jnp.asarray(INVERSE), ((yl * C + c) * Z + z, 0, 0, 0), (1,) + INVERSE.shape[1:]
    )[0]
    powers = call(powers_kernel, [(16, NB)], [VMEM] * 2, omega, zeta, dtype=F32)

    spread = call(
        spread_kernel,
        [(Z, PH, COLS)],
        [HBM],
        wake[0],
        out_specs=[HBM],
        vmem=60,
        scratch=[
            pltpu.VMEM((PH, COLS), BF),
            pltpu.VMEM((Z, PH, COLS), BF),
            pltpu.SemaphoreType.DMA((3,)),
        ],
    )
    blocks = lax.all_to_all(spread, "z", 0, 0, tiled=True)

    near = call(pack_kernel, [(NB + 16, COLS)], [VMEM] * 3, basis[0], block_index, phase_index)
    swap = [(0, 1), (1, 0)]
    by_yl = lax.ppermute(near, "yl", swap)
    by_c = lax.ppermute(near, "c", swap)
    by_both = lax.ppermute(by_yl, "c", swap)
    near, forward, inverse, powers = lax.optimization_barrier((near, forward, inverse, powers))

    sectors = (near, by_yl, by_c, by_both)
    onehot = call(select_kernel, [(4, NT, Z * PH)], [SMEM] + [VMEM] * 4, pos, *sectors)
    picked = call(
        project_kernel, [(PEERS, 4 * TS, NB)], [VMEM] * 6, blocks, onehot, *sectors
    )
    parts = lax.all_to_all(picked, PLANE, 0, 0, tiled=True)
    forcing = call(gather_sum_kernel, [(Z, 4 * TS, NB)], [VMEM], parts)
    forcing = lax.all_to_all(forcing, "z", 0, 0, tiled=True)
    harmonic = call(forward_kernel, [(PEERS, TS, NB)], [VMEM, VMEM], forward, forcing)
    harmonic = lax.all_to_all(harmonic, PLANE, 0, 0, tiled=True)
    physical = call(
        modal_kernel,
        [(Z, TD, NB)],
        [SMEM] + [VMEM] * 4,
        pos,
        harmonic,
        shapes[0],
        flex[0],
        powers,
        scratch=[pltpu.VMEM((NT, NB), F32)],
    )
    physical = lax.all_to_all(physical, "z", 0, 0, tiled=True)
    sectoral = call(inverse_kernel, [(PEERS, TD, NB)], [VMEM] * 2, inverse, physical)
    sectoral = lax.all_to_all(sectoral, PLANE, 0, 0, tiled=True)
    rows = stress_map.shape[1]
    stress = call(
        stress_kernel,
        [(rows, NT)],
        [VMEM, VMEM],
        sectoral,
        stress_map[0],
        out_specs=[HBM],
        scratch=[pltpu.VMEM((rows, NT), BF), pltpu.SemaphoreType.DMA((CHUNKS,))],
    )
    return stress[None]


def solution(mesh):
    sector, dof = ("yl", "z", "c"), ("x", "yh")
    return jax.shard_map(
        local,
        mesh=Mesh(mesh.devices.reshape(SIZES), AXES),
        in_specs=(
            P(sector, None, dof),
            P(sector, None, dof),
            P(sector, None),
            P(sector, None),
            P(sector, None, None),
            P(sector, None, None),
            P(sector, None),
            P(sector, None),
            P(sector, dof, None),
        ),
        out_specs=P(sector, dof, None),
        check_vma=False,
    )
```

```python
import numpy as np
import jax
import jax.numpy as jnp
from jax import lax
from jax.experimental import pallas as pl
from jax.experimental.pallas import tpu as pltpu
from jax.sharding import Mesh, PartitionSpec as P

AXES = ("yl", "z", "c", "x", "yh")
SIZES = (2, 16, 2, 4, 2)
PLANE = ("yl", "c", "x", "yh")
YL, Z, C, D = 2, 16, 2, 8
PEERS = YL * C * D
BLADES, PH, NT, NB, MODES = YL * Z * C, 8, 256, 128, 40
COLS = 1792
TS = NT // PEERS
TD = NT // D
BF = jnp.bfloat16
F32 = jnp.float32
HI = lax.Precision.HIGHEST


def fourier_table(count):
    h = np.arange(count)[:, None]
    s = np.arange(count)[None, :]
    angle = 2.0 * np.pi * ((((h + 1) // 2) * s) % count) / count
    table = np.where(h % 2 == 1, np.cos(angle), np.sin(angle))
    table = np.where(h == 0, 1.0, table)
    edges = (h == 0) | (h == count - 1)
    return table * np.where(edges, np.sqrt(1.0 / count), np.sqrt(2.0 / count))


FOURIER = fourier_table(BLADES)


def forward_table():
    table = FOURIER.reshape(YL, Z, C, YL, Z, C).transpose(1, 0, 2, 4, 3, 5)
    table = np.einsum("zij,tu->zitju", table.reshape(Z, 4, BLADES), np.eye(TS))
    table = table.reshape(Z, 4 * TS, BLADES * TS).astype(np.float32)
    high = table.astype(BF)
    return np.stack([high, (table - high.astype(np.float32)).astype(BF)], axis=1)


FORWARD = forward_table()


def inverse_table():
    table = FOURIER.reshape(YL, Z, C, YL, Z, C).transpose(0, 2, 4, 3, 5, 1)
    table = np.einsum("dij,tu->ditju", table.reshape(BLADES, 4, Z), np.eye(TS))
    table = table.reshape(BLADES, 4 * TS, Z * TS).astype(np.float32)
    high = table.astype(BF)
    return np.stack([high, (table - high.astype(np.float32)).astype(BF)], axis=1)


INVERSE = inverse_table()


def dot_nt(a, b, **kw):
    return lax.dot_general(
        a, b, (((1,), (1,)), ((), ())), preferred_element_type=F32, **kw
    )


def spread_kernel(in_ref, out_ref, wake_ref, hold_ref, sems):
    copy = pltpu.make_async_copy(in_ref, wake_ref, sems.at[2])
    copy.start()
    copy.wait()
    copies = []
    for k in range(2):
        rows = pl.ds(k * Z // 2, Z // 2)
        hold_ref[rows] = jnp.broadcast_to(wake_ref[...][None], (Z // 2, PH, COLS))
        copies.append(pltpu.make_async_copy(hold_ref.at[rows], out_ref.at[rows], sems.at[k]))
        copies[-1].start()
    for copy in copies:
        copy.wait()


def pack_kernel(basis_ref, block_ref, phase_ref, out_ref):
    index = jnp.concatenate(
        [block_ref[...].astype(F32), phase_ref[...].astype(F32), jnp.zeros((14, NT), F32)], axis=0
    )
    index = jnp.concatenate([index, jnp.zeros((16, COLS - NT), F32)], axis=1).astype(BF)
    out_ref[0:NB] = basis_ref[...]
    out_ref[NB : NB + 16] = index


def select_kernel(pos, *refs):
    onehot_ref = refs[4]
    codes = []
    for ref in refs[:4]:
        index = ref[NB : NB + 16, 0:NT].astype(F32)
        block, phase = index[0:1].astype(jnp.int32), index[1:2].astype(jnp.int32)
        code = (((block >> 1) & (Z - 1)) * PH + phase).astype(F32)
        here = ((block & 1) == pos[1]) & ((block >> 5) == pos[0])
        codes.append(jnp.where(here, code, -1.0))
    codes = jnp.concatenate(codes + [jnp.zeros((4, NT), F32)], axis=0).T
    pair = lax.broadcasted_iota(jnp.int32, (NT, Z * PH), 1).astype(F32)
    for r in range(4):
        onehot_ref[r] = jnp.where(codes[:, r : r + 1] == pair, 1.0, 0.0).astype(BF)


def project_kernel(wake_ref, onehot_ref, *refs):
    out_ref = refs[4]
    wake = wake_ref[...].reshape(Z * PH, COLS)
    basis = jnp.concatenate([ref[0:NB] for ref in refs[:4]], axis=0)
    table = dot_nt(basis, wake).astype(BF)
    picks = []
    for r in range(4):
        part = dot_nt(onehot_ref[r], table[r * NB : (r + 1) * NB])
        picks.append(part.reshape(PEERS, TS, NB))
    out_ref[...] = jnp.concatenate(picks, axis=1).astype(BF)


def gather_sum_kernel(in_ref, out_ref):
    sums = {}
    for yl in range(YL):
        for c in range(C):
            total = None
            for d in range(D):
                part = in_ref[(yl * C + c) * D + d].astype(F32)
                total = part if total is None else total + part
            sums[yl, c] = total
    rows = []
    for yl in range(YL):
        for c in range(C):
            total = None
            for y in range(YL):
                for k in range(C):
                    r = (yl ^ y) + 2 * (c ^ k)
                    part = sums[y, k][r * TS : (r + 1) * TS]
                    total = part if total is None else total + part
            rows.append(total)
    block = jnp.concatenate(rows, axis=0).astype(BF)
    out_ref[...] = jnp.broadcast_to(block[None], out_ref.shape)


def forward_kernel(table_ref, in_ref, out_ref):
    block = in_ref[...].reshape(BLADES * TS, NB)
    block = sum(jnp.dot(table_ref[k], block, preferred_element_type=F32) for k in range(2))
    for h in range(4):
        part = block[h * TS : (h + 1) * TS].astype(BF)
        out_ref[h * D : (h + 1) * D] = jnp.broadcast_to(part[None], (D, TS, NB))


def powers_kernel(omega_ref, zeta_ref, out_ref):
    omega, zeta = omega_ref[...], zeta_ref[...]
    size = jnp.exp(-omega * zeta)
    angle = omega * jnp.sqrt(1.0 - zeta * zeta)
    real, imag = size * jnp.cos(angle), size * jnp.sin(angle)
    out_ref[...] = jnp.zeros_like(out_ref)
    for k in range(8):
        out_ref[2 * k : 2 * k + 1, 0:MODES] = real
        out_ref[2 * k + 1 : 2 * k + 2, 0:MODES] = imag
        real, imag = real * real - imag * imag, 2.0 * real * imag


def modal_kernel(pos, in_ref, shapes_ref, flex_ref, powers_ref, out_ref, hold_ref):
    shapes = jnp.concatenate(
        [shapes_ref[...].astype(F32), jnp.zeros((NB - MODES, NB), F32)], axis=0
    ).astype(BF)
    real = dot_nt(in_ref[...].reshape(NT, NB), shapes)
    imag = jnp.zeros_like(real)
    row = lax.broadcasted_iota(jnp.int32, (NT, NB), 0)
    for k in range(8):
        s = 2**k
        pr, pi = powers_ref[2 * k : 2 * k + 1, :], powers_ref[2 * k + 1 : 2 * k + 2, :]
        if s < 8:
            sr = jnp.where(row >= s, pltpu.roll(real, s, 0), 0.0)
            if k == 0:
                real, imag = real + pr * sr, pi * sr
            else:
                si = jnp.where(row >= s, pltpu.roll(imag, s, 0), 0.0)
                real, imag = real + (pr * sr - pi * si), imag + (pr * si + pi * sr)
        else:
            sr, si = real[: NT - s], imag[: NT - s]
            real = jnp.concatenate([real[:s], real[s:] + (pr * sr - pi * si)], axis=0)
            imag = jnp.concatenate([imag[:s], imag[s:] + (pr * si + pi * sr)], axis=0)
    hold_ref[...] = imag
    own = hold_ref[pl.ds(pl.multiple_of(pos[2] * TD, TD), TD), :]
    high = own.astype(BF)
    low = (own - high.astype(F32)).astype(BF)
    rows = in_ref[pl.ds(pos[2] * (TD // TS), TD // TS)].reshape(TD, NB)
    total = (
        jnp.dot(high, shapes, preferred_element_type=F32)
        + jnp.dot(low, shapes, preferred_element_type=F32)
        + dot_nt(rows, flex_ref[...])
    )
    out_ref[...] = jnp.broadcast_to(total.astype(BF)[None], out_ref.shape)


def inverse_kernel(table_ref, in_ref, out_ref):
    block = in_ref[...].astype(F32)
    parts = []
    for g in range(TD // TS):
        part = block[:, g * TS : (g + 1) * TS].reshape(Z * TS, NB).astype(BF)
        parts.append(
            sum(jnp.dot(table_ref[k], part, preferred_element_type=F32) for k in range(2))
        )
    for s in range(4):
        part = jnp.concatenate([p[s * TS : (s + 1) * TS] for p in parts], axis=0).astype(BF)
        out_ref[s * D : (s + 1) * D] = jnp.broadcast_to(part[None], (D, TD, NB))


CHUNKS = 8


def stress_kernel(in_ref, map_ref, out_ref, hold_ref, sems):
    total = None
    for q in range(YL * C):
        part = in_ref[q * D : (q + 1) * D].astype(F32)
        total = part if total is None else total + part
    motion = total.reshape(NT, NB).astype(BF)
    step = map_ref.shape[0] // CHUNKS
    copies = []
    for k in range(CHUNKS):
        rows = pl.ds(k * step, step)
        hold_ref[rows] = dot_nt(map_ref[rows], motion).astype(BF)
        copies.append(pltpu.make_async_copy(hold_ref.at[rows], out_ref.at[rows], sems.at[k]))
        copies[-1].start()
    for copy in copies:
        copy.wait()


VMEM = pl.BlockSpec(memory_space=pltpu.VMEM)
SMEM = pl.BlockSpec(memory_space=pltpu.SMEM)
HBM = pl.BlockSpec(memory_space=pl.ANY)


def call(kernel, outs, specs, *args, out_specs=None, scratch=(), dtype=BF, vmem=24):
    outs = [jax.ShapeDtypeStruct(shape, dtype) for shape in outs]
    got = pl.pallas_call(
        kernel,
        out_shape=outs,
        in_specs=specs,
        out_specs=out_specs or [VMEM] * len(outs),
        scratch_shapes=list(scratch),
        compiler_params=pltpu.CompilerParams(vmem_limit_bytes=vmem * 1024 * 1024),
    )(*args)
    return got[0] if len(outs) == 1 else got


def local(wake, basis, block_index, phase_index, shapes, flex, omega, zeta, stress_map):
    yl, z, c = lax.axis_index("yl"), lax.axis_index("z"), lax.axis_index("c")
    d = lax.axis_index("x") * 2 + lax.axis_index("yh")
    pos = jnp.stack([yl, c, d]).astype(jnp.int32)
    forward = lax.dynamic_slice(jnp.asarray(FORWARD), (z, 0, 0, 0), (1,) + FORWARD.shape[1:])[0]
    inverse = lax.dynamic_slice(
        jnp.asarray(INVERSE), ((yl * C + c) * Z + z, 0, 0, 0), (1,) + INVERSE.shape[1:]
    )[0]
    powers = call(powers_kernel, [(16, NB)], [VMEM] * 2, omega, zeta, dtype=F32)

    spread = call(
        spread_kernel,
        [(Z, PH, COLS)],
        [HBM],
        wake[0],
        out_specs=[HBM],
        vmem=60,
        scratch=[
            pltpu.VMEM((PH, COLS), BF),
            pltpu.VMEM((Z, PH, COLS), BF),
            pltpu.SemaphoreType.DMA((3,)),
        ],
    )
    blocks = lax.all_to_all(spread, "z", 0, 0, tiled=True)

    near = call(pack_kernel, [(NB + 16, COLS)], [VMEM] * 3, basis[0], block_index, phase_index)
    swap = [(0, 1), (1, 0)]
    by_yl = lax.ppermute(near, "yl", swap)
    by_c = lax.ppermute(near, "c", swap)
    by_both = lax.ppermute(by_yl, "c", swap)
    near, forward, inverse, powers = lax.optimization_barrier((near, forward, inverse, powers))

    sectors = (near, by_yl, by_c, by_both)
    onehot = call(select_kernel, [(4, NT, Z * PH)], [SMEM] + [VMEM] * 4, pos, *sectors)
    picked = call(
        project_kernel, [(PEERS, 4 * TS, NB)], [VMEM] * 6, blocks, onehot, *sectors
    )
    parts = lax.all_to_all(picked, PLANE, 0, 0, tiled=True)
    forcing = call(gather_sum_kernel, [(Z, 4 * TS, NB)], [VMEM], parts)
    forcing = lax.all_to_all(forcing, "z", 0, 0, tiled=True)
    harmonic = call(forward_kernel, [(PEERS, TS, NB)], [VMEM, VMEM], forward, forcing)
    harmonic = lax.all_to_all(harmonic, PLANE, 0, 0, tiled=True)
    physical = call(
        modal_kernel,
        [(Z, TD, NB)],
        [SMEM] + [VMEM] * 4,
        pos,
        harmonic,
        shapes[0],
        flex[0],
        powers,
        scratch=[pltpu.VMEM((NT, NB), F32)],
    )
    physical = lax.all_to_all(physical, "z", 0, 0, tiled=True)
    sectoral = call(inverse_kernel, [(PEERS, TD, NB)], [VMEM] * 2, inverse, physical)
    sectoral = lax.all_to_all(sectoral, PLANE, 0, 0, tiled=True)
    rows = stress_map.shape[1]
    stress = call(
        stress_kernel,
        [(rows, NT)],
        [VMEM, VMEM],
        sectoral,
        stress_map[0],
        out_specs=[HBM],
        scratch=[pltpu.VMEM((rows, NT), BF), pltpu.SemaphoreType.DMA((CHUNKS,))],
    )
    return stress[None]


def solution(mesh):
    sector, dof = ("yl", "z", "c"), ("x", "yh")
    return jax.shard_map(
        local,
        mesh=Mesh(mesh.devices.reshape(SIZES), AXES),
        in_specs=(
            P(sector, None, dof),
            P(sector, None, dof),
            P(sector, None),
            P(sector, None),
            P(sector, None, None),
            P(sector, None, None),
            P(sector, None),
            P(sector, None),
            P(sector, dof, None),
        ),
        out_specs=P(sector, dof, None),
        check_vma=False,
    )
```
